32 devices in a mesh: dom: 8 (over y, x, core), mode: 4 (over z).
Axes of the slice: x: 2, y: 2, z: 4, core: 2. Of those that a mesh axis runs over, the one named last changes fastest.
Arguments:
- iterate: float32 [256, 256, 256], P('mode', 'dom'), may hold values from -6 to 6
- source: float32 [256, 256, 256], P('mode', 'dom'), may hold values from -6 to 6
- mean_coef: float32 [256, 256], P('dom'), may hold values from 0.5 to 2
- kl_fields: float32 [20, 256, 256], P(None, 'dom'), may hold values from -1 to 1
- tri_index: int32 [5376, 3], replicated, may hold values from 0 to 255, as said below
- tri_value: float32 [5376], replicated, may hold values from 0.25 to 1.75, as said below
Outputs:
- updated: float32 [256, 256, 256], P('mode', 'dom')
- residual: float32 [256, 256, 256], P('mode', 'dom')
The draws below stay inside these ranges and needn't reach their ends.
Inputs may be any that keep to these rules, and one draw needn't show every extreme that they name: `tri_index`: every pair of a mode i and a field l appears in exactly one entry; entries of field 0 have j = i; for fields 1 to 20 the entry (i, j, l) is listed together with (j, i, l), j differing from i; rows stand in a random order. `tri_value`: the entries (i, j, l) and (j, i, l) carry the same value.
All inputs are finite; a program needn't handle non-finite values.
Results may differ from the reference program's by a relative error of at most 0.0062.
Values may be sent and summed in bfloat16 or wider, within the bound.
No kernel may reach another device: no remote copies, remote signals or barrier semaphores. Data moves between devices by JAX's collectives and lax.ppermute only.
A program may use at most 64 MiB of HBM per device.

```python
import math
import jax
import jax.numpy as jnp
from jax import lax

P_SIZE = 256
L = 20
NY = 16
NZ = 16
NX = 256


def pairing_tables(key):
    partners = []
    slots = []
    for level in range(1, L + 1):
        order = jax.random.permutation(jax.random.fold_in(key, 1000 + level), P_SIZE).astype(jnp.int32)
        place = jnp.argsort(order).astype(jnp.int32)
        partners.append(order[place ^ 1])
        slots.append(place // 2)
    row_order = jax.random.permutation(jax.random.fold_in(key, 77), P_SIZE * (L + 1)).astype(jnp.int32)
    return (jnp.stack(partners), jnp.stack(slots), row_order)


def draw_tri_index(key, part):
    partners, slots, row_order = pairing_tables(key)
    modes = jnp.arange(P_SIZE, dtype=jnp.int32)
    blocks = [jnp.stack([modes, modes, jnp.zeros_like(modes)], 1)]
    for level in range(1, L + 1):
        blocks.append(jnp.stack([modes, partners[level - 1], jnp.full_like(modes, level)], 1))
    listing = jnp.concatenate(blocks, 0)
    return listing[row_order]


def draw_tri_value(key, part):
    partners, slots, row_order = pairing_tables(key)
    low_end, high_end = (0.5, 1.5)
    diagonal = jax.random.uniform(jax.random.fold_in(key, 2000), (P_SIZE,), jnp.float32, low_end, high_end)
    paired = jax.random.uniform(jax.random.fold_in(key, 2001), (L, P_SIZE // 2), jnp.float32, low_end, high_end)
    blocks = [diagonal]
    for level in range(1, L + 1):
        blocks.append(paired[level - 1][slots[level - 1]])
    listing = jnp.concatenate(blocks, 0)
    return listing[row_order]


def block_levels(rng, dims, cuts, low, largest):
    def one(dim, shards_of):
        draws = jax.random.uniform(jax.random.fold_in(jax.random.fold_in(rng, 6), dim), (shards_of,), jnp.float32, low / len(cuts), largest / len(cuts))
        return jnp.repeat(jnp.exp(draws), dims[dim] // shards_of).reshape((-1,) + (1,) * (len(dims) - dim - 1))

    gain = one(*cuts[0])
    for cut in cuts[1:]:
        gain = gain * one(*cut)
    return gain


def scatter_about(rng, extent, width, bound, pieces=(), held_as=jnp.bfloat16):
    values = jax.random.normal(rng, extent, jnp.float32) * width
    if len(pieces) > 0:
        values = block_levels(rng, extent, pieces, -0.22, 0.18) * values
    return jnp.clip(values, min=-bound, max=bound).astype(held_as)


def setup_inputs(seed: int = 0) -> dict:
    splits = jax.random.split(jax.random.key(seed), 7)
    return {
        "iterate": scatter_about(splits[0], (P_SIZE, NX, NY * NZ), 1.0, 6.0, ((0, 4), (1, 8)), jnp.float32),
        "source": scatter_about(splits[1], (P_SIZE, NX, NY * NZ), 1.0, 6.0, ((0, 4), (1, 8)), jnp.float32),
        "mean_coef": jnp.clip(jnp.exp(math.log(2.0) - 1.3862944 * jax.random.uniform(splits[2], (NX, NY * NZ), jnp.float32) ** block_levels(splits[2], (NX, NY * NZ), ((0, 8),), -0.2, 0.2)), 0.5, 2.0),
        "kl_fields": scatter_about(splits[3], (L, NX, NY * NZ), 0.25, 1.0, ((1, 8),), jnp.float32),
        "tri_index": draw_tri_index(jax.random.fold_in(splits[6], 71), 0),
        "tri_value": draw_tri_value(jax.random.fold_in(splits[6], 71), 0),
    }


cheb_center = 1.125
cheb_radius = 0.875


def shifted(field, offset):
    if offset > 0:
        filler = jnp.zeros(field.shape[:-1] + (offset,), field.dtype)
        return jnp.concatenate([field[..., offset:], filler], -1)
    amount = -offset
    filler = jnp.zeros(field.shape[:-1] + (amount,), field.dtype)
    return jnp.concatenate([filler, field[..., :-amount]], -1)


def z_masks(cells, z_depth):
    z_place = jnp.arange(cells) % z_depth
    return (z_place < z_depth - 1).astype(jnp.float32), (z_place > 0).astype(jnp.float32)


def face_weights(padded_coef, upper_mask, lower_mask, z_depth):
    centre = padded_coef[:, 1:-1]
    return (0.5 * (centre + padded_coef[:, 2:]),
            0.5 * (centre + padded_coef[:, :-2]),
            0.5 * (centre + shifted(centre, z_depth)),
            0.5 * (centre + shifted(centre, -z_depth)),
            0.5 * (centre + shifted(centre, 1) * upper_mask),
            0.5 * (centre + shifted(centre, -1) * lower_mask))


def apply_stencil(padded, face_set, upper_mask, lower_mask, z_depth):
    centre = padded[:, 1:-1]
    result = face_set[0] * (centre - padded[:, 2:]) + face_set[1] * (centre - padded[:, :-2])
    result = result + face_set[2] * (centre - shifted(centre, z_depth)) + face_set[3] * (centre - shifted(centre, -z_depth))
    result = result + face_set[4] * (centre - shifted(centre, 1) * upper_mask)
    return result + face_set[5] * (centre - shifted(centre, -1) * lower_mask)


def reference(iterate, source, mean_coef, kl_fields, tri_index, tri_value):
    cells = NY * NZ
    coef = jnp.concatenate([mean_coef[None], kl_fields], 0)
    padded_coef = jnp.pad(coef, ((0, 0), (1, 1), (0, 0)))
    upper_mask, lower_mask = z_masks(cells, NZ)
    face_set = face_weights(padded_coef, upper_mask, lower_mask, NZ)
    dense = jnp.zeros((P_SIZE, L + 1, P_SIZE), jnp.float32)
    dense = dense.at[tri_index[:, 0], tri_index[:, 2], tri_index[:, 1]].add(tri_value)
    dense = dense.astype(jnp.bfloat16).astype(jnp.float32)
    matrices = jnp.transpose(dense, (1, 0, 2))
    rounded = iterate.astype(jnp.bfloat16).astype(jnp.float32)
    flat = jnp.pad(rounded, ((0, 0), (1, 1), (0, 0))).reshape(P_SIZE, -1)

    def accumulate(total, items):
        matrix, faces_here = items
        mixed = jnp.dot(matrix, flat, precision=lax.Precision.HIGHEST).reshape(P_SIZE, NX + 2, cells)
        return total + apply_stencil(mixed, faces_here, upper_mask, lower_mask, NZ), None

    image, _ = lax.scan(accumulate, jnp.zeros((P_SIZE, NX, cells), jnp.float32), (matrices, face_set))
    residual = source - image
    mean_faces = tuple(weight[0] for weight in face_set)
    diag = mean_faces[0] + mean_faces[1] + mean_faces[2] + mean_faces[3] + mean_faces[4] + mean_faces[5]
    sigma = cheb_center / cheb_radius
    rho_zero = 1.0 / sigma
    rho_one = 1.0 / (2.0 * sigma - rho_zero)
    first = residual / (cheb_center * diag)
    padded_first = jnp.pad(first, ((0, 0), (1, 1), (0, 0)))
    smoothed = residual - apply_stencil(padded_first, mean_faces, upper_mask, lower_mask, NZ)
    second = rho_one * rho_zero * first + (2.0 * rho_one / cheb_radius) * smoothed / diag
    return iterate + first + second, residual
```

```python
import functools
import jax
import jax.numpy as jnp
from jax import lax
from jax.experimental import pallas as pl
from jax.experimental.pallas import tpu as pltpu
from jax.sharding import PartitionSpec as P

NZ = 16
GROUP = 7

cheb_center = 1.125
cheb_radius = 0.875
VMEM_LIMIT = 48 * 1024 * 1024


def in_vmem(count):
    return [pl.BlockSpec(memory_space=pltpu.VMEM)] * count


def in_smem():
    return pl.BlockSpec(memory_space=pltpu.SMEM)


def row_of(place, rho, slab, count, rows):
    upward = slab * place + rho
    downward = slab * place + (slab - 1 - rho)
    row = jnp.where(place < count // 2, upward, downward)
    return jnp.clip(row, 0, rows - 1)


def rim_row(place, slab, count, rows):
    row = row_of(place, -1, slab, count, rows)
    return jnp.where(place == 0, rows - 1, jnp.where(place == count - 1, 0, row))


def pack_kernel(count, slab, half, rows, z_ref, x_ref, *refs):
    z = z_ref[0]
    outs, turned = refs[:-1], refs[-1]
    turned[...] = jnp.swapaxes(x_ref[...], 0, 1).astype(jnp.bfloat16)
    for p in range(count):
        place = jnp.bitwise_xor(z, p)
        rim, early, late = outs[3 * p : 3 * p + 3]

        rim[0] = turned[rim_row(place, slab, count, rows)]
        for rho in range(slab + 1):
            row = row_of(place, rho, slab, count, rows)
            if rho <= half:
                early[rho] = turned[row]
            else:
                late[rho - half - 1] = turned[row]


def masks(cells):
    lane = lax.broadcasted_iota(jnp.int32, (1, cells), 1)
    in_z = lane % NZ
    one = jnp.float32(1.0)
    zero = jnp.float32(0.0)
    return (
        jnp.where(lane < cells - NZ, one, zero),
        jnp.where(lane >= NZ, one, zero),
        jnp.where(in_z < NZ - 1, one, zero),
        jnp.where(in_z > 0, one, zero),
    )


def beside(field, mask_set):
    cells = field.shape[-1]
    axis = field.ndim - 1
    return (
        pltpu.roll(field, cells - NZ, axis) * mask_set[0],
        pltpu.roll(field, NZ, axis) * mask_set[1],
        pltpu.roll(field, cells - 1, axis) * mask_set[2],
        pltpu.roll(field, 1, axis) * mask_set[3],
    )


def setup_kernel(
    slab, groups, modes_here, z_ref, i_ref, j_ref, l_ref, v_ref, coef_ref, dense_ref, weight_ref
):
    cells = coef_ref.shape[-1]
    size = dense_ref.shape[1]
    entries = i_ref.shape[1]
    flip = z_ref[0] * modes_here
    mode_id = jnp.bitwise_xor(lax.broadcasted_iota(jnp.int32, (size, entries), 0), flip)
    pick = jnp.where(mode_id == i_ref[...], 1.0, 0.0).astype(jnp.bfloat16)
    depth = groups * 8
    place = lax.broadcasted_iota(jnp.int32, (depth, entries), 0)
    field_of = jnp.where(place % 8 < GROUP, (place // 8) * GROUP + place % 8, -1)
    here = field_of == l_ref[...]
    partner = jnp.where(here, j_ref[...].astype(jnp.float32), 0.0).astype(jnp.bfloat16)
    value = jnp.where(here, v_ref[...], 0.0).astype(jnp.bfloat16)
    dims = (((1,), (1,)), ((), ()))
    partner_of = lax.dot_general(pick, partner, dims, preferred_element_type=jnp.float32)
    value_of = lax.dot_general(pick, value, dims, preferred_element_type=jnp.float32)
    column = jnp.bitwise_xor(lax.broadcasted_iota(jnp.int32, (size, size), 1), flip)
    column = column.astype(jnp.float32)
    for g in range(groups):
        for k in range(GROUP):
            at = g * 8 + k
            tile = jnp.where(column == partner_of[:, at : at + 1], value_of[:, at : at + 1], 0.0)
            dense_ref[g, :, k * size : (k + 1) * size] = tile.astype(jnp.bfloat16)
    mask_set = masks(cells)
    for rho in range(slab):
        centre = coef_ref[rho + 1]
        others = (coef_ref[rho + 2], coef_ref[rho]) + beside(centre, mask_set)
        for f, other in enumerate(others):
            weight_ref[rho, f] = 0.5 * (centre + other)


def mix_kernel(count, half, groups, window, *refs):
    rows_in = len(window)
    arrays = max(a for a, _ in window) + 1
    sources = refs[: arrays * count]
    dense_ref, weight_ref = refs[arrays * count : arrays * count + 2]
    outs = refs[arrays * count + 2 : arrays * count + 2 + count]
    rows_ref, diff_ref, term_ref, total_ref = refs[arrays * count + 2 + count :]
    size, cells = total_ref.shape
    here = size // count
    for k, (array, row) in enumerate(window):
        for p in range(count):
            rows_ref[k, p * here : (p + 1) * here, :] = sources[array * count + p][row]
    mask_set = masks(cells)

    def each_row(r, carry):
        centre = rows_ref[r + 1].astype(jnp.float32)
        diff_ref[0] = centre - rows_ref[r + 2].astype(jnp.float32)
        diff_ref[1] = centre - rows_ref[r].astype(jnp.float32)
        for f, other in enumerate(beside(centre, mask_set)):
            diff_ref[2 + f] = centre - other
        total_ref[...] = jnp.zeros_like(total_ref)

        def each_group(g, carry):
            for k in range(GROUP):
                term = None
                for f in range(6):
                    part = weight_ref[r, f, g, k : k + 1, :] * diff_ref[f]
                    term = part if term is None else term + part
                term_ref[k * size : (k + 1) * size, :] = term.astype(jnp.bfloat16)
            total_ref[...] += jnp.dot(
                dense_ref[g], term_ref[...], preferred_element_type=jnp.float32
            )
            return carry

        lax.fori_loop(0, groups, each_group, 0)
        for p in range(count):
            outs[p][r] = total_ref[p * here : (p + 1) * here, :].astype(jnp.bfloat16)
        return carry

    lax.fori_loop(0, half, each_row, 0)


def post_kernel(count, slab, half, rows, rho_zero, rho_one, z_ref, *refs):
    early = refs[:count]
    late = refs[count : 2 * count]
    source, iterate, low, high, faces, inverse = refs[2 * count : 2 * count + 6]
    updated, residual, image = refs[2 * count + 6 :]
    z = z_ref[0]
    modes, _, cells = source.shape
    for p in range(count):
        place = jnp.bitwise_xor(z, p)
        for rho in range(slab):
            part = early[p][rho] if rho < half else late[p][rho - half]
            image[row_of(place, rho, slab, count, rows)] = part.astype(jnp.float32)
    residual[...] = source[...] - jnp.swapaxes(image[...], 0, 1)
    place = lax.broadcasted_iota(jnp.int32, (rows, cells), 0)
    inv = inverse[...]
    for m in range(modes):
        res = residual[m]
        first = res * (inv * (1.0 / cheb_center))
        up = jnp.where(place == rows - 1, high[m : m + 1, :], pltpu.roll(first, rows - 1, 0))
        down = jnp.where(place == 0, low[m : m + 1, :], pltpu.roll(first, 1, 0))
        near = faces[0] * up + faces[1] * down
        near = near + faces[2] * pltpu.roll(first, cells - NZ, 1)
        near = near + faces[3] * pltpu.roll(first, NZ, 1)
        near = near + faces[4] * pltpu.roll(first, cells - 1, 1)
        near = near + faces[5] * pltpu.roll(first, 1, 1)
        smoothed = (1.0 - 1.0 / cheb_center) * res + near
        step = (1.0 + rho_one * rho_zero) * first + (2.0 * rho_one / cheb_radius) * smoothed * inv
        updated[m] = iterate[m] + step


def mean_faces(padded, cells):
    centre = padded[1:-1]
    lane = jnp.arange(cells)

    def shift(amount, keep):
        return jnp.where(keep, jnp.roll(centre, -amount, -1), 0.0)

    keeps = (lane < cells - NZ, lane >= NZ, lane % NZ < NZ - 1, lane % NZ > 0)
    others = [padded[2:], padded[:-2]]
    others += [shift(a, k) for a, k in zip((NZ, -NZ, 1, -1), keeps)]
    weights = [0.5 * (centre + other) for other in others]
    diag = weights[0] + weights[1] + weights[2] + weights[3] + weights[4] + weights[5]
    inner = weights[:2] + [jnp.where(k, w, 0.0) for k, w in zip(keeps, weights[2:])]
    return jnp.stack(inner), 1.0 / diag


def body(iterate, source, mean_coef, kl_fields, tri_index, tri_value):
    count = lax.axis_size("mode")
    doms = lax.axis_size("dom")
    z = lax.axis_index("mode")
    z_arg = z.astype(jnp.int32).reshape(1)
    here, rows, cells = iterate.shape
    size = here * count
    slab = rows // count
    half = slab // 2
    fields = kl_fields.shape[0] + 1
    groups = -(-fields // GROUP)
    bf16 = jnp.bfloat16
    params = pltpu.CompilerParams(vmem_limit_bytes=VMEM_LIMIT)

    shapes = []
    for _ in range(count):
        shapes += [
            jax.ShapeDtypeStruct((1, here, cells), bf16),
            jax.ShapeDtypeStruct((half + 1, here, cells), bf16),
            jax.ShapeDtypeStruct((slab - half, here, cells), bf16),
        ]
    packed = pl.pallas_call(
        functools.partial(pack_kernel, count, slab, half, rows),
        out_shape=shapes,
        in_specs=[in_smem()] + in_vmem(1),
        out_specs=in_vmem(3 * count),
        scratch_shapes=[pltpu.VMEM((rows, here, cells), bf16)],
        compiler_params=params,
        name="pack",
    )(z_arg, iterate)

    def swap(array, p):
        return lax.ppermute(array, "mode", [(i, i ^ p) for i in range(count)])

    def swap_rim(array, p):
        pairs = []
        for d in range(doms):
            for i in range(count):
                to = i ^ p
                target = d + 1 if to == 0 else d - 1 if to == count - 1 else d
                if p == 0 and target == d:
                    continue
                if 0 <= target < doms:
                    pairs.append((d * count + i, target * count + to))
        return lax.ppermute(array, ("dom", "mode"), pairs)

    rims = [swap_rim(packed[3 * p], p) for p in range(count)]
    edge = jnp.logical_or(z == 0, z == count - 1)
    rims[0] = jnp.where(edge, rims[0], packed[0])
    early = [packed[1]] + [swap(packed[3 * p + 1], p) for p in range(1, count)]
    late = [packed[2]] + [swap(packed[3 * p + 2], p) for p in range(1, count)]

    coef = jnp.concatenate([mean_coef[None], kl_fields], 0)
    upward = [(i, i + 1) for i in range(doms - 1)]
    downward = [(b, a) for a, b in upward]
    low_coef = lax.ppermute(coef[:, -1:], "dom", upward)
    high_coef = lax.ppermute(coef[:, :1], "dom", downward)
    padded = jnp.concatenate([low_coef, coef, high_coef], 1)
    slab_coef = lax.dynamic_slice_in_dim(padded, z * slab, slab + 2, 1)
    slab_coef = jnp.where(z < count // 2, slab_coef, jnp.flip(slab_coef, 1))
    slab_coef = jnp.pad(slab_coef, ((0, groups * GROUP - fields), (0, 0), (0, 0)))
    slab_coef = slab_coef.reshape(groups, GROUP, slab + 2, cells)
    slab_coef = jnp.pad(slab_coef, ((0, 0), (0, 8 - GROUP), (0, 0), (0, 0)))
    slab_coef = jnp.transpose(slab_coef, (2, 0, 1, 3))
    entries = tri_index.T
    dense, weights = pl.pallas_call(
        functools.partial(setup_kernel, slab, groups, here),
        out_shape=[
            jax.ShapeDtypeStruct((groups, size, GROUP * size), bf16),
            jax.ShapeDtypeStruct((slab, 6, groups, 8, cells), jnp.float32),
        ],
        in_specs=[in_smem()] + in_vmem(5),
        out_specs=in_vmem(2),
        compiler_params=params,
        name="setup",
    )(z_arg, entries[0:1], entries[1:2], entries[2:3], tri_value[None], slab_coef)
    faces, inverse = mean_faces(padded[0], cells)

    def mix(arrays, window, weight_rows):
        flat = [a for group in arrays for a in group]
        return pl.pallas_call(
            functools.partial(mix_kernel, count, half, groups, window),
            out_shape=[jax.ShapeDtypeStruct((half, here, cells), bf16)] * count,
            in_specs=in_vmem(len(flat) + 2),
            out_specs=in_vmem(count),
            scratch_shapes=[
                pltpu.VMEM((half + 2, size, cells), bf16),
                pltpu.VMEM((6, size, cells), jnp.float32),
                pltpu.VMEM((GROUP * size, cells), bf16),
                pltpu.VMEM((size, cells), jnp.float32),
            ],
            compiler_params=params,
            name="mix",
        )(*flat, dense, weight_rows)

    window = ((0, 0),) + tuple((1, k) for k in range(half + 1))
    mixed_early = mix([rims, early], window, weights[:half])
    back_early = [mixed_early[0]] + [swap(mixed_early[p], p) for p in range(1, count)]
    window = ((0, half - 1), (0, half)) + tuple((1, k) for k in range(slab - half))
    mixed_late = mix([early, late], window, weights[half:])
    back_late = [mixed_late[0]] + [swap(mixed_late[p], p) for p in range(1, count)]

    outer = jnp.stack([b[0] for b in back_early])
    bottom = lax.dynamic_index_in_dim(outer, z, 0, keepdims=False).astype(jnp.float32)
    top = lax.dynamic_index_in_dim(outer, z ^ (count - 1), 0, keepdims=False).astype(jnp.float32)
    first_bottom = (source[:, 0] - bottom) * (inverse[0] / cheb_center)
    first_top = (source[:, -1] - top) * (inverse[-1] / cheb_center)
    low = lax.ppermute(first_top, "dom", upward)
    high = lax.ppermute(first_bottom, "dom", downward)

    sigma = cheb_center / cheb_radius
    rho_zero = 1.0 / sigma
    rho_one = 1.0 / (2.0 * sigma - rho_zero)
    block = min(16, here)
    image_spec = pl.BlockSpec((half, block, cells), lambda i: (0, i, 0))
    flat_spec = pl.BlockSpec((block, rows, cells), lambda i: (i, 0, 0))
    row_spec = pl.BlockSpec((block, cells), lambda i: (i, 0))
    updated, residual = pl.pallas_call(
        functools.partial(post_kernel, count, slab, half, rows, rho_zero, rho_one),
        grid=(here // block,),
        out_shape=[jax.ShapeDtypeStruct((here, rows, cells), jnp.float32)] * 2,
        in_specs=[in_smem()]
        + [image_spec] * (2 * count)
        + [flat_spec, flat_spec, row_spec, row_spec]
        + [
            pl.BlockSpec((6, rows, cells), lambda i: (0, 0, 0)),
            pl.BlockSpec((rows, cells), lambda i: (0, 0)),
        ],
        out_specs=[flat_spec, flat_spec],
        scratch_shapes=[pltpu.VMEM((rows, block, cells), jnp.float32)],
        compiler_params=params,
        name="post",
    )(
        z_arg,
        *back_early,
        *back_late,
        source,
        iterate,
        low,
        high,
        faces,
        inverse,
    )
    return updated, residual


def solution(mesh):
    return jax.shard_map(
        body,
        mesh=mesh,
        in_specs=(
            P("mode", "dom", None),
            P("mode", "dom", None),
            P("dom", None),
            P(None, "dom", None),
            P(),
            P(),
        ),
        out_specs=(P("mode", "dom", None), P("mode", "dom", None)),
        check_vma=False,
    )
```

```python
import functools
import jax
import jax.numpy as jnp
from jax import lax
from jax.experimental import pallas as pl
from jax.experimental.pallas import tpu as pltpu
from jax.sharding import PartitionSpec as P

NZ = 16
GROUP = 5

cheb_center = 1.125
cheb_radius = 0.875
VMEM_LIMIT = 48 * 1024 * 1024


def in_vmem(count):
    return [pl.BlockSpec(memory_space=pltpu.VMEM)] * count


def in_smem():
    return pl.BlockSpec(memory_space=pltpu.SMEM)


def row_of(place, rho, slab, count, rows):
    upward = slab * place + rho
    downward = slab * place + (slab - 1 - rho)
    row = jnp.where(place < count // 2, upward, downward)
    return jnp.clip(row, 0, rows - 1)


def pack_kernel(count, slab, half, rows, z_ref, x_ref, low_ref, high_ref, *refs):
    z = z_ref[0]
    outs, turned = refs[:-1], refs[-1]
    here = turned.shape[1]
    turned[...] = jnp.swapaxes(x_ref[...], 0, 1).astype(jnp.bfloat16)
    low = low_ref[:here].astype(jnp.bfloat16)
    high = high_ref[:here].astype(jnp.bfloat16)
    for p in range(count):
        place = jnp.bitwise_xor(z, p)
        early, late = outs[2 * p : 2 * p + 2]
        for rho in range(slab + 1):
            row = row_of(place, rho, slab, count, rows)
            if rho <= half:
                early[rho + 1] = turned[row]
            else:
                late[rho - half - 1] = turned[row]
        early[0] = turned[row_of(place, -1, slab, count, rows)]

        @pl.when(place == 0)
        def _():
            early[0] = low

        @pl.when(place == count - 1)
        def _():
            early[0] = high


def masks(cells):
    lane = lax.broadcasted_iota(jnp.int32, (1, cells), 1)
    in_z = lane % NZ
    one = jnp.float32(1.0)
    zero = jnp.float32(0.0)
    return (
        jnp.where(lane < cells - NZ, one, zero),
        jnp.where(lane >= NZ, one, zero),
        jnp.where(in_z < NZ - 1, one, zero),
        jnp.where(in_z > 0, one, zero),
    )


def beside(field, mask_set):
    cells = field.shape[-1]
    axis = field.ndim - 1
    return (
        pltpu.roll(field, cells - NZ, axis) * mask_set[0],
        pltpu.roll(field, NZ, axis) * mask_set[1],
        pltpu.roll(field, cells - 1, axis) * mask_set[2],
        pltpu.roll(field, 1, axis) * mask_set[3],
    )


def setup_kernel(
    groups,
    modes_here,
    z_ref,
    entry_ref,
    value_ref,
    mean_ref,
    fields_ref,
    low_ref,
    high_ref,
    dense_ref,
    own_ref,
    weight_ref,
    faces_ref,
    inverse_ref,
):
    fields, rows, cells = fields_ref.shape
    size = dense_ref.shape[1]
    entries = entry_ref.shape[1]
    flip = z_ref[0] * modes_here
    mode_id = jnp.bitwise_xor(lax.broadcasted_iota(jnp.int32, (size, entries), 0), flip)
    pick = jnp.where(mode_id == entry_ref[0:1], 1.0, 0.0).astype(jnp.bfloat16)
    depth = -(-(fields + 1) // 16) * 16
    here = lax.broadcasted_iota(jnp.int32, (depth, entries), 0) == entry_ref[2:3]
    partner = jnp.where(here, entry_ref[1:2].astype(jnp.float32), 0.0).astype(jnp.bfloat16)
    value = jnp.where(here, value_ref[...], 0.0).astype(jnp.bfloat16)
    dims = (((1,), (1,)), ((), ()))
    partner_of = lax.dot_general(pick, partner, dims, preferred_element_type=jnp.float32)
    value_of = lax.dot_general(pick, value, dims, preferred_element_type=jnp.float32)
    column = jnp.bitwise_xor(lax.broadcasted_iota(jnp.int32, (size, size), 1), flip)
    column = column.astype(jnp.float32)
    own_ref[...] = jnp.broadcast_to(value_of[:, 0:1], own_ref.shape)
    for g in range(groups):
        for k in range(GROUP):
            at = 1 + g * GROUP + k
            if at > fields:
                tile = jnp.zeros((size, size), jnp.float32)
            else:
                tile = jnp.where(
                    column == partner_of[:, at : at + 1], value_of[:, at : at + 1], 0.0
                )
            dense_ref[g, :, k * size : (k + 1) * size] = tile.astype(jnp.bfloat16)
    mask_set = masks(cells)
    place = lax.broadcasted_iota(jnp.int32, (rows, cells), 0)
    start = low_ref.shape[0] - fields - 1
    for field in range(fields + 1):
        centre = mean_ref[...] if field == 0 else fields_ref[field - 1]
        low = low_ref[start + field : start + field + 1, :]
        high = high_ref[start + field : start + field + 1, :]
        up = jnp.where(place == rows - 1, high, pltpu.roll(centre, rows - 1, 0))
        down = jnp.where(place == 0, low, pltpu.roll(centre, 1, 0))
        diag = None
        for f, other in enumerate((up, down) + beside(centre, mask_set)):
            weight = 0.5 * (centre + other)
            weight_ref[f, field] = weight
            if field == 0:
                diag = weight if diag is None else diag + weight
                faces_ref[f] = weight if f < 2 else weight * mask_set[f - 2]
        if field == 0:
            inverse_ref[...] = 1.0 / diag


def mix_kernel(count, slab, half, groups, fields, window, begin, z_ref, *refs):
    arrays = max(a for a, _ in window) + 1
    sources = refs[: arrays * count]
    dense_ref, own_ref, weight_ref = refs[arrays * count : arrays * count + 3]
    outs = refs[arrays * count + 3 : arrays * count + 3 + count]
    rows_ref, diff_ref, term_ref, total_ref = refs[arrays * count + 3 + count :]
    size, cells = total_ref.shape
    here = size // count
    bf16 = jnp.bfloat16
    for k, (array, row) in enumerate(window):
        for p in range(count):
            rows_ref[k, p * here : (p + 1) * here, :] = sources[array * count + p][row]
    mask_set = masks(cells)
    z = z_ref[0]
    rows = weight_ref.shape[2]
    ahead = jnp.where(z < count // 2, 0, 1)
    faces = (ahead, 1 - ahead, 2, 3, 4, 5)

    def each_row(r, carry):
        row = row_of(z, begin + r, slab, count, rows)
        mean_weights = [weight_ref[f, 0, pl.ds(row, 1), :] for f in faces]
        for t in range(0, size, 16):
            at = slice(t, t + 16)
            centre = rows_ref[r + 1, at].astype(jnp.float32)
            others = (rows_ref[r + 2, at].astype(jnp.float32), rows_ref[r, at].astype(jnp.float32))
            mean = None
            for f, other in enumerate(others + beside(centre, mask_set)):
                diff = centre - other
                diff_ref[f, at] = diff.astype(bf16)
                part = mean_weights[f] * diff
                mean = part if mean is None else mean + part
            total_ref[at, :] = jnp.concatenate([own_ref[at]] * (cells // 128), 1) * mean
        for g in range(groups):
            for k in range(GROUP):
                field = min(1 + g * GROUP + k, fields - 1)
                weights = [
                    jnp.broadcast_to(weight_ref[f, field, pl.ds(row, 1), :], (16, cells))
                    for f in faces
                ]
                weights = [w.astype(bf16) for w in weights]
                for t in range(0, size, 16):
                    part = [weights[f] * diff_ref[f, t : t + 16] for f in range(6)]
                    term = ((part[0] + part[1]) + (part[2] + part[3])) + (part[4] + part[5])
                    term_ref[k * size + t : k * size + t + 16, :] = term
            total_ref[...] += jnp.dot(
                dense_ref[g], term_ref[...], preferred_element_type=jnp.float32
            )
        for p in range(count):
            outs[p][r] = total_ref[p * here : (p + 1) * here, :].astype(bf16)
        return carry

    lax.fori_loop(0, half, each_row, 0)


def post_kernel(count, slab, half, rows, rho_zero, rho_one, z_ref, *refs):
    early = refs[:count]
    late = refs[count : 2 * count]
    source, iterate, low, high, faces, inverse = refs[2 * count : 2 * count + 6]
    updated, residual, image = refs[2 * count + 6 :]
    z = z_ref[0]
    modes, _, cells = source.shape
    for p in range(count):
        place = jnp.bitwise_xor(z, p)
        for rho in range(slab):
            part = early[p][rho] if rho < half else late[p][rho - half]
            image[row_of(place, rho, slab, count, rows)] = part.astype(jnp.float32)
    residual[...] = source[...] - jnp.swapaxes(image[...], 0, 1)
    place = lax.broadcasted_iota(jnp.int32, (rows, cells), 0)
    inv = inverse[...]
    for m in range(modes):
        res = residual[m]
        first = res * (inv * (1.0 / cheb_center))
        up = jnp.where(place == rows - 1, high[m : m + 1, :], pltpu.roll(first, rows - 1, 0))
        down = jnp.where(place == 0, low[m : m + 1, :], pltpu.roll(first, 1, 0))
        near = faces[0] * up + faces[1] * down
        near = near + faces[2] * pltpu.roll(first, cells - NZ, 1)
        near = near + faces[3] * pltpu.roll(first, NZ, 1)
        near = near + faces[4] * pltpu.roll(first, cells - 1, 1)
        near = near + faces[5] * pltpu.roll(first, 1, 1)
        smoothed = (1.0 - 1.0 / cheb_center) * res + near
        step = (1.0 + rho_one * rho_zero) * first + (2.0 * rho_one / cheb_radius) * smoothed * inv
        updated[m] = iterate[m] + step


def body(iterate, source, mean_coef, kl_fields, tri_index, tri_value):
    count = lax.axis_size("mode")
    doms = lax.axis_size("dom")
    z = lax.axis_index("mode")
    z_arg = z.astype(jnp.int32).reshape(1)
    here, rows, cells = iterate.shape
    size = here * count
    slab = rows // count
    half = slab // 2
    fields = kl_fields.shape[0] + 1
    groups = -(-(fields - 1) // GROUP)
    bf16 = jnp.bfloat16
    params = pltpu.CompilerParams(vmem_limit_bytes=VMEM_LIMIT)

    upward = [(i, i + 1) for i in range(doms - 1)]
    downward = [(b, a) for a, b in upward]
    low_rim, high_rim = (
        lax.ppermute(
            jnp.concatenate([iterate[:, at], mean_coef[at][None], kl_fields[:, at]], 0), "dom", pairs
        )
        for at, pairs in ((rows - 1, upward), (0, downward))
    )

    packed = pl.pallas_call(
        functools.partial(pack_kernel, count, slab, half, rows),
        out_shape=[
            jax.ShapeDtypeStruct((half + 2, here, cells), bf16),
            jax.ShapeDtypeStruct((slab - half, here, cells), bf16),
        ]
        * count,
        in_specs=[in_smem()] + in_vmem(3),
        out_specs=in_vmem(2 * count),
        scratch_shapes=[pltpu.VMEM((rows, here, cells), bf16)],
        compiler_params=params,
        name="pack",
    )(z_arg, iterate, low_rim, high_rim)

    def swap(array, p):
        return lax.ppermute(array, "mode", [(i, i ^ p) for i in range(count)])

    early = [packed[0]] + [swap(packed[2 * p], p) for p in range(1, count)]
    late = [packed[1]] + [swap(packed[2 * p + 1], p) for p in range(1, count)]

    dense, own, weights, faces, inverse = pl.pallas_call(
        functools.partial(setup_kernel, groups, here),
        out_shape=[
            jax.ShapeDtypeStruct((groups, size, GROUP * size), bf16),
            jax.ShapeDtypeStruct((size, 128), jnp.float32),
            jax.ShapeDtypeStruct((6, fields, rows, cells), jnp.float32),
            jax.ShapeDtypeStruct((6, rows, cells), jnp.float32),
            jax.ShapeDtypeStruct((rows, cells), jnp.float32),
        ],
        in_specs=[in_smem()] + in_vmem(6),
        out_specs=in_vmem(5),
        compiler_params=params,
        name="setup",
    )(z_arg, tri_index.T, tri_value[None], mean_coef, kl_fields, low_rim, high_rim)

    def mix(arrays, window, begin):
        flat = [a for group in arrays for a in group]
        return pl.pallas_call(
            functools.partial(mix_kernel, count, slab, half, groups, fields, window, begin),
            out_shape=[jax.ShapeDtypeStruct((half, here, cells), bf16)] * count,
            in_specs=[in_smem()] + in_vmem(len(flat) + 3),
            out_specs=in_vmem(count),
            scratch_shapes=[
                pltpu.VMEM((half + 2, size, cells), bf16),
                pltpu.VMEM((6, size, cells), bf16),
                pltpu.VMEM((GROUP * size, cells), bf16),
                pltpu.VMEM((size, cells), jnp.float32),
            ],
            compiler_params=params,
            name="mix",
        )(z_arg, *flat, dense, own, weights)

    window = tuple((0, k) for k in range(half + 2))
    mixed_early = mix([early], window, 0)
    back_early = [mixed_early[0]] + [swap(mixed_early[p], p) for p in range(1, count)]
    window = ((0, half), (0, half + 1)) + tuple((1, k) for k in range(slab - half))
    mixed_late = mix([early, late], window, half)
    back_late = [mixed_late[0]] + [swap(mixed_late[p], p) for p in range(1, count)]

    outer = jnp.stack([b[0] for b in back_early])
    bottom = lax.dynamic_index_in_dim(outer, z, 0, keepdims=False).astype(jnp.float32)
    top = lax.dynamic_index_in_dim(outer, z ^ (count - 1), 0, keepdims=False).astype(jnp.float32)
    first_bottom = (source[:, 0] - bottom) * (inverse[0] / cheb_center)
    first_top = (source[:, -1] - top) * (inverse[-1] / cheb_center)
    low = lax.ppermute(first_top, "dom", upward)
    high = lax.ppermute(first_bottom, "dom", downward)

    sigma = cheb_center / cheb_radius
    rho_zero = 1.0 / sigma
    rho_one = 1.0 / (2.0 * sigma - rho_zero)
    block = min(16, here)
    image_spec = pl.BlockSpec((half, block, cells), lambda i: (0, i, 0))
    flat_spec = pl.BlockSpec((block, rows, cells), lambda i: (i, 0, 0))
    row_spec = pl.BlockSpec((block, cells), lambda i: (i, 0))
    updated, residual = pl.pallas_call(
        functools.partial(post_kernel, count, slab, half, rows, rho_zero, rho_one),
        grid=(here // block,),
        out_shape=[jax.ShapeDtypeStruct((here, rows, cells), jnp.float32)] * 2,
        in_specs=[in_smem()]
        + [image_spec] * (2 * count)
        + [flat_spec, flat_spec, row_spec, row_spec]
        + [
            pl.BlockSpec((6, rows, cells), lambda i: (0, 0, 0)),
            pl.BlockSpec((rows, cells), lambda i: (0, 0)),
        ],
        out_specs=[flat_spec, flat_spec],
        scratch_shapes=[pltpu.VMEM((rows, block, cells), jnp.float32)],
        compiler_params=params,
        name="post",
    )(
        z_arg,
        *back_early,
        *back_late,
        source,
        iterate,
        low,
        high,
        faces,
        inverse,
    )
    return updated, residual


def solution(mesh):
    return jax.shard_map(
        body,
        mesh=mesh,
        in_specs=(
            P("mode", "dom", None),
            P("mode", "dom", None),
            P("dom", None),
            P(None, "dom", None),
            P(),
            P(),
        ),
        out_specs=(P("mode", "dom", None), P("mode", "dom", None)),
        check_vma=False,
    )
```

```python
import functools
import jax
import jax.numpy as jnp
from jax import lax
from jax.experimental import pallas as pl
from jax.experimental.pallas import tpu as pltpu
from jax.sharding import PartitionSpec as P

NZ = 16
GROUP = 5

cheb_center = 1.125
cheb_radius = 0.875
SMALL = pl.CostEstimate(flops=1, bytes_accessed=1, transcendentals=0)
VMEM_LIMIT = 48 * 1024 * 1024


def in_vmem(count):
    return [pl.BlockSpec(memory_space=pltpu.VMEM)] * count


def in_smem():
    return pl.BlockSpec(memory_space=pltpu.SMEM)


def row_of(place, rho, slab, count, rows):
    upward = slab * place + rho
    downward = slab * place + (slab - 1 - rho)
    row = jnp.where(place < count // 2, upward, downward)
    return jnp.clip(row, 0, rows - 1)


def turn_kernel(x_ref, turned):
    turned[...] = jnp.swapaxes(x_ref[...], 0, 1).astype(jnp.bfloat16)


def late_kernel(count, slab, half, rows, z_ref, turned, after, *outs):
    z = z_ref[0]
    for p in range(count):
        place = jnp.bitwise_xor(z, p)
        for rho in range(half + 1, slab + 1):
            outs[p][rho - half - 1] = turned[row_of(place, rho, slab, count, rows)]


def early_kernel(count, slab, half, rows, z_ref, turned, low_ref, high_ref, *outs):
    z = z_ref[0]
    here = turned.shape[1]
    for p in range(count):
        place = jnp.bitwise_xor(z, p)
        for rho in range(-1, half + 1):
            outs[p][rho + 1] = turned[row_of(place, rho, slab, count, rows)]

        @pl.when(place == 0)
        def _():
            outs[p][0] = low_ref[:here].astype(jnp.bfloat16)

        @pl.when(place == count - 1)
        def _():
            outs[p][0] = high_ref[:here].astype(jnp.bfloat16)


def masks(cells):
    lane = lax.broadcasted_iota(jnp.int32, (1, cells), 1)
    in_z = lane % NZ
    one = jnp.float32(1.0)
    zero = jnp.float32(0.0)
    return (
        jnp.where(lane < cells - NZ, one, zero),
        jnp.where(lane >= NZ, one, zero),
        jnp.where(in_z < NZ - 1, one, zero),
        jnp.where(in_z > 0, one, zero),
    )


def beside(field, mask_set):
    cells = field.shape[-1]
    axis = field.ndim - 1
    return (
        pltpu.roll(field, cells - NZ, axis) * mask_set[0],
        pltpu.roll(field, NZ, axis) * mask_set[1],
        pltpu.roll(field, cells - 1, axis) * mask_set[2],
        pltpu.roll(field, 1, axis) * mask_set[3],
    )


def dense_kernel(groups, fields, modes_here, z_ref, entry_ref, value_ref, dense_ref, own_ref):
    size = dense_ref.shape[1]
    entries = entry_ref.shape[1]
    flip = z_ref[0] * modes_here
    mode_id = jnp.bitwise_xor(lax.broadcasted_iota(jnp.int32, (size, entries), 0), flip)
    pick = jnp.where(mode_id == entry_ref[0:1], 1.0, 0.0).astype(jnp.bfloat16)
    depth = -(-fields // 16) * 16
    here = lax.broadcasted_iota(jnp.int32, (depth, entries), 0) == entry_ref[2:3]
    partner = jnp.where(here, entry_ref[1:2].astype(jnp.float32), 0.0).astype(jnp.bfloat16)
    value = jnp.where(here, value_ref[...], 0.0).astype(jnp.bfloat16)
    dims = (((1,), (1,)), ((), ()))
    partner_of = lax.dot_general(pick, partner, dims, preferred_element_type=jnp.float32)
    value_of = lax.dot_general(pick, value, dims, preferred_element_type=jnp.float32)
    column = jnp.bitwise_xor(lax.broadcasted_iota(jnp.int32, (size, size), 1), flip)
    column = column.astype(jnp.float32)
    own_ref[...] = jnp.broadcast_to(value_of[:, 0:1], own_ref.shape)
    for g in range(groups):
        for k in range(GROUP):
            at = 1 + g * GROUP + k
            if at >= fields:
                tile = jnp.zeros((size, size), jnp.float32)
            else:
                tile = jnp.where(
                    column == partner_of[:, at : at + 1], value_of[:, at : at + 1], 0.0
                )
            dense_ref[g, :, k * size : (k + 1) * size] = tile.astype(jnp.bfloat16)


def weight_kernel(
    mean_ref, fields_ref, low_ref, high_ref, weight_ref, faces_ref, inverse_ref, stack_ref, turned
):
    fields, rows, cells = fields_ref.shape
    deep = stack_ref.shape[0]
    mask_set = masks(cells)
    start = low_ref.shape[0] - deep
    stack_ref[0] = mean_ref[...]
    stack_ref[1 : fields + 1] = fields_ref[...]
    stack_ref[fields + 1 :] = jnp.zeros((deep - fields - 1, rows, cells), jnp.float32)
    turned[...] = jnp.swapaxes(stack_ref[...], 0, 1)
    for row in range(rows):
        centre = turned[row]
        up = high_ref[start:, :] if row == rows - 1 else turned[row + 1]
        down = low_ref[start:, :] if row == 0 else turned[row - 1]
        for f, other in enumerate((up, down) + beside(centre, mask_set)):
            weight_ref[row, f] = 0.5 * (centre + other)
    place = lax.broadcasted_iota(jnp.int32, (rows, cells), 0)
    centre = mean_ref[...]
    high, low = high_ref[start : start + 1, :], low_ref[start : start + 1, :]
    up = jnp.where(place == rows - 1, high, pltpu.roll(centre, rows - 1, 0))
    down = jnp.where(place == 0, low, pltpu.roll(centre, 1, 0))
    diag = None
    for f, other in enumerate((up, down) + beside(centre, mask_set)):
        weight = 0.5 * (centre + other)
        diag = weight if diag is None else diag + weight
        faces_ref[f] = weight if f < 2 else weight * mask_set[f - 2]
    inverse_ref[...] = 1.0 / diag


def mix_kernel(count, slab, half, groups, fields, window, begin, z_ref, *refs):
    arrays = max(a for a, _ in window) + 1
    sources = refs[: arrays * count]
    dense_ref, own_ref, weight_ref = refs[arrays * count : arrays * count + 3]
    outs = refs[arrays * count + 3 : arrays * count + 3 + count]
    rows_ref, diff_ref, term_ref, total_ref = refs[arrays * count + 3 + count :]
    size, cells = total_ref.shape
    here = size // count
    bf16 = jnp.bfloat16
    for k, (array, row) in enumerate(window):
        for p in range(count):
            rows_ref[k, p * here : (p + 1) * here, :] = sources[array * count + p][row]
    mask_set = masks(cells)
    z = z_ref[0]
    rows = weight_ref.shape[0]
    ahead = jnp.where(z < count // 2, 0, 1)
    faces = (ahead, 1 - ahead, 2, 3, 4, 5)

    def each_row(r, carry):
        row = row_of(z, begin + r, slab, count, rows)
        mean_weights = [weight_ref[row, f, 0:1, :] for f in faces]
        for t in range(0, size, 16):
            at = slice(t, t + 16)
            centre = rows_ref[r + 1, at].astype(jnp.float32)
            others = (rows_ref[r + 2, at].astype(jnp.float32), rows_ref[r, at].astype(jnp.float32))
            mean = None
            for f, other in enumerate(others + beside(centre, mask_set)):
                diff = centre - other
                diff_ref[f, at] = diff.astype(bf16)
                part = mean_weights[f] * diff
                mean = part if mean is None else mean + part
            total_ref[at, :] = jnp.concatenate([own_ref[at]] * (cells // 128), 1) * mean
        for g in range(groups):
            for k in range(GROUP):
                field = min(1 + g * GROUP + k, fields - 1)
                weights = [
                    jnp.broadcast_to(weight_ref[row, f, field : field + 1, :], (16, cells))
                    for f in faces
                ]
                weights = [w.astype(bf16) for w in weights]
                for t in range(0, size, 16):
                    part = [weights[f] * diff_ref[f, t : t + 16] for f in range(6)]
                    term = ((part[0] + part[1]) + (part[2] + part[3])) + (part[4] + part[5])
                    term_ref[k * size + t : k * size + t + 16, :] = term
            total_ref[...] += jnp.dot(
                dense_ref[g], term_ref[...], preferred_element_type=jnp.float32
            )
        for p in range(count):
            outs[p][r] = total_ref[p * here : (p + 1) * here, :].astype(bf16)
        return carry

    lax.fori_loop(0, half, each_row, 0)


def post_kernel(count, slab, half, rows, rho_zero, rho_one, z_ref, *refs):
    early = refs[:count]
    late = refs[count : 2 * count]
    source, iterate, low, high, faces, inverse = refs[2 * count : 2 * count + 6]
    updated, residual, image = refs[2 * count + 6 :]
    z = z_ref[0]
    modes, _, cells = source.shape
    for p in range(count):
        place = jnp.bitwise_xor(z, p)
        for rho in range(slab):
            part = early[p][rho] if rho < half else late[p][rho - half]
            image[row_of(place, rho, slab, count, rows)] = part.astype(jnp.float32)
    residual[...] = source[...] - jnp.swapaxes(image[...], 0, 1)
    place = lax.broadcasted_iota(jnp.int32, (rows, cells), 0)
    inv = inverse[...]
    for m in range(modes):
        res = residual[m]
        first = res * (inv * (1.0 / cheb_center))
        up = jnp.where(place == rows - 1, high[m : m + 1, :], pltpu.roll(first, rows - 1, 0))
        down = jnp.where(place == 0, low[m : m + 1, :], pltpu.roll(first, 1, 0))
        near = faces[0] * up + faces[1] * down
        near = near + faces[2] * pltpu.roll(first, cells - NZ, 1)
        near = near + faces[3] * pltpu.roll(first, NZ, 1)
        near = near + faces[4] * pltpu.roll(first, cells - 1, 1)
        near = near + faces[5] * pltpu.roll(first, 1, 1)
        smoothed = (1.0 - 1.0 / cheb_center) * res + near
        step = (1.0 + rho_one * rho_zero) * first + (2.0 * rho_one / cheb_radius) * smoothed * inv
        updated[m] = iterate[m] + step


def body(iterate, source, mean_coef, kl_fields, tri_index, tri_value):
    count = lax.axis_size("mode")
    doms = lax.axis_size("dom")
    z = lax.axis_index("mode")
    z_arg = z.astype(jnp.int32).reshape(1)
    here, rows, cells = iterate.shape
    size = here * count
    slab = rows // count
    half = slab // 2
    fields = kl_fields.shape[0] + 1
    groups = -(-(fields - 1) // GROUP)
    bf16 = jnp.bfloat16
    params = pltpu.CompilerParams(vmem_limit_bytes=VMEM_LIMIT)

    deep = -(-fields // 8) * 8

    upward = [(i, i + 1) for i in range(doms - 1)]
    downward = [(b, a) for a, b in upward]
    filler = jnp.zeros((deep - fields, cells), jnp.float32)
    low_rim, high_rim = (
        lax.ppermute(
            jnp.concatenate([iterate[:, at], mean_coef[at][None], kl_fields[:, at], filler], 0),
            "dom",
            pairs,
        )
        for at, pairs in ((rows - 1, upward), (0, downward))
    )
    turned = pl.pallas_call(
        turn_kernel,
        out_shape=jax.ShapeDtypeStruct((rows, here, cells), bf16),
        in_specs=in_vmem(1),
        out_specs=in_vmem(1)[0],
        compiler_params=params,
        cost_estimate=SMALL,
        name="turn",
    )(iterate)
    early = pl.pallas_call(
        functools.partial(early_kernel, count, slab, half, rows),
        out_shape=[jax.ShapeDtypeStruct((half + 2, here, cells), bf16)] * count,
        in_specs=[in_smem()] + in_vmem(3),
        out_specs=in_vmem(count),
        compiler_params=params,
        cost_estimate=SMALL,
        name="early",
    )(z_arg, turned, low_rim, high_rim)

    def swap(array, p):
        if p == 0:
            return array
        return lax.ppermute(array, "mode", [(i, i ^ p) for i in range(count)])

    entries, values, low_coef, high_coef, _ = lax.optimization_barrier(
        (tri_index, tri_value, low_rim, high_rim, early[0])
    )
    early = [swap(e, p) for p, e in enumerate(early)]
    dense, own = pl.pallas_call(
        functools.partial(dense_kernel, groups, fields, here),
        out_shape=[
            jax.ShapeDtypeStruct((groups, size, GROUP * size), bf16),
            jax.ShapeDtypeStruct((size, 128), jnp.float32),
        ],
        in_specs=[in_smem()] + in_vmem(2),
        out_specs=in_vmem(2),
        compiler_params=params,
        cost_estimate=SMALL,
        name="dense",
    )(z_arg, entries.T, values[None])
    weights, faces, inverse = pl.pallas_call(
        weight_kernel,
        out_shape=[
            jax.ShapeDtypeStruct((rows, 6, deep, cells), jnp.float32),
            jax.ShapeDtypeStruct((6, rows, cells), jnp.float32),
            jax.ShapeDtypeStruct((rows, cells), jnp.float32),
        ],
        in_specs=in_vmem(4),
        out_specs=in_vmem(3),
        scratch_shapes=[
            pltpu.VMEM((deep, rows, cells), jnp.float32),
            pltpu.VMEM((rows, deep, cells), jnp.float32),
        ],
        compiler_params=params,
        cost_estimate=SMALL,
        name="weights",
    )(mean_coef, kl_fields, low_coef, high_coef)
    late = pl.pallas_call(
        functools.partial(late_kernel, count, slab, half, rows),
        out_shape=[jax.ShapeDtypeStruct((slab - half, here, cells), bf16)] * count,
        in_specs=[in_smem()] + in_vmem(2),
        out_specs=in_vmem(count),
        compiler_params=params,
        cost_estimate=SMALL,
        name="late",
    )(z_arg, turned, inverse)
    late = [swap(a, p) for p, a in enumerate(late)]

    def mix(arrays, window, begin):
        flat = [a for group in arrays for a in group]
        return pl.pallas_call(
            functools.partial(mix_kernel, count, slab, half, groups, fields, window, begin),
            out_shape=[jax.ShapeDtypeStruct((half, here, cells), bf16)] * count,
            in_specs=[in_smem()] + in_vmem(len(flat) + 3),
            out_specs=in_vmem(count),
            scratch_shapes=[
                pltpu.VMEM((half + 2, size, cells), bf16),
                pltpu.VMEM((6, size, cells), bf16),
                pltpu.VMEM((GROUP * size, cells), bf16),
                pltpu.VMEM((size, cells), jnp.float32),
            ],
            compiler_params=params,
            name="mix",
        )(z_arg, *flat, dense, own, weights)

    window = tuple((0, k) for k in range(half + 2))
    back_early = [swap(a, p) for p, a in enumerate(mix([early], window, 0))]
    window = ((0, half), (0, half + 1)) + tuple((1, k) for k in range(slab - half))
    back_late = [swap(a, p) for p, a in enumerate(mix([early, late], window, half))]

    outer = jnp.stack([b[0] for b in back_early])
    bottom = lax.dynamic_index_in_dim(outer, z, 0, keepdims=False).astype(jnp.float32)
    top = lax.dynamic_index_in_dim(outer, z ^ (count - 1), 0, keepdims=False).astype(jnp.float32)
    first_bottom = (source[:, 0] - bottom) * (inverse[0] / cheb_center)
    first_top = (source[:, -1] - top) * (inverse[-1] / cheb_center)
    low = lax.ppermute(first_top, "dom", upward)
    high = lax.ppermute(first_bottom, "dom", downward)

    sigma = cheb_center / cheb_radius
    rho_zero = 1.0 / sigma
    rho_one = 1.0 / (2.0 * sigma - rho_zero)
    block = min(16, here)
    image_spec = pl.BlockSpec((half, block, cells), lambda i: (0, i, 0))
    flat_spec = pl.BlockSpec((block, rows, cells), lambda i: (i, 0, 0))
    row_spec = pl.BlockSpec((block, cells), lambda i: (i, 0))
    updated, residual = pl.pallas_call(
        functools.partial(post_kernel, count, slab, half, rows, rho_zero, rho_one),
        grid=(here // block,),
        out_shape=[jax.ShapeDtypeStruct((here, rows, cells), jnp.float32)] * 2,
        in_specs=[in_smem()]
        + [image_spec] * (2 * count)
        + [flat_spec, flat_spec, row_spec, row_spec]
        + [
            pl.BlockSpec((6, rows, cells), lambda i: (0, 0, 0)),
            pl.BlockSpec((rows, cells), lambda i: (0, 0)),
        ],
        out_specs=[flat_spec, flat_spec],
        scratch_shapes=[pltpu.VMEM((rows, block, cells), jnp.float32)],
        compiler_params=params,
        name="post",
    )(
        z_arg,
        *back_early,
        *back_late,
        source,
        iterate,
        low,
        high,
        faces,
        inverse,
    )
    return updated, residual


def solution(mesh):
    return jax.shard_map(
        body,
        mesh=mesh,
        in_specs=(
            P("mode", "dom", None),
            P("mode", "dom", None),
            P("dom", None),
            P(None, "dom", None),
            P(),
            P(),
        ),
        out_specs=(P("mode", "dom", None), P("mode", "dom", None)),
        check_vma=False,
    )
```

```python
import functools
import jax
import jax.numpy as jnp
from jax import lax
from jax.experimental import pallas as pl
from jax.experimental.pallas import tpu as pltpu
from jax.sharding import PartitionSpec as P

NZ = 16
GROUP = 5

cheb_center = 1.125
cheb_radius = 0.875
SMALL = pl.CostEstimate(flops=1, bytes_accessed=1, transcendentals=0)
VMEM_LIMIT = 48 * 1024 * 1024


def in_vmem(count):
    return [pl.BlockSpec(memory_space=pltpu.VMEM)] * count


def in_smem():
    return pl.BlockSpec(memory_space=pltpu.SMEM)


def row_of(place, rho, slab, count, rows):
    upward = slab * place + rho
    downward = slab * place + (slab - 1 - rho)
    row = jnp.where(place < count // 2, upward, downward)
    return jnp.clip(row, 0, rows - 1)


def turn_kernel(x_ref, mean_ref, fields_ref, turned, last, first):
    step = pl.program_id(0)
    modes, rows, _ = x_ref.shape
    block = jnp.swapaxes(x_ref[...], 0, 1)
    turned[...] = block.astype(jnp.bfloat16)
    at = pl.ds(pl.multiple_of(step * modes, modes), modes)
    first[at, :] = block[0]
    last[at, :] = block[rows - 1]

    @pl.when(step == pl.num_programs(0) - 1)
    def _():
        fields = fields_ref.shape[0]
        here = modes * pl.num_programs(0)
        for out, row in ((first, 0), (last, rows - 1)):
            out[here : here + 1, :] = mean_ref[row : row + 1, :]
            for field in range(fields):
                out[here + 1 + field : here + 2 + field, :] = fields_ref[field, row : row + 1, :]
            rest = out.shape[0] - here - 1 - fields
            out[here + 1 + fields :, :] = jnp.zeros((rest, out.shape[1]), jnp.float32)


def late_kernel(count, slab, half, rows, z_ref, turned, after, *outs):
    z = z_ref[0]
    for p in range(count):
        place = jnp.bitwise_xor(z, p)
        for rho in range(half + 1, slab + 1):
            outs[p][rho - half - 1] = turned[row_of(place, rho, slab, count, rows)]


def early_kernel(count, slab, half, rows, z_ref, turned, low_ref, high_ref, *outs):
    z = z_ref[0]
    here = turned.shape[1]
    for p in range(count):
        place = jnp.bitwise_xor(z, p)
        for rho in range(-1, half + 1):
            outs[p][rho + 1] = turned[row_of(place, rho, slab, count, rows)]

        @pl.when(place == 0)
        def _():
            outs[p][0] = low_ref[:here].astype(jnp.bfloat16)

        @pl.when(place == count - 1)
        def _():
            outs[p][0] = high_ref[:here].astype(jnp.bfloat16)


def masks(cells):
    lane = lax.broadcasted_iota(jnp.int32, (1, cells), 1)
    in_z = lane % NZ
    one = jnp.float32(1.0)
    zero = jnp.float32(0.0)
    return (
        jnp.where(lane < cells - NZ, one, zero),
        jnp.where(lane >= NZ, one, zero),
        jnp.where(in_z < NZ - 1, one, zero),
        jnp.where(in_z > 0, one, zero),
    )


def beside(field, mask_set):
    cells = field.shape[-1]
    axis = field.ndim - 1
    return (
        pltpu.roll(field, cells - NZ, axis) * mask_set[0],
        pltpu.roll(field, NZ, axis) * mask_set[1],
        pltpu.roll(field, cells - 1, axis) * mask_set[2],
        pltpu.roll(field, 1, axis) * mask_set[3],
    )


def dense_kernel(groups, fields, modes_here, z_ref, entry_ref, value_ref, dense_ref, own_ref):
    size = dense_ref.shape[1]
    entries = entry_ref.shape[1]
    flip = z_ref[0] * modes_here
    mode_id = jnp.bitwise_xor(lax.broadcasted_iota(jnp.int32, (size, entries), 0), flip)
    pick = jnp.where(mode_id == entry_ref[0:1], 1.0, 0.0).astype(jnp.bfloat16)
    depth = -(-fields // 16) * 16
    here = lax.broadcasted_iota(jnp.int32, (depth, entries), 0) == entry_ref[2:3]
    partner = jnp.where(here, entry_ref[1:2].astype(jnp.float32), 0.0).astype(jnp.bfloat16)
    value = jnp.where(here, value_ref[...], 0.0).astype(jnp.bfloat16)
    dims = (((1,), (1,)), ((), ()))
    partner_of = lax.dot_general(pick, partner, dims, preferred_element_type=jnp.float32)
    value_of = lax.dot_general(pick, value, dims, preferred_element_type=jnp.float32)
    column = jnp.bitwise_xor(lax.broadcasted_iota(jnp.int32, (size, size), 1), flip)
    column = column.astype(jnp.float32)
    own_ref[...] = jnp.broadcast_to(value_of[:, 0:1], own_ref.shape)
    for g in range(groups):
        for k in range(GROUP):
            at = 1 + g * GROUP + k
            if at >= fields:
                tile = jnp.zeros((size, size), jnp.float32)
            else:
                tile = jnp.where(
                    column == partner_of[:, at : at + 1], value_of[:, at : at + 1], 0.0
                )
            dense_ref[g, :, k * size : (k + 1) * size] = tile.astype(jnp.bfloat16)


def weight_kernel(
    mean_ref, fields_ref, low_ref, high_ref, weight_ref, faces_ref, inverse_ref, stack_ref, turned
):
    fields, rows, cells = fields_ref.shape
    deep = stack_ref.shape[0]
    mask_set = masks(cells)
    start = low_ref.shape[0] - deep
    stack_ref[0] = mean_ref[...]
    stack_ref[1 : fields + 1] = fields_ref[...]
    stack_ref[fields + 1 :] = jnp.zeros((deep - fields - 1, rows, cells), jnp.float32)
    turned[...] = jnp.swapaxes(stack_ref[...], 0, 1)
    for row in range(rows):
        centre = turned[row]
        up = high_ref[start:, :] if row == rows - 1 else turned[row + 1]
        down = low_ref[start:, :] if row == 0 else turned[row - 1]
        for f, other in enumerate((up, down) + beside(centre, mask_set)):
            weight_ref[row, f] = 0.5 * (centre + other)
    place = lax.broadcasted_iota(jnp.int32, (rows, cells), 0)
    centre = mean_ref[...]
    high, low = high_ref[start : start + 1, :], low_ref[start : start + 1, :]
    up = jnp.where(place == rows - 1, high, pltpu.roll(centre, rows - 1, 0))
    down = jnp.where(place == 0, low, pltpu.roll(centre, 1, 0))
    diag = None
    for f, other in enumerate((up, down) + beside(centre, mask_set)):
        weight = 0.5 * (centre + other)
        diag = weight if diag is None else diag + weight
        faces_ref[f] = weight if f < 2 else weight * mask_set[f - 2]
    inverse_ref[...] = 1.0 / diag


def mix_kernel(count, slab, half, groups, fields, window, begin, z_ref, *refs):
    arrays = max(a for a, _ in window) + 1
    sources = refs[: arrays * count]
    dense_ref, own_ref, weight_ref = refs[arrays * count : arrays * count + 3]
    outs = refs[arrays * count + 3 : arrays * count + 3 + count]
    rows_ref, diff_ref, term_ref, total_ref = refs[arrays * count + 3 + count :]
    size, cells = total_ref.shape
    here = size // count
    bf16 = jnp.bfloat16
    for k, (array, row) in enumerate(window):
        for p in range(count):
            part = sources[array * count + (count - p) % count]
            rows_ref[k, p * here : (p + 1) * here, :] = part[row]
    mask_set = masks(cells)
    z = z_ref[0]
    rows = weight_ref.shape[0]
    ahead = jnp.where(z < count // 2, 0, 1)
    faces = (ahead, 1 - ahead, 2, 3, 4, 5)

    def each_row(r, carry):
        row = row_of(z, begin + r, slab, count, rows)
        mean_weights = [weight_ref[row, f, 0:1, :] for f in faces]
        for t in range(0, size, 16):
            at = slice(t, t + 16)
            centre = rows_ref[r + 1, at].astype(jnp.float32)
            others = (rows_ref[r + 2, at].astype(jnp.float32), rows_ref[r, at].astype(jnp.float32))
            mean = None
            for f, other in enumerate(others + beside(centre, mask_set)):
                diff = centre - other
                diff_ref[f, at] = diff.astype(bf16)
                part = mean_weights[f] * diff
                mean = part if mean is None else mean + part
            total_ref[at, :] = jnp.concatenate([own_ref[at]] * (cells // 128), 1) * mean
        for g in range(groups):
            for k in range(GROUP):
                field = min(1 + g * GROUP + k, fields - 1)
                weights = [
                    jnp.broadcast_to(weight_ref[row, f, field : field + 1, :], (16, cells))
                    for f in faces
                ]
                weights = [w.astype(bf16) for w in weights]
                for t in range(0, size, 16):
                    part = [weights[f] * diff_ref[f, t : t + 16] for f in range(6)]
                    term = ((part[0] + part[1]) + (part[2] + part[3])) + (part[4] + part[5])
                    term_ref[k * size + t : k * size + t + 16, :] = term
            total_ref[...] += jnp.dot(
                dense_ref[g], term_ref[...], preferred_element_type=jnp.float32
            )
        for p in range(count):
            outs[p][r] = total_ref[p * here : (p + 1) * here, :].astype(bf16)
        return carry

    lax.fori_loop(0, half, each_row, 0)


def post_kernel(count, slab, half, rows, rho_zero, rho_one, z_ref, *refs):
    early = refs[:count]
    late = refs[count : 2 * count]
    source, iterate, low, high, faces, inverse = refs[2 * count : 2 * count + 6]
    updated, residual, image = refs[2 * count + 6 :]
    z = z_ref[0]
    modes, _, cells = source.shape
    for k in range(count):
        place = jnp.bitwise_xor(z, (count - k) % count)
        for rho in range(slab):
            part = early[k][rho] if rho < half else late[k][rho - half]
            image[row_of(place, rho, slab, count, rows)] = part.astype(jnp.float32)
    residual[...] = source[...] - jnp.swapaxes(image[...], 0, 1)
    place = lax.broadcasted_iota(jnp.int32, (rows, cells), 0)
    inv = inverse[...]
    for m in range(modes):
        res = residual[m]
        first = res * (inv * (1.0 / cheb_center))
        up = jnp.where(place == rows - 1, high[m : m + 1, :], pltpu.roll(first, rows - 1, 0))
        down = jnp.where(place == 0, low[m : m + 1, :], pltpu.roll(first, 1, 0))
        near = faces[0] * up + faces[1] * down
        near = near + faces[2] * pltpu.roll(first, cells - NZ, 1)
        near = near + faces[3] * pltpu.roll(first, NZ, 1)
        near = near + faces[4] * pltpu.roll(first, cells - 1, 1)
        near = near + faces[5] * pltpu.roll(first, 1, 1)
        smoothed = (1.0 - 1.0 / cheb_center) * res + near
        step = (1.0 + rho_one * rho_zero) * first + (2.0 * rho_one / cheb_radius) * smoothed * inv
        updated[m] = iterate[m] + step


def body(iterate, source, mean_coef, kl_fields, tri_index, tri_value):
    count = lax.axis_size("mode")
    doms = lax.axis_size("dom")
    z = lax.axis_index("mode")
    z_arg = z.astype(jnp.int32).reshape(1)
    here, rows, cells = iterate.shape
    size = here * count
    slab = rows // count
    half = slab // 2
    fields = kl_fields.shape[0] + 1
    groups = -(-(fields - 1) // GROUP)
    bf16 = jnp.bfloat16
    params = pltpu.CompilerParams(vmem_limit_bytes=VMEM_LIMIT)

    deep = -(-fields // 8) * 8

    upward = [(i, i + 1) for i in range(doms - 1)]
    downward = [(b, a) for a, b in upward]
    block = min(16, here)
    rim_shape = jax.ShapeDtypeStruct((here + deep, cells), jnp.float32)
    rim_spec = pl.BlockSpec((here + deep, cells), lambda i: (0, 0))
    turned, last_rim, first_rim = pl.pallas_call(
        turn_kernel,
        grid=(here // block,),
        out_shape=[jax.ShapeDtypeStruct((rows, here, cells), bf16), rim_shape, rim_shape],
        in_specs=[
            pl.BlockSpec((block, rows, cells), lambda i: (i, 0, 0)),
            pl.BlockSpec((rows, cells), lambda i: (0, 0)),
            pl.BlockSpec((fields - 1, rows, cells), lambda i: (0, 0, 0)),
        ],
        out_specs=[pl.BlockSpec((rows, block, cells), lambda i: (0, i, 0)), rim_spec, rim_spec],
        compiler_params=params,
        cost_estimate=SMALL,
        name="turn",
    )(iterate, mean_coef, kl_fields)
    low_rim = lax.ppermute(last_rim, "dom", upward)
    high_rim = lax.ppermute(first_rim, "dom", downward)
    early = pl.pallas_call(
        functools.partial(early_kernel, count, slab, half, rows),
        out_shape=[jax.ShapeDtypeStruct((half + 2, here, cells), bf16)] * count,
        in_specs=[in_smem()] + in_vmem(3),
        out_specs=in_vmem(count),
        compiler_params=params,
        cost_estimate=SMALL,
        name="early",
    )(z_arg, turned, low_rim, high_rim)

    def swap(arrays):
        taken = [arrays[0]]
        for p in reversed(range(1, count)):
            taken.append(lax.ppermute(arrays[p], "mode", [(i, i ^ p) for i in range(count)]))
        return taken

    entries, values, low_coef, high_coef, _ = lax.optimization_barrier(
        (tri_index, tri_value, low_rim, high_rim, early[0])
    )
    early = swap(early)
    dense, own = pl.pallas_call(
        functools.partial(dense_kernel, groups, fields, here),
        out_shape=[
            jax.ShapeDtypeStruct((groups, size, GROUP * size), bf16),
            jax.ShapeDtypeStruct((size, 128), jnp.float32),
        ],
        in_specs=[in_smem()] + in_vmem(2),
        out_specs=in_vmem(2),
        compiler_params=params,
        cost_estimate=SMALL,
        name="dense",
    )(z_arg, entries.T, values[None])
    weights, faces, inverse = pl.pallas_call(
        weight_kernel,
        out_shape=[
            jax.ShapeDtypeStruct((rows, 6, deep, cells), jnp.float32),
            jax.ShapeDtypeStruct((6, rows, cells), jnp.float32),
            jax.ShapeDtypeStruct((rows, cells), jnp.float32),
        ],
        in_specs=in_vmem(4),
        out_specs=in_vmem(3),
        scratch_shapes=[
            pltpu.VMEM((deep, rows, cells), jnp.float32),
            pltpu.VMEM((rows, deep, cells), jnp.float32),
        ],
        compiler_params=params,
        cost_estimate=SMALL,
        name="weights",
    )(mean_coef, kl_fields, low_coef, high_coef)
    late = pl.pallas_call(
        functools.partial(late_kernel, count, slab, half, rows),
        out_shape=[jax.ShapeDtypeStruct((slab - half, here, cells), bf16)] * count,
        in_specs=[in_smem()] + in_vmem(2),
        out_specs=in_vmem(count),
        compiler_params=params,
        cost_estimate=SMALL,
        name="late",
    )(z_arg, turned, own)
    late = swap(late)

    def mix(arrays, window, begin):
        flat = [a for group in arrays for a in group]
        return pl.pallas_call(
            functools.partial(mix_kernel, count, slab, half, groups, fields, window, begin),
            out_shape=[jax.ShapeDtypeStruct((half, here, cells), bf16)] * count,
            in_specs=[in_smem()] + in_vmem(len(flat) + 3),
            out_specs=in_vmem(count),
            scratch_shapes=[
                pltpu.VMEM((half + 2, size, cells), bf16),
                pltpu.VMEM((6, size, cells), bf16),
                pltpu.VMEM((GROUP * size, cells), bf16),
                pltpu.VMEM((size, cells), jnp.float32),
            ],
            compiler_params=params,
            name="mix",
        )(z_arg, *flat, dense, own, weights)

    window = tuple((0, k) for k in range(half + 2))
    back_early = swap(mix([early], window, 0))
    window = ((0, half), (0, half + 1)) + tuple((1, k) for k in range(slab - half))
    back_late = swap(mix([early, late], window, half))

    outer = jnp.stack([b[0] for b in back_early])
    place_of = lambda p: (count - p) % count
    bottom = lax.dynamic_index_in_dim(outer, place_of(z), 0, keepdims=False).astype(jnp.float32)
    top = lax.dynamic_index_in_dim(outer, place_of(z ^ (count - 1)), 0, keepdims=False)
    top = top.astype(jnp.float32)
    first_bottom = (source[:, 0] - bottom) * (inverse[0] / cheb_center)
    first_top = (source[:, -1] - top) * (inverse[-1] / cheb_center)
    low = lax.ppermute(first_top, "dom", upward)
    high = lax.ppermute(first_bottom, "dom", downward)

    sigma = cheb_center / cheb_radius
    rho_zero = 1.0 / sigma
    rho_one = 1.0 / (2.0 * sigma - rho_zero)
    image_spec = pl.BlockSpec((half, block, cells), lambda i: (0, i, 0))
    flat_spec = pl.BlockSpec((block, rows, cells), lambda i: (i, 0, 0))
    row_spec = pl.BlockSpec((block, cells), lambda i: (i, 0))
    updated, residual = pl.pallas_call(
        functools.partial(post_kernel, count, slab, half, rows, rho_zero, rho_one),
        grid=(here // block,),
        out_shape=[jax.ShapeDtypeStruct((here, rows, cells), jnp.float32)] * 2,
        in_specs=[in_smem()]
        + [image_spec] * (2 * count)
        + [flat_spec, flat_spec, row_spec, row_spec]
        + [
            pl.BlockSpec((6, rows, cells), lambda i: (0, 0, 0)),
            pl.BlockSpec((rows, cells), lambda i: (0, 0)),
        ],
        out_specs=[flat_spec, flat_spec],
        scratch_shapes=[pltpu.VMEM((rows, block, cells), jnp.float32)],
        compiler_params=params,
        name="post",
    )(
        z_arg,
        *back_early,
        *back_late,
        source,
        iterate,
        low,
        high,
        faces,
        inverse,
    )
    return updated, residual


def solution(mesh):
    return jax.shard_map(
        body,
        mesh=mesh,
        in_specs=(
            P("mode", "dom", None),
            P("mode", "dom", None),
            P("dom", None),
            P(None, "dom", None),
            P(),
            P(),
        ),
        out_specs=(P("mode", "dom", None), P("mode", "dom", None)),
        check_vma=False,
    )
```

```python
import functools
import jax
import jax.numpy as jnp
from jax import lax
from jax.experimental import pallas as pl
from jax.experimental.pallas import tpu as pltpu
from jax.sharding import PartitionSpec as P

NZ = 16
GROUP = 5

cheb_center = 1.125
cheb_radius = 0.875
SMALL = pl.CostEstimate(flops=1, bytes_accessed=1, transcendentals=0)
LARGE = pl.CostEstimate(flops=10**10, bytes_accessed=2**24, transcendentals=0)
VMEM_LIMIT = 48 * 1024 * 1024


def in_vmem(count):
    return [pl.BlockSpec(memory_space=pltpu.VMEM)] * count


def in_smem():
    return pl.BlockSpec(memory_space=pltpu.SMEM)


def row_of(place, rho, slab, count, rows):
    upward = slab * place + rho
    downward = slab * place + (slab - 1 - rho)
    row = jnp.where(place < count // 2, upward, downward)
    return jnp.clip(row, 0, rows - 1)


def turn_kernel(count, slab, rows, z_ref, x_ref, turned, *refs):
    outs, block_ref, sems = refs[:count], refs[count], refs[count + 1]
    z = z_ref[0]
    parts, modes = block_ref.shape[:2]
    copies = [
        pltpu.make_async_copy(
            x_ref.at[k * modes : (k + 1) * modes], block_ref.at[k], sems.at[k]
        )
        for k in range(parts)
    ]
    for copy in copies:
        copy.start()
    for k, copy in enumerate(copies):
        copy.wait()
        block = jnp.swapaxes(block_ref[k], 0, 1).astype(jnp.bfloat16)
        turned[:, k * modes : (k + 1) * modes, :] = block
    for p in range(count):
        place = jnp.bitwise_xor(z, p)
        for rho in range(outs[p].shape[0]):
            outs[p][rho] = turned[row_of(place, rho, slab, count, rows)]


def late_kernel(count, slab, rows, z_ref, turned, low_ref, high_ref, after, *outs):
    z = z_ref[0]
    here = turned.shape[1]
    for p in range(count):
        place = jnp.bitwise_xor(z, p)
        for k in range(1, outs[p].shape[0]):
            rho = slab - outs[p].shape[0] + 1 + k
            outs[p][k] = turned[row_of(place, rho, slab, count, rows)]
        outs[p][0] = turned[row_of(place, -1, slab, count, rows)]

        @pl.when(place == 0)
        def _():
            outs[p][0] = low_ref[:here].astype(jnp.bfloat16)

        @pl.when(place == count - 1)
        def _():
            outs[p][0] = high_ref[:here].astype(jnp.bfloat16)


def masks(cells):
    lane = lax.broadcasted_iota(jnp.int32, (1, cells), 1)
    in_z = lane % NZ
    one = jnp.float32(1.0)
    zero = jnp.float32(0.0)
    return (
        jnp.where(lane < cells - NZ, one, zero),
        jnp.where(lane >= NZ, one, zero),
        jnp.where(in_z < NZ - 1, one, zero),
        jnp.where(in_z > 0, one, zero),
    )


def beside(field, mask_set):
    cells = field.shape[-1]
    axis = field.ndim - 1
    return (
        pltpu.roll(field, cells - NZ, axis) * mask_set[0],
        pltpu.roll(field, NZ, axis) * mask_set[1],
        pltpu.roll(field, cells - 1, axis) * mask_set[2],
        pltpu.roll(field, 1, axis) * mask_set[3],
    )


def dense_kernel(groups, fields, modes_here, z_ref, entry_ref, value_ref, dense_ref, own_ref):
    size = dense_ref.shape[1]
    entries = entry_ref.shape[1]
    flip = z_ref[0] * modes_here
    mode_id = jnp.bitwise_xor(lax.broadcasted_iota(jnp.int32, (size, entries), 0), flip)
    pick = jnp.where(mode_id == entry_ref[0:1], 1.0, 0.0).astype(jnp.bfloat16)
    depth = -(-fields // 16) * 16
    here = lax.broadcasted_iota(jnp.int32, (depth, entries), 0) == entry_ref[2:3]
    partner = jnp.where(here, entry_ref[1:2].astype(jnp.float32), 0.0).astype(jnp.bfloat16)
    value = jnp.where(here, value_ref[...], 0.0).astype(jnp.bfloat16)
    dims = (((1,), (1,)), ((), ()))
    partner_of = lax.dot_general(pick, partner, dims, preferred_element_type=jnp.float32)
    value_of = lax.dot_general(pick, value, dims, preferred_element_type=jnp.float32)
    column = jnp.bitwise_xor(lax.broadcasted_iota(jnp.int32, (size, size), 1), flip)
    column = column.astype(jnp.float32)
    own_ref[...] = jnp.broadcast_to(value_of[:, 0:1], own_ref.shape)
    for g in range(groups):
        for k in range(GROUP):
            at = 1 + g * GROUP + k
            if at >= fields:
                tile = jnp.zeros((size, size), jnp.float32)
            else:
                tile = jnp.where(
                    column == partner_of[:, at : at + 1], value_of[:, at : at + 1], 0.0
                )
            dense_ref[g, :, k * size : (k + 1) * size] = tile.astype(jnp.bfloat16)


def weight_kernel(
    mean_ref, fields_ref, low_ref, high_ref, weight_ref, faces_ref, inverse_ref, stack_ref, turned
):
    fields, rows, cells = fields_ref.shape
    deep = stack_ref.shape[0]
    mask_set = masks(cells)
    start = low_ref.shape[0] - deep
    stack_ref[0] = mean_ref[...]
    stack_ref[1 : fields + 1] = fields_ref[...]
    stack_ref[fields + 1 :] = jnp.zeros((deep - fields - 1, rows, cells), jnp.float32)
    turned[...] = jnp.swapaxes(stack_ref[...], 0, 1)
    for row in range(rows):
        centre = turned[row]
        up = high_ref[start:, :] if row == rows - 1 else turned[row + 1]
        down = low_ref[start:, :] if row == 0 else turned[row - 1]
        for f, other in enumerate((up, down) + beside(centre, mask_set)):
            weight_ref[row, f] = 0.5 * (centre + other)
    place = lax.broadcasted_iota(jnp.int32, (rows, cells), 0)
    centre = mean_ref[...]
    high, low = high_ref[start : start + 1, :], low_ref[start : start + 1, :]
    up = jnp.where(place == rows - 1, high, pltpu.roll(centre, rows - 1, 0))
    down = jnp.where(place == 0, low, pltpu.roll(centre, 1, 0))
    diag = None
    for f, other in enumerate((up, down) + beside(centre, mask_set)):
        weight = 0.5 * (centre + other)
        diag = weight if diag is None else diag + weight
        faces_ref[f] = weight if f < 2 else weight * mask_set[f - 2]
    inverse_ref[...] = 1.0 / diag


def mix_kernel(count, slab, groups, fields, window, skip, begin, extra, z_ref, *refs):
    arrays = max(a for a, _ in window) + 1
    sources = refs[: arrays * count]
    dense_ref, own_ref, weight_ref = refs[arrays * count : arrays * count + 3]
    outs = refs[arrays * count + 3 + extra : -4]
    rows_ref, diff_ref, term_ref, total_ref = refs[-4:]
    size, cells = total_ref.shape
    here = size // count
    bf16 = jnp.bfloat16
    for k, (array, row) in enumerate(window):
        for p in range(count):
            part = sources[array * count + (count - p) % count]
            rows_ref[k, p * here : (p + 1) * here, :] = part[row]
    mask_set = masks(cells)
    z = z_ref[0]
    rows = weight_ref.shape[0]
    ahead = jnp.where(z < count // 2, 0, 1)
    faces = (ahead, 1 - ahead, 2, 3, 4, 5)

    def each_row(r, carry):
        row = row_of(z, jnp.where(r == 0, begin[0], begin[1] + r), slab, count, rows)
        r_in = r + jnp.where(r == 0, 0, skip)
        mean_weights = [weight_ref[row, f, 0:1, :] for f in faces]
        for t in range(0, size, 16):
            at = slice(t, t + 16)
            centre = rows_ref[r_in + 1, at].astype(jnp.float32)
            others = (
                rows_ref[r_in + 2, at].astype(jnp.float32),
                rows_ref[r_in, at].astype(jnp.float32),
            )
            mean = None
            for f, other in enumerate(others + beside(centre, mask_set)):
                diff = centre - other
                diff_ref[f, at] = diff.astype(bf16)
                part = mean_weights[f] * diff
                mean = part if mean is None else mean + part
            total_ref[at, :] = jnp.concatenate([own_ref[at]] * (cells // 128), 1) * mean
        for g in range(groups):
            for k in range(GROUP):
                field = min(1 + g * GROUP + k, fields - 1)
                weights = [
                    jnp.broadcast_to(weight_ref[row, f, field : field + 1, :], (16, cells))
                    for f in faces
                ]
                weights = [w.astype(bf16) for w in weights]
                for t in range(0, size, 16):
                    part = [weights[f] * diff_ref[f, t : t + 16] for f in range(6)]
                    term = ((part[0] + part[1]) + (part[2] + part[3])) + (part[4] + part[5])
                    term_ref[k * size + t : k * size + t + 16, :] = term
            total_ref[...] += jnp.dot(
                dense_ref[g], term_ref[...], preferred_element_type=jnp.float32
            )
        for p in range(count):
            outs[p][r] = total_ref[p * here : (p + 1) * here, :].astype(bf16)
        return carry

    lax.fori_loop(0, outs[0].shape[0], each_row, 0)


def edge_kernel(count, z_ref, *refs):
    parts = refs[:count]
    bottom_source, top_source, inverse = refs[count : count + 3]
    bottom, top = refs[-2:]
    z = z_ref[0]
    rows = inverse.shape[0]
    for k in range(count):
        place = jnp.bitwise_xor(z, (count - k) % count)
        image = parts[k][0].astype(jnp.float32)

        @pl.when(place == 0)
        def _():
            scale = inverse[0:1] * (1.0 / cheb_center)
            bottom[...] = (bottom_source[...] - image) * scale

        @pl.when(place == count - 1)
        def _():
            scale = inverse[rows - 1 : rows] * (1.0 / cheb_center)
            top[...] = (top_source[...] - image) * scale


def post_kernel(count, slab, half, rows, rho_zero, rho_one, z_ref, *refs):
    early = refs[:count]
    late = refs[count : 2 * count]
    source, iterate, faces, inverse = refs[2 * count : 2 * count + 4]
    updated, residual, image = refs[2 * count + 4 :]
    z = z_ref[0]
    modes, _, cells = source.shape
    for k in range(count):
        place = jnp.bitwise_xor(z, (count - k) % count)
        for rho in range(slab):
            if 1 <= rho <= half:
                part = early[k][rho - 1]
            else:
                part = late[k][max(rho - half, 0)]
            image[row_of(place, rho, slab, count, rows)] = part.astype(jnp.float32)
    residual[...] = source[...] - jnp.swapaxes(image[...], 0, 1)
    place = lax.broadcasted_iota(jnp.int32, (rows, cells), 0)
    inv = inverse[...]
    up_face = jnp.where(place == rows - 1, 0.0, faces[0])
    down_face = jnp.where(place == 0, 0.0, faces[1])
    for m in range(modes):
        res = residual[m]
        first = res * (inv * (1.0 / cheb_center))
        near = up_face * pltpu.roll(first, rows - 1, 0) + down_face * pltpu.roll(first, 1, 0)
        near = near + faces[2] * pltpu.roll(first, cells - NZ, 1)
        near = near + faces[3] * pltpu.roll(first, NZ, 1)
        near = near + faces[4] * pltpu.roll(first, cells - 1, 1)
        near = near + faces[5] * pltpu.roll(first, 1, 1)
        smoothed = (1.0 - 1.0 / cheb_center) * res + near
        step = (1.0 + rho_one * rho_zero) * first + (2.0 * rho_one / cheb_radius) * smoothed * inv
        updated[m] = iterate[m] + step


def close_kernel(rho_one, low, high, faces, inverse, partial, updated):
    modes, deep, cells = partial.shape
    bottom = pl.program_id(0) == 0
    rows = inverse.shape[0]
    scale = 2.0 * rho_one / cheb_radius
    weight = jnp.where(
        bottom, faces[1, 0:1] * inverse[0:1], faces[0, rows - 1 : rows] * inverse[rows - 1 : rows]
    )
    share = jnp.where(bottom, low[...], high[...]) * (weight * scale)
    place = lax.broadcasted_iota(jnp.int32, (deep, cells), 0)
    here = place == jnp.where(bottom, 0, deep - 1)
    for m in range(modes):
        updated[m] = partial[m] + jnp.where(here, share[m : m + 1], 0.0)


def body(iterate, source, mean_coef, kl_fields, tri_index, tri_value):
    count = lax.axis_size("mode")
    doms = lax.axis_size("dom")
    z = lax.axis_index("mode")
    z_arg = z.astype(jnp.int32).reshape(1)
    here, rows, cells = iterate.shape
    size = here * count
    slab = rows // count
    half = slab // 2
    fields = kl_fields.shape[0] + 1
    groups = -(-(fields - 1) // GROUP)
    bf16 = jnp.bfloat16
    params = pltpu.CompilerParams(vmem_limit_bytes=VMEM_LIMIT)

    deep = -(-fields // 8) * 8

    parts = max(1, here // 16)
    turned, *early = pl.pallas_call(
        functools.partial(turn_kernel, count, slab, rows),
        out_shape=[jax.ShapeDtypeStruct((rows, here, cells), bf16)]
        + [jax.ShapeDtypeStruct((half + 2, here, cells), bf16)] * count,
        in_specs=[in_smem(), pl.BlockSpec(memory_space=pltpu.HBM)],
        out_specs=in_vmem(count + 1),
        scratch_shapes=[
            pltpu.VMEM((parts, here // parts, rows, cells), jnp.float32),
            pltpu.SemaphoreType.DMA((parts,)),
        ],
        compiler_params=params,
        cost_estimate=SMALL,
        name="turn",
    )(z_arg, iterate)

    def swap(arrays):
        taken = [arrays[0]]
        for p in reversed(range(1, count)):
            taken.append(lax.ppermute(arrays[p], "mode", [(i, i ^ p) for i in range(count)]))
        return taken

    early = swap(early)
    entries, values, _ = lax.optimization_barrier((tri_index, tri_value, turned))
    dense, own = pl.pallas_call(
        functools.partial(dense_kernel, groups, fields, here),
        out_shape=[
            jax.ShapeDtypeStruct((groups, size, GROUP * size), bf16),
            jax.ShapeDtypeStruct((size, 128), jnp.float32),
        ],
        in_specs=[in_smem()] + in_vmem(2),
        out_specs=in_vmem(2),
        compiler_params=params,
        cost_estimate=SMALL,
        name="dense",
    )(z_arg, entries.T, values[None])
    upward = [(i, i + 1) for i in range(doms - 1)]
    downward = [(b, a) for a, b in upward]
    iterate_here, mean_here, fields_here, _ = lax.optimization_barrier(
        (iterate, mean_coef, kl_fields, own)
    )
    filler = jnp.zeros((deep - fields, cells), jnp.float32)
    low_rim, high_rim = (
        lax.ppermute(
            jnp.concatenate(
                [iterate_here[:, at], mean_here[at][None], fields_here[:, at], filler], 0
            ),
            "dom",
            pairs,
        )
        for at, pairs in ((rows - 1, upward), (0, downward))
    )
    weights, faces, inverse = pl.pallas_call(
        weight_kernel,
        out_shape=[
            jax.ShapeDtypeStruct((rows, 6, deep, cells), jnp.float32),
            jax.ShapeDtypeStruct((6, rows, cells), jnp.float32),
            jax.ShapeDtypeStruct((rows, cells), jnp.float32),
        ],
        in_specs=in_vmem(4),
        out_specs=in_vmem(3),
        scratch_shapes=[
            pltpu.VMEM((deep, rows, cells), jnp.float32),
            pltpu.VMEM((rows, deep, cells), jnp.float32),
        ],
        compiler_params=params,
        cost_estimate=SMALL,
        name="weights",
    )(mean_coef, kl_fields, low_rim, high_rim)
    late = pl.pallas_call(
        functools.partial(late_kernel, count, slab, rows),
        out_shape=[jax.ShapeDtypeStruct((slab - half, here, cells), bf16)] * count,
        in_specs=[in_smem()] + in_vmem(3) + [pl.BlockSpec(memory_space=pl.ANY)],
        out_specs=in_vmem(count),
        compiler_params=params,
        cost_estimate=SMALL,
        name="late",
    )(z_arg, turned, low_rim, high_rim, early[-2])
    late = swap(late)

    def mix(arrays, window, skip, begin, rows_out, after=()):
        flat = [a for group in arrays for a in group]
        return pl.pallas_call(
            functools.partial(
                mix_kernel, count, slab, groups, fields, window, skip, begin, len(after)
            ),
            out_shape=[jax.ShapeDtypeStruct((rows_out, here, cells), bf16)] * count,
            in_specs=[in_smem()]
            + in_vmem(len(flat) + 3)
            + [pl.BlockSpec(memory_space=pl.ANY)] * len(after),
            out_specs=in_vmem(count),
            scratch_shapes=[
                pltpu.VMEM((len(window), size, cells), bf16),
                pltpu.VMEM((6, size, cells), bf16),
                pltpu.VMEM((GROUP * size, cells), bf16),
                pltpu.VMEM((size, cells), jnp.float32),
            ],
            compiler_params=params,
            cost_estimate=LARGE,
            name="mix",
        )(z_arg, *flat, dense, own, weights, *after)

    window = tuple((0, k) for k in range(half + 2))
    mixed = mix([early], window, 0, (1, 1), half)
    back_early = swap(mixed)
    window = ((1, 0), (0, 0), (0, 1), (0, half), (0, half + 1))
    window += tuple((1, k) for k in range(1, slab - half))
    back_late = swap(mix([early, late], window, 2, (0, half), slab - half, mixed[-1:]))

    bottom, top = pl.pallas_call(
        functools.partial(edge_kernel, count),
        out_shape=[jax.ShapeDtypeStruct((here, cells), jnp.float32)] * 2,
        in_specs=[in_smem()]
        + in_vmem(count + 3)
        + [pl.BlockSpec(memory_space=pl.ANY)] * (count - 1),
        out_specs=in_vmem(2),
        compiler_params=params,
        cost_estimate=SMALL,
        name="edge",
    )(z_arg, *back_late, source[:, 0], source[:, rows - 1], inverse, *back_early[1:])
    low = lax.ppermute(top, "dom", upward)
    high = lax.ppermute(bottom, "dom", downward)

    sigma = cheb_center / cheb_radius
    rho_zero = 1.0 / sigma
    rho_one = 1.0 / (2.0 * sigma - rho_zero)
    block = min(16, here)
    early_spec = pl.BlockSpec((half, block, cells), lambda i: (0, i, 0))
    late_spec = pl.BlockSpec((slab - half, block, cells), lambda i: (0, i, 0))
    flat_spec = pl.BlockSpec((block, rows, cells), lambda i: (i, 0, 0))
    updated, residual = pl.pallas_call(
        functools.partial(post_kernel, count, slab, half, rows, rho_zero, rho_one),
        grid=(here // block,),
        out_shape=[jax.ShapeDtypeStruct((here, rows, cells), jnp.float32)] * 2,
        in_specs=[in_smem()]
        + [early_spec] * count
        + [late_spec] * count
        + [flat_spec, flat_spec]
        + [
            pl.BlockSpec((6, rows, cells), lambda i: (0, 0, 0)),
            pl.BlockSpec((rows, cells), lambda i: (0, 0)),
        ],
        out_specs=[flat_spec, flat_spec],
        scratch_shapes=[pltpu.VMEM((rows, block, cells), jnp.float32)],
        compiler_params=params,
        name="post",
    )(
        z_arg,
        *back_early,
        *back_late,
        source,
        iterate,
        faces,
        inverse,
    )
    tile = 8 if rows % 8 == 0 else rows
    last = rows // tile - 1
    tile_spec = pl.BlockSpec((here, tile, cells), lambda i: (0, i * last, 0))
    updated = pl.pallas_call(
        functools.partial(close_kernel, rho_one),
        grid=(2 if last else 1,),
        out_shape=jax.ShapeDtypeStruct((here, rows, cells), jnp.float32),
        in_specs=[
            pl.BlockSpec((here, cells), lambda i: (0, 0)),
            pl.BlockSpec((here, cells), lambda i: (0, 0)),
            pl.BlockSpec((6, rows, cells), lambda i: (0, 0, 0)),
            pl.BlockSpec((rows, cells), lambda i: (0, 0)),
            tile_spec,
        ],
        out_specs=tile_spec,
        input_output_aliases={4: 0},
        compiler_params=params,
        name="close",
    )(low, high, faces, inverse, updated)
    return updated, residual


def solution(mesh):
    return jax.shard_map(
        body,
        mesh=mesh,
        in_specs=(
            P("mode", "dom", None),
            P("mode", "dom", None),
            P("dom", None),
            P(None, "dom", None),
            P(),
            P(),
        ),
        out_specs=(P("mode", "dom", None), P("mode", "dom", None)),
        check_vma=False,
    )
```

```python
import functools
import jax
import jax.numpy as jnp
from jax import lax
from jax.experimental import pallas as pl
from jax.experimental.pallas import tpu as pltpu
from jax.sharding import PartitionSpec as P

NZ = 16
GROUP = 5

cheb_center = 1.125
cheb_radius = 0.875
SMALL = pl.CostEstimate(flops=1, bytes_accessed=1, transcendentals=0)
LARGE = pl.CostEstimate(flops=10**10, bytes_accessed=2**24, transcendentals=0)
VMEM_LIMIT = 16 * 1024 * 1024
VMEM_MOST = 115 * 512 * 1024


def in_vmem(count):
    return [pl.BlockSpec(memory_space=pltpu.VMEM)] * count


def in_smem():
    return pl.BlockSpec(memory_space=pltpu.SMEM)


def row_of(place, rho, slab, count, rows):
    upward = slab * place + rho
    downward = slab * place + (slab - 1 - rho)
    row = jnp.where(place < count // 2, upward, downward)
    return jnp.clip(row, 0, rows - 1)


def turn_kernel(count, slab, rows, z_ref, x_ref, turned, *refs):
    outs, block_ref, sems = refs[:count], refs[count], refs[count + 1]
    z = z_ref[0]
    parts, modes = block_ref.shape[:2]
    copies = [
        pltpu.make_async_copy(
            x_ref.at[k * modes : (k + 1) * modes], block_ref.at[k], sems.at[k]
        )
        for k in range(parts)
    ]
    for copy in copies:
        copy.start()
    for k, copy in enumerate(copies):
        copy.wait()
        block = jnp.swapaxes(block_ref[k], 0, 1).astype(jnp.bfloat16)
        turned[:, k * modes : (k + 1) * modes, :] = block
    for p in range(count):
        place = jnp.bitwise_xor(z, p)
        for rho in range(outs[p].shape[0]):
            outs[p][rho] = turned[row_of(place, rho, slab, count, rows)]


def rim_kernel(turned, mean_ref, fields_ref, after, last, first):
    rows, here, cells = turned.shape
    fields = fields_ref.shape[0]
    for out, row in ((first, 0), (last, rows - 1)):
        out[:here] = turned[row].astype(jnp.float32)
        out[here : here + 1, :] = mean_ref[row : row + 1, :]
        for field in range(fields):
            out[here + 1 + field : here + 2 + field, :] = fields_ref[field, row : row + 1, :]
        rest = out.shape[0] - here - 1 - fields
        out[here + 1 + fields :, :] = jnp.zeros((rest, cells), jnp.float32)


def late_kernel(count, slab, rows, z_ref, turned, low_ref, high_ref, after, *outs):
    z = z_ref[0]
    here = turned.shape[1]
    for p in range(count):
        place = jnp.bitwise_xor(z, p)
        for k in range(1, outs[p].shape[0]):
            rho = slab - outs[p].shape[0] + 1 + k
            outs[p][k] = turned[row_of(place, rho, slab, count, rows)]
        outs[p][0] = turned[row_of(place, -1, slab, count, rows)]

        @pl.when(place == 0)
        def _():
            outs[p][0] = low_ref[:here].astype(jnp.bfloat16)

        @pl.when(place == count - 1)
        def _():
            outs[p][0] = high_ref[:here].astype(jnp.bfloat16)


def masks(cells):
    lane = lax.broadcasted_iota(jnp.int32, (1, cells), 1)
    in_z = lane % NZ
    one = jnp.float32(1.0)
    zero = jnp.float32(0.0)
    return (
        jnp.where(lane < cells - NZ, one, zero),
        jnp.where(lane >= NZ, one, zero),
        jnp.where(in_z < NZ - 1, one, zero),
        jnp.where(in_z > 0, one, zero),
    )


def beside(field, mask_set):
    cells = field.shape[-1]
    axis = field.ndim - 1
    return (
        pltpu.roll(field, cells - NZ, axis) * mask_set[0],
        pltpu.roll(field, NZ, axis) * mask_set[1],
        pltpu.roll(field, cells - 1, axis) * mask_set[2],
        pltpu.roll(field, 1, axis) * mask_set[3],
    )


def dense_kernel(groups, fields, modes_here, z_ref, entry_ref, value_ref, dense_ref, own_ref):
    size = dense_ref.shape[1]
    entries = entry_ref.shape[1]
    flip = z_ref[0] * modes_here
    mode_id = jnp.bitwise_xor(lax.broadcasted_iota(jnp.int32, (size, entries), 0), flip)
    pick = jnp.where(mode_id == entry_ref[0:1], 1.0, 0.0).astype(jnp.bfloat16)
    depth = -(-fields // 16) * 16
    here = lax.broadcasted_iota(jnp.int32, (depth, entries), 0) == entry_ref[2:3]
    partner = jnp.where(here, entry_ref[1:2].astype(jnp.float32), 0.0).astype(jnp.bfloat16)
    value = jnp.where(here, value_ref[...], 0.0).astype(jnp.bfloat16)
    dims = (((1,), (1,)), ((), ()))
    partner_of = lax.dot_general(pick, partner, dims, preferred_element_type=jnp.float32)
    value_of = lax.dot_general(pick, value, dims, preferred_element_type=jnp.float32)
    column = jnp.bitwise_xor(lax.broadcasted_iota(jnp.int32, (size, size), 1), flip)
    column = column.astype(jnp.float32)
    own_ref[...] = jnp.broadcast_to(value_of[:, 0:1], own_ref.shape)
    for g in range(groups):
        for k in range(GROUP):
            at = 1 + g * GROUP + k
            if at >= fields:
                tile = jnp.zeros((size, size), jnp.float32)
            else:
                tile = jnp.where(
                    column == partner_of[:, at : at + 1], value_of[:, at : at + 1], 0.0
                )
            dense_ref[g, :, k * size : (k + 1) * size] = tile.astype(jnp.bfloat16)


def weight_kernel(
    count,
    z_ref,
    mean_ref,
    fields_ref,
    low_ref,
    high_ref,
    weight_ref,
    faces_ref,
    inverse_ref,
    stack_ref,
    turned,
):
    fields, rows, cells = fields_ref.shape
    deep = stack_ref.shape[0]
    mask_set = masks(cells)
    start = low_ref.shape[0] - deep
    stack_ref[0] = mean_ref[...]
    stack_ref[1 : fields + 1] = fields_ref[...]
    stack_ref[fields + 1 :] = jnp.zeros((deep - fields - 1, rows, cells), jnp.float32)
    turned[1 : rows + 1] = jnp.swapaxes(stack_ref[...], 0, 1)
    turned[0] = low_ref[start:, :]
    turned[rows + 1] = high_ref[start:, :]
    z = z_ref[0]
    slab = weight_ref.shape[0]
    ahead = jnp.where(z < count // 2, 1, -1)
    for rho in range(slab):
        row = 1 + row_of(z, rho, slab, count, rows)
        centre = turned[row]
        others = (turned[row + ahead], turned[row - ahead]) + beside(centre, mask_set)
        for f, other in enumerate(others):
            weight_ref[rho, f] = 0.5 * (centre + other)
    place = lax.broadcasted_iota(jnp.int32, (rows, cells), 0)
    centre = mean_ref[...]
    high, low = high_ref[start : start + 1, :], low_ref[start : start + 1, :]
    up = jnp.where(place == rows - 1, high, pltpu.roll(centre, rows - 1, 0))
    down = jnp.where(place == 0, low, pltpu.roll(centre, 1, 0))
    diag = None
    for f, other in enumerate((up, down) + beside(centre, mask_set)):
        weight = 0.5 * (centre + other)
        diag = weight if diag is None else diag + weight
        faces_ref[f] = weight if f < 2 else weight * mask_set[f - 2]
    inverse_ref[...] = 1.0 / diag


def mix_kernel(count, groups, fields, window, skip, begin, extra, *refs):
    arrays = max(a for a, _ in window) + 1
    sources = refs[: arrays * count]
    dense_ref, own_ref, weight_ref = refs[arrays * count : arrays * count + 3]
    outs = refs[arrays * count + 3 + extra : -4]
    rows_ref, diff_ref, term_ref, total_ref = refs[-4:]
    size, cells = total_ref.shape
    here = size // count
    bf16 = jnp.bfloat16
    for k, (array, row) in enumerate(window):
        for p in range(count):
            part = sources[array * count + (count - p) % count]
            rows_ref[k, p * here : (p + 1) * here, :] = part[row]
    mask_set = masks(cells)
    def each_row(r, carry):
        row = jnp.where(r == 0, begin[0], begin[1] + r)
        r_in = r + jnp.where(r == 0, 0, skip)
        mean_weights = [weight_ref[row, f, 0:1, :] for f in range(6)]
        for t in range(0, size, 16):
            at = slice(t, t + 16)
            centre = rows_ref[r_in + 1, at].astype(jnp.float32)
            others = (
                rows_ref[r_in + 2, at].astype(jnp.float32),
                rows_ref[r_in, at].astype(jnp.float32),
            )
            mean = None
            for f, other in enumerate(others + beside(centre, mask_set)):
                diff = centre - other
                diff_ref[f, at] = diff.astype(bf16)
                part = mean_weights[f] * diff
                mean = part if mean is None else mean + part
            total_ref[at, :] = jnp.concatenate([own_ref[at]] * (cells // 128), 1) * mean
        for g in range(groups):
            for k in range(GROUP):
                field = min(1 + g * GROUP + k, fields - 1)
                weights = [
                    jnp.broadcast_to(weight_ref[row, f, field : field + 1, :], (16, cells))
                    for f in range(6)
                ]
                weights = [w.astype(bf16) for w in weights]
                for t in range(0, size, 16):
                    part = [weights[f] * diff_ref[f, t : t + 16] for f in range(6)]
                    term = ((part[0] + part[1]) + (part[2] + part[3])) + (part[4] + part[5])
                    term_ref[k * size + t : k * size + t + 16, :] = term
            total_ref[...] += jnp.dot(
                dense_ref[g], term_ref[...], preferred_element_type=jnp.float32
            )
        for p in range(count):
            outs[p][r] = total_ref[p * here : (p + 1) * here, :].astype(bf16)
        return carry

    lax.fori_loop(0, outs[0].shape[0], each_row, 0)


def edge_kernel(count, z_ref, *refs):
    parts = refs[:count]
    bottom_source, top_source, inverse = refs[count : count + 3]
    bottom, top = refs[-2:]
    z = z_ref[0]
    rows = inverse.shape[0]
    for k in range(count):
        place = jnp.bitwise_xor(z, (count - k) % count)
        image = parts[k][0].astype(jnp.float32)

        @pl.when(place == 0)
        def _():
            scale = inverse[0:1] * (1.0 / cheb_center)
            bottom[...] = (bottom_source[...] - image) * scale

        @pl.when(place == count - 1)
        def _():
            scale = inverse[rows - 1 : rows] * (1.0 / cheb_center)
            top[...] = (top_source[...] - image) * scale


def post_kernel(count, slab, half, rows, rho_zero, rho_one, z_ref, *refs):
    early = refs[:count]
    late = refs[count : 2 * count]
    source, iterate, faces, inverse = refs[2 * count : 2 * count + 4]
    updated, residual, image = refs[2 * count + 4 :]
    z = z_ref[0]
    modes, _, cells = source.shape
    for k in range(count):
        place = jnp.bitwise_xor(z, (count - k) % count)
        for rho in range(slab):
            if 1 <= rho <= half:
                part = early[k][rho - 1]
            else:
                part = late[k][max(rho - half, 0)]
            image[row_of(place, rho, slab, count, rows)] = part.astype(jnp.float32)
    residual[...] = source[...] - jnp.swapaxes(image[...], 0, 1)
    place = lax.broadcasted_iota(jnp.int32, (rows, cells), 0)
    inv = inverse[...]
    up_face = jnp.where(place == rows - 1, 0.0, faces[0])
    down_face = jnp.where(place == 0, 0.0, faces[1])
    for m in range(modes):
        res = residual[m]
        first = res * (inv * (1.0 / cheb_center))
        near = up_face * pltpu.roll(first, rows - 1, 0) + down_face * pltpu.roll(first, 1, 0)
        near = near + faces[2] * pltpu.roll(first, cells - NZ, 1)
        near = near + faces[3] * pltpu.roll(first, NZ, 1)
        near = near + faces[4] * pltpu.roll(first, cells - 1, 1)
        near = near + faces[5] * pltpu.roll(first, 1, 1)
        smoothed = (1.0 - 1.0 / cheb_center) * res + near
        step = (1.0 + rho_one * rho_zero) * first + (2.0 * rho_one / cheb_radius) * smoothed * inv
        updated[m] = iterate[m] + step


def close_kernel(rho_one, low, high, faces, inverse, partial, updated):
    modes, deep, cells = partial.shape
    bottom = pl.program_id(0) == 0
    rows = inverse.shape[0]
    scale = 2.0 * rho_one / cheb_radius
    weight = jnp.where(
        bottom, faces[1, 0:1] * inverse[0:1], faces[0, rows - 1 : rows] * inverse[rows - 1 : rows]
    )
    share = jnp.where(bottom, low[...], high[...]) * (weight * scale)
    place = lax.broadcasted_iota(jnp.int32, (deep, cells), 0)
    here = place == jnp.where(bottom, 0, deep - 1)
    for m in range(modes):
        updated[m] = partial[m] + jnp.where(here, share[m : m + 1], 0.0)


def body(iterate, source, mean_coef, kl_fields, tri_index, tri_value):
    count = lax.axis_size("mode")
    doms = lax.axis_size("dom")
    z = lax.axis_index("mode")
    z_arg = z.astype(jnp.int32).reshape(1)
    here, rows, cells = iterate.shape
    size = here * count
    slab = rows // count
    half = slab // 2
    fields = kl_fields.shape[0] + 1
    groups = -(-(fields - 1) // GROUP)
    bf16 = jnp.bfloat16
    params = pltpu.CompilerParams(vmem_limit_bytes=VMEM_LIMIT)

    deep = -(-fields // 8) * 8

    parts = max(1, here // 16)
    turned, *early = pl.pallas_call(
        functools.partial(turn_kernel, count, slab, rows),
        out_shape=[jax.ShapeDtypeStruct((rows, here, cells), bf16)]
        + [jax.ShapeDtypeStruct((half + 2, here, cells), bf16)] * count,
        in_specs=[in_smem(), pl.BlockSpec(memory_space=pltpu.HBM)],
        out_specs=in_vmem(count + 1),
        scratch_shapes=[
            pltpu.VMEM((parts, here // parts, rows, cells), jnp.float32),
            pltpu.SemaphoreType.DMA((parts,)),
        ],
        compiler_params=pltpu.CompilerParams(vmem_limit_bytes=VMEM_MOST),
        cost_estimate=SMALL,
        name="turn",
    )(z_arg, iterate)

    def swap(arrays):
        taken = [arrays[0]]
        for p in reversed(range(1, count)):
            taken.append(lax.ppermute(arrays[p], "mode", [(i, i ^ p) for i in range(count)]))
        return taken

    early = swap(early)
    entries, values, _ = lax.optimization_barrier((tri_index, tri_value, turned))
    dense, own = pl.pallas_call(
        functools.partial(dense_kernel, groups, fields, here),
        out_shape=[
            jax.ShapeDtypeStruct((groups, size, GROUP * size), bf16),
            jax.ShapeDtypeStruct((size, 128), jnp.float32),
        ],
        in_specs=[in_smem()] + in_vmem(2),
        out_specs=in_vmem(2),
        compiler_params=params,
        cost_estimate=SMALL,
        name="dense",
    )(z_arg, entries.T, values[None])
    upward = [(i, i + 1) for i in range(doms - 1)]
    downward = [(b, a) for a, b in upward]
    last_rim, first_rim = pl.pallas_call(
        rim_kernel,
        out_shape=[jax.ShapeDtypeStruct((here + deep, cells), jnp.float32)] * 2,
        in_specs=in_vmem(3) + [pl.BlockSpec(memory_space=pl.ANY)],
        out_specs=in_vmem(2),
        compiler_params=params,
        cost_estimate=SMALL,
        name="rim",
    )(turned, mean_coef, kl_fields, own)
    low_rim = lax.ppermute(last_rim, "dom", upward)
    high_rim = lax.ppermute(first_rim, "dom", downward)
    weights, faces, inverse = pl.pallas_call(
        functools.partial(weight_kernel, count),
        out_shape=[
            jax.ShapeDtypeStruct((slab, 6, deep, cells), jnp.float32),
            jax.ShapeDtypeStruct((6, rows, cells), jnp.float32),
            jax.ShapeDtypeStruct((rows, cells), jnp.float32),
        ],
        in_specs=[in_smem()] + in_vmem(4),
        out_specs=in_vmem(3),
        scratch_shapes=[
            pltpu.VMEM((deep, rows, cells), jnp.float32),
            pltpu.VMEM((rows + 2, deep, cells), jnp.float32),
        ],
        compiler_params=params,
        cost_estimate=SMALL,
        name="weights",
    )(z_arg, mean_coef, kl_fields, low_rim, high_rim)
    late = pl.pallas_call(
        functools.partial(late_kernel, count, slab, rows),
        out_shape=[jax.ShapeDtypeStruct((slab - half, here, cells), bf16)] * count,
        in_specs=[in_smem()] + in_vmem(3) + [pl.BlockSpec(memory_space=pl.ANY)],
        out_specs=in_vmem(count),
        compiler_params=params,
        cost_estimate=SMALL,
        name="late",
    )(z_arg, turned, low_rim, high_rim, early[-2])
    late = swap(late)

    def mix(arrays, window, skip, begin, rows_out, after=()):
        flat = [a for group in arrays for a in group]
        return pl.pallas_call(
            functools.partial(
                mix_kernel, count, groups, fields, window, skip, begin, len(after)
            ),
            out_shape=[jax.ShapeDtypeStruct((rows_out, here, cells), bf16)] * count,
            in_specs=in_vmem(len(flat) + 3)
            + [pl.BlockSpec(memory_space=pl.ANY)] * len(after),
            out_specs=in_vmem(count),
            scratch_shapes=[
                pltpu.VMEM((len(window), size, cells), bf16),
                pltpu.VMEM((6, size, cells), bf16),
                pltpu.VMEM((GROUP * size, cells), bf16),
                pltpu.VMEM((size, cells), jnp.float32),
            ],
            compiler_params=params,
            cost_estimate=LARGE,
            name="mix",
        )(*flat, dense, own, weights, *after)

    window = tuple((0, k) for k in range(half + 2))
    mixed = mix([early], window, 0, (1, 1), half)
    back_early = swap(mixed)
    window = ((1, 0), (0, 0), (0, 1), (0, half), (0, half + 1))
    window += tuple((1, k) for k in range(1, slab - half))
    back_late = swap(mix([early, late], window, 2, (0, half), slab - half, mixed[-1:]))

    bottom, top = pl.pallas_call(
        functools.partial(edge_kernel, count),
        out_shape=[jax.ShapeDtypeStruct((here, cells), jnp.float32)] * 2,
        in_specs=[in_smem()]
        + in_vmem(count + 3)
        + [pl.BlockSpec(memory_space=pl.ANY)] * (count - 1),
        out_specs=in_vmem(2),
        compiler_params=params,
        cost_estimate=SMALL,
        name="edge",
    )(z_arg, *back_late, source[:, 0], source[:, rows - 1], inverse, *back_early[1:])
    low = lax.ppermute(top, "dom", upward)
    high = lax.ppermute(bottom, "dom", downward)

    sigma = cheb_center / cheb_radius
    rho_zero = 1.0 / sigma
    rho_one = 1.0 / (2.0 * sigma - rho_zero)
    block = min(16, here)
    early_spec = pl.BlockSpec((half, block, cells), lambda i: (0, i, 0))
    late_spec = pl.BlockSpec((slab - half, block, cells), lambda i: (0, i, 0))
    flat_spec = pl.BlockSpec((block, rows, cells), lambda i: (i, 0, 0))
    updated, residual = pl.pallas_call(
        functools.partial(post_kernel, count, slab, half, rows, rho_zero, rho_one),
        grid=(here // block,),
        out_shape=[jax.ShapeDtypeStruct((here, rows, cells), jnp.float32)] * 2,
        in_specs=[in_smem()]
        + [early_spec] * count
        + [late_spec] * count
        + [flat_spec, flat_spec]
        + [
            pl.BlockSpec((6, rows, cells), lambda i: (0, 0, 0)),
            pl.BlockSpec((rows, cells), lambda i: (0, 0)),
        ],
        out_specs=[flat_spec, flat_spec],
        scratch_shapes=[pltpu.VMEM((rows, block, cells), jnp.float32)],
        compiler_params=params,
        name="post",
    )(
        z_arg,
        *back_early,
        *back_late,
        source,
        iterate,
        faces,
        inverse,
    )
    tile = 8 if rows % 8 == 0 else rows
    last = rows // tile - 1
    tile_spec = pl.BlockSpec((here, tile, cells), lambda i: (0, i * last, 0))
    updated = pl.pallas_call(
        functools.partial(close_kernel, rho_one),
        grid=(2 if last else 1,),
        out_shape=jax.ShapeDtypeStruct((here, rows, cells), jnp.float32),
        in_specs=[
            pl.BlockSpec((here, cells), lambda i: (0, 0)),
            pl.BlockSpec((here, cells), lambda i: (0, 0)),
            pl.BlockSpec((6, rows, cells), lambda i: (0, 0, 0)),
            pl.BlockSpec((rows, cells), lambda i: (0, 0)),
            tile_spec,
        ],
        out_specs=tile_spec,
        input_output_aliases={4: 0},
        compiler_params=params,
        name="close",
    )(low, high, faces, inverse, updated)
    return updated, residual


def solution(mesh):
    return jax.shard_map(
        body,
        mesh=mesh,
        in_specs=(
            P("mode", "dom", None),
            P("mode", "dom", None),
            P("dom", None),
            P(None, "dom", None),
            P(),
            P(),
        ),
        out_specs=(P("mode", "dom", None), P("mode", "dom", None)),
        check_vma=False,
    )
```

```python
import functools
import jax
import jax.numpy as jnp
from jax import lax
from jax.experimental import pallas as pl
from jax.experimental.pallas import tpu as pltpu
from jax.sharding import PartitionSpec as P

NZ = 16
GROUP = 5

cheb_center = 1.125
cheb_radius = 0.875
SMALL = pl.CostEstimate(flops=1, bytes_accessed=1, transcendentals=0)
LARGE = pl.CostEstimate(flops=10**10, bytes_accessed=2**24, transcendentals=0)
VMEM_LIMIT = 16 * 1024 * 1024


def in_vmem(count):
    return [pl.BlockSpec(memory_space=pltpu.VMEM)] * count


def in_smem():
    return pl.BlockSpec(memory_space=pltpu.SMEM)


def row_of(place, rho, slab, count, rows):
    upward = slab * place + rho
    downward = slab * place + (slab - 1 - rho)
    row = jnp.where(place < count // 2, upward, downward)
    return jnp.clip(row, 0, rows - 1)


def turn_kernel(count, slab, rows, z_ref, x_ref, turned, *outs):
    z = z_ref[0]
    turned[...] = jnp.swapaxes(x_ref[...], 0, 1).astype(jnp.bfloat16)
    for p in range(count):
        place = jnp.bitwise_xor(z, p)
        for rho in range(outs[p].shape[0]):
            outs[p][rho] = turned[row_of(place, rho, slab, count, rows)]


def rim_kernel(turned, mean_ref, fields_ref, source_ref, after, last, first):
    rows, here, cells = turned.shape
    fields = fields_ref.shape[0]
    deep = last.shape[0] - 2 * here
    for out, row, inner in ((first, 0, 1), (last, rows - 1, rows - 2)):
        out[:here] = turned[row].astype(jnp.float32)
        out[here : here + 1, :] = mean_ref[row : row + 1, :]
        for field in range(fields):
            out[here + 1 + field : here + 2 + field, :] = fields_ref[field, row : row + 1, :]
        at = here + 1 + fields
        out[at : at + 1, :] = mean_ref[inner : inner + 1, :]
        rest = deep - fields - 2
        if rest:
            out[at + 1 : at + 1 + rest, :] = jnp.zeros((rest, cells), jnp.float32)
        out[here + deep :] = source_ref[0 if row == 0 else 1]


def late_kernel(count, slab, rows, z_ref, turned, low_ref, high_ref, *refs):
    outs = refs[2:]
    z = z_ref[0]
    here = turned.shape[1]
    for p in range(count):
        place = jnp.bitwise_xor(z, p)
        for k in range(1, outs[p].shape[0]):
            rho = slab - outs[p].shape[0] + 1 + k
            outs[p][k] = turned[row_of(place, rho, slab, count, rows)]
        outs[p][0] = turned[row_of(place, -1, slab, count, rows)]

        @pl.when(place == 0)
        def _():
            outs[p][0] = low_ref[:here].astype(jnp.bfloat16)

        @pl.when(place == count - 1)
        def _():
            outs[p][0] = high_ref[:here].astype(jnp.bfloat16)


def masks(cells):
    lane = lax.broadcasted_iota(jnp.int32, (1, cells), 1)
    in_z = lane % NZ
    one = jnp.float32(1.0)
    zero = jnp.float32(0.0)
    return (
        jnp.where(lane < cells - NZ, one, zero),
        jnp.where(lane >= NZ, one, zero),
        jnp.where(in_z < NZ - 1, one, zero),
        jnp.where(in_z > 0, one, zero),
    )


def beside(field, mask_set):
    cells = field.shape[-1]
    axis = field.ndim - 1
    return (
        pltpu.roll(field, cells - NZ, axis) * mask_set[0],
        pltpu.roll(field, NZ, axis) * mask_set[1],
        pltpu.roll(field, cells - 1, axis) * mask_set[2],
        pltpu.roll(field, 1, axis) * mask_set[3],
    )


def dense_kernel(groups, fields, modes_here, z_ref, entry_ref, value_ref, dense_ref, own_ref):
    size = dense_ref.shape[1]
    entries = entry_ref.shape[1]
    flip = z_ref[0] * modes_here
    mode_id = jnp.bitwise_xor(lax.broadcasted_iota(jnp.int32, (size, entries), 0), flip)
    pick = jnp.where(mode_id == entry_ref[0:1], 1.0, 0.0).astype(jnp.bfloat16)
    depth = -(-fields // 16) * 16
    here = lax.broadcasted_iota(jnp.int32, (depth, entries), 0) == entry_ref[2:3]
    partner = jnp.where(here, entry_ref[1:2].astype(jnp.float32), 0.0).astype(jnp.bfloat16)
    value = jnp.where(here, value_ref[...], 0.0).astype(jnp.bfloat16)
    dims = (((1,), (1,)), ((), ()))
    partner_of = lax.dot_general(pick, partner, dims, preferred_element_type=jnp.float32)
    value_of = lax.dot_general(pick, value, dims, preferred_element_type=jnp.float32)
    column = jnp.bitwise_xor(lax.broadcasted_iota(jnp.int32, (size, size), 1), flip)
    column = column.astype(jnp.float32)
    own_ref[...] = jnp.broadcast_to(value_of[:, 0:1], own_ref.shape)
    for g in range(groups):
        for k in range(GROUP):
            at = 1 + g * GROUP + k
            if at >= fields:
                tile = jnp.zeros((size, size), jnp.float32)
            else:
                tile = jnp.where(
                    column == partner_of[:, at : at + 1], value_of[:, at : at + 1], 0.0
                )
            dense_ref[g, :, k * size : (k + 1) * size] = tile.astype(jnp.bfloat16)


def weight_kernel(
    count,
    z_ref,
    mean_ref,
    fields_ref,
    low_ref,
    high_ref,
    weight_ref,
    faces_ref,
    inverse_ref,
    beyond_ref,
    stack_ref,
    turned,
):
    fields, rows, cells = fields_ref.shape
    deep = stack_ref.shape[0]
    mask_set = masks(cells)
    start = (low_ref.shape[0] - deep) // 2
    stack_ref[0] = mean_ref[...]
    stack_ref[1 : fields + 1] = fields_ref[...]
    stack_ref[fields + 1 :] = jnp.zeros((deep - fields - 1, rows, cells), jnp.float32)
    turned[1 : rows + 1] = jnp.swapaxes(stack_ref[...], 0, 1)
    turned[0] = low_ref[start : start + deep, :]
    turned[rows + 1] = high_ref[start : start + deep, :]
    z = z_ref[0]
    slab = weight_ref.shape[0]
    ahead = jnp.where(z < count // 2, 1, -1)
    for rho in range(slab):
        row = 1 + row_of(z, rho, slab, count, rows)
        centre = turned[row]
        others = (turned[row + ahead], turned[row - ahead]) + beside(centre, mask_set)
        for f, other in enumerate(others):
            weight_ref[rho, f] = 0.5 * (centre + other)
    place = lax.broadcasted_iota(jnp.int32, (rows, cells), 0)
    centre = mean_ref[...]
    high, low = high_ref[start : start + 1, :], low_ref[start : start + 1, :]
    up = jnp.where(place == rows - 1, high, pltpu.roll(centre, rows - 1, 0))
    down = jnp.where(place == 0, low, pltpu.roll(centre, 1, 0))
    diag = None
    for f, other in enumerate((up, down) + beside(centre, mask_set)):
        weight = 0.5 * (centre + other)
        diag = weight if diag is None else diag + weight
        faces_ref[f] = weight if f < 2 else weight * mask_set[f - 2]
    inverse_ref[...] = 1.0 / diag
    second = start + fields + 1
    edges = (
        (low, low_ref[second : second + 1, :], centre[0:1], z_ref[1] > 0),
        (high, high_ref[second : second + 1, :], centre[rows - 1 : rows], z_ref[1] < z_ref[2] - 1),
    )
    for k, (own, outer, inner, there) in enumerate(edges):
        diag = 0.5 * (own + outer) + 0.5 * (own + inner)
        for other in beside(own, mask_set):
            diag = diag + 0.5 * (own + other)
        beyond_ref[k : k + 1, :] = jnp.where(there, 1.0 / jnp.where(there, diag, 1.0), 0.0)


def mix_kernel(count, groups, fields, window, skip, begin, extra, *refs):
    arrays = max(a for a, _ in window) + 1
    sources = refs[: arrays * count]
    dense_ref, own_ref, weight_ref = refs[arrays * count : arrays * count + 3]
    outs = refs[arrays * count + 3 + extra : -4]
    rows_ref, diff_ref, term_ref, total_ref = refs[-4:]
    size, cells = total_ref.shape
    here = size // count
    bf16 = jnp.bfloat16
    for k, (array, row) in enumerate(window):
        for p in range(count):
            part = sources[array * count + (count - p) % count]
            rows_ref[k, p * here : (p + 1) * here, :] = part[row]
    mask_set = masks(cells)
    def each_row(r, carry):
        row = jnp.where(r == 0, begin[0], begin[1] + r)
        r_in = r + jnp.where(r == 0, 0, skip)
        mean_weights = [weight_ref[row, f, 0:1, :] for f in range(6)]
        for t in range(0, size, 16):
            at = slice(t, t + 16)
            centre = rows_ref[r_in + 1, at].astype(jnp.float32)
            others = (
                rows_ref[r_in + 2, at].astype(jnp.float32),
                rows_ref[r_in, at].astype(jnp.float32),
            )
            mean = None
            for f, other in enumerate(others + beside(centre, mask_set)):
                diff = centre - other
                diff_ref[f, at] = diff.astype(bf16)
                part = mean_weights[f] * diff
                mean = part if mean is None else mean + part
            total_ref[at, :] = jnp.concatenate([own_ref[at]] * (cells // 128), 1) * mean
        for g in range(groups):
            for k in range(GROUP):
                field = min(1 + g * GROUP + k, fields - 1)
                weights = [
                    jnp.broadcast_to(weight_ref[row, f, field : field + 1, :], (16, cells))
                    for f in range(6)
                ]
                weights = [w.astype(bf16) for w in weights]
                for t in range(0, size, 16):
                    part = [weights[f] * diff_ref[f, t : t + 16] for f in range(6)]
                    term = ((part[0] + part[1]) + (part[2] + part[3])) + (part[4] + part[5])
                    term_ref[k * size + t : k * size + t + 16, :] = term
            total_ref[...] += jnp.dot(
                dense_ref[g], term_ref[...], preferred_element_type=jnp.float32
            )
        for p in range(count):
            outs[p][r] = total_ref[p * here : (p + 1) * here, :].astype(bf16)
        return carry

    lax.fori_loop(0, outs[0].shape[0], each_row, 0)


def edge_kernel(count, z_ref, low_rim, high_rim, beyond, *refs):
    parts = refs[:count]
    low, high = refs[-2:]
    here = low.shape[0]
    z = z_ref[0]
    start = low_rim.shape[0] - here
    scale = beyond[...] * (1.0 / cheb_center)
    for k in range(count):
        image = parts[k][0].astype(jnp.float32)

        @pl.when(z == k)
        def _():
            high[...] = (high_rim[start:] - image) * scale[1:2]

        @pl.when(jnp.bitwise_xor(z, count - 1) == k)
        def _():
            low[...] = (low_rim[start:] - image) * scale[0:1]


def post_kernel(count, slab, half, rows, rho_zero, rho_one, z_ref, *refs):
    early = refs[:count]
    late = refs[count : 2 * count]
    source, iterate, low, high, faces, inverse = refs[2 * count : 2 * count + 6]
    updated, residual, image = refs[2 * count + 6 :]
    z = z_ref[0]
    modes, _, cells = source.shape
    for k in range(count):
        place = jnp.bitwise_xor(z, (count - k) % count)
        for rho in range(slab):
            if 1 <= rho <= half:
                part = early[k][rho - 1]
            else:
                part = late[k][max(rho - half, 0)]
            image[row_of(place, rho, slab, count, rows)] = part.astype(jnp.float32)
    residual[...] = source[...] - jnp.swapaxes(image[...], 0, 1)
    place = lax.broadcasted_iota(jnp.int32, (rows, cells), 0)
    inv = inverse[...]
    for m in range(modes):
        res = residual[m]
        first = res * (inv * (1.0 / cheb_center))
        up = jnp.where(place == rows - 1, high[m : m + 1, :], pltpu.roll(first, rows - 1, 0))
        down = jnp.where(place == 0, low[m : m + 1, :], pltpu.roll(first, 1, 0))
        near = faces[0] * up + faces[1] * down
        near = near + faces[2] * pltpu.roll(first, cells - NZ, 1)
        near = near + faces[3] * pltpu.roll(first, NZ, 1)
        near = near + faces[4] * pltpu.roll(first, cells - 1, 1)
        near = near + faces[5] * pltpu.roll(first, 1, 1)
        smoothed = (1.0 - 1.0 / cheb_center) * res + near
        step = (1.0 + rho_one * rho_zero) * first + (2.0 * rho_one / cheb_radius) * smoothed * inv
        updated[m] = iterate[m] + step


def body(iterate, source, mean_coef, kl_fields, tri_index, tri_value):
    count = lax.axis_size("mode")
    doms = lax.axis_size("dom")
    z = lax.axis_index("mode")
    places = [z, lax.axis_index("dom"), doms]
    z_arg = jnp.stack([jnp.asarray(a, jnp.int32) for a in places])
    here, rows, cells = iterate.shape
    size = here * count
    slab = rows // count
    half = slab // 2
    fields = kl_fields.shape[0] + 1
    groups = -(-(fields - 1) // GROUP)
    bf16 = jnp.bfloat16
    params = pltpu.CompilerParams(vmem_limit_bytes=VMEM_LIMIT)

    deep = -(-(fields + 1) // 8) * 8

    turned, *early = pl.pallas_call(
        functools.partial(turn_kernel, count, slab, rows),
        out_shape=[jax.ShapeDtypeStruct((rows, here, cells), bf16)]
        + [jax.ShapeDtypeStruct((half + 2, here, cells), bf16)] * count,
        in_specs=[in_smem()] + in_vmem(1),
        out_specs=in_vmem(count + 1),
        compiler_params=params,
        cost_estimate=SMALL,
        name="turn",
    )(z_arg, iterate)

    def swap(arrays):
        taken = [arrays[0]]
        for p in reversed(range(1, count)):
            taken.append(lax.ppermute(arrays[p], "mode", [(i, i ^ p) for i in range(count)]))
        return taken

    early = swap(early)
    entries, values, _ = lax.optimization_barrier((tri_index, tri_value, turned))
    dense, own = pl.pallas_call(
        functools.partial(dense_kernel, groups, fields, here),
        out_shape=[
            jax.ShapeDtypeStruct((groups, size, GROUP * size), bf16),
            jax.ShapeDtypeStruct((size, 128), jnp.float32),
        ],
        in_specs=[in_smem()] + in_vmem(2),
        out_specs=in_vmem(2),
        compiler_params=params,
        cost_estimate=SMALL,
        name="dense",
    )(z_arg, entries.T, values[None])
    upward = [(i, i + 1) for i in range(doms - 1)]
    downward = [(b, a) for a, b in upward]
    source_rows = jnp.stack([source[:, 0], source[:, rows - 1]])
    last_rim, first_rim = pl.pallas_call(
        rim_kernel,
        out_shape=[jax.ShapeDtypeStruct((2 * here + deep, cells), jnp.float32)] * 2,
        in_specs=in_vmem(4) + [pl.BlockSpec(memory_space=pl.ANY)],
        out_specs=in_vmem(2),
        compiler_params=params,
        cost_estimate=SMALL,
        name="rim",
    )(turned, mean_coef, kl_fields, source_rows, own)
    low_rim = lax.ppermute(last_rim, "dom", upward)
    high_rim = lax.ppermute(first_rim, "dom", downward)
    weights, faces, inverse, beyond = pl.pallas_call(
        functools.partial(weight_kernel, count),
        out_shape=[
            jax.ShapeDtypeStruct((slab, 6, deep, cells), jnp.float32),
            jax.ShapeDtypeStruct((6, rows, cells), jnp.float32),
            jax.ShapeDtypeStruct((rows, cells), jnp.float32),
            jax.ShapeDtypeStruct((2, cells), jnp.float32),
        ],
        in_specs=[in_smem()] + in_vmem(4),
        out_specs=in_vmem(4),
        scratch_shapes=[
            pltpu.VMEM((deep, rows, cells), jnp.float32),
            pltpu.VMEM((rows + 2, deep, cells), jnp.float32),
        ],
        compiler_params=params,
        cost_estimate=SMALL,
        name="weights",
    )(z_arg, mean_coef, kl_fields, low_rim, high_rim)
    late = pl.pallas_call(
        functools.partial(late_kernel, count, slab, rows),
        out_shape=[jax.ShapeDtypeStruct((slab - half, here, cells), bf16)] * count,
        in_specs=[in_smem()] + in_vmem(3) + [pl.BlockSpec(memory_space=pl.ANY)] * 2,
        out_specs=in_vmem(count),
        compiler_params=params,
        cost_estimate=SMALL,
        name="late",
    )(z_arg, turned, low_rim, high_rim, early[1], inverse)
    late = swap(late)

    def mix(arrays, window, skip, begin, rows_out, after=()):
        flat = [a for group in arrays for a in group]
        return pl.pallas_call(
            functools.partial(
                mix_kernel, count, groups, fields, window, skip, begin, len(after)
            ),
            out_shape=[jax.ShapeDtypeStruct((rows_out, here, cells), bf16)] * count,
            in_specs=in_vmem(len(flat) + 3)
            + [pl.BlockSpec(memory_space=pl.ANY)] * len(after),
            out_specs=in_vmem(count),
            scratch_shapes=[
                pltpu.VMEM((len(window), size, cells), bf16),
                pltpu.VMEM((6, size, cells), bf16),
                pltpu.VMEM((GROUP * size, cells), bf16),
                pltpu.VMEM((size, cells), jnp.float32),
            ],
            compiler_params=params,
            cost_estimate=LARGE,
            name="mix",
        )(*flat, dense, own, weights, *after)

    window = tuple((0, k) for k in range(half + 2))
    mixed = mix([early], window, 0, (1, 1), half)
    back_early = swap(mixed)
    window = ((1, 0), (0, 0), (0, 1), (0, half), (0, half + 1))
    window += tuple((1, k) for k in range(1, slab - half))
    mixed_late = mix([early, late], window, 2, (0, half), slab - half, mixed[-1:])
    back_late = swap(mixed_late)

    def swap_edge(array, p):
        pairs = []
        for d in range(doms):
            for place, target in ((0, d - 1), (count - 1, d + 1)):
                if 0 <= target < doms:
                    pairs.append((d * count + place, target * count + (place ^ p)))
        return lax.ppermute(array[:1], ("dom", "mode"), pairs)

    edges = [swap_edge(a, p) for p, a in enumerate(mixed_late)]
    low, high = pl.pallas_call(
        functools.partial(edge_kernel, count),
        out_shape=[jax.ShapeDtypeStruct((here, cells), jnp.float32)] * 2,
        in_specs=[in_smem()]
        + in_vmem(count + 3)
        + [pl.BlockSpec(memory_space=pl.ANY)] * (count - 1),
        out_specs=in_vmem(2),
        compiler_params=params,
        cost_estimate=SMALL,
        name="edge",
    )(z_arg, low_rim, high_rim, beyond, *edges, *back_early[1:])

    sigma = cheb_center / cheb_radius
    rho_zero = 1.0 / sigma
    rho_one = 1.0 / (2.0 * sigma - rho_zero)
    block = min(16, here)
    row_spec = pl.BlockSpec((block, cells), lambda i: (i, 0))
    early_spec = pl.BlockSpec((half, block, cells), lambda i: (0, i, 0))
    late_spec = pl.BlockSpec((slab - half, block, cells), lambda i: (0, i, 0))
    flat_spec = pl.BlockSpec((block, rows, cells), lambda i: (i, 0, 0))
    updated, residual = pl.pallas_call(
        functools.partial(post_kernel, count, slab, half, rows, rho_zero, rho_one),
        grid=(here // block,),
        out_shape=[jax.ShapeDtypeStruct((here, rows, cells), jnp.float32)] * 2,
        in_specs=[in_smem()]
        + [early_spec] * count
        + [late_spec] * count
        + [flat_spec, flat_spec, row_spec, row_spec]
        + [
            pl.BlockSpec((6, rows, cells), lambda i: (0, 0, 0)),
            pl.BlockSpec((rows, cells), lambda i: (0, 0)),
        ],
        out_specs=[flat_spec, flat_spec],
        scratch_shapes=[pltpu.VMEM((rows, block, cells), jnp.float32)],
        compiler_params=params,
        name="post",
    )(
        z_arg,
        *back_early,
        *back_late,
        source,
        iterate,
        low,
        high,
        faces,
        inverse,
    )
    return updated, residual


def solution(mesh):
    return jax.shard_map(
        body,
        mesh=mesh,
        in_specs=(
            P("mode", "dom", None),
            P("mode", "dom", None),
            P("dom", None),
            P(None, "dom", None),
            P(),
            P(),
        ),
        out_specs=(P("mode", "dom", None), P("mode", "dom", None)),
        check_vma=False,
    )
```

```python
import functools
import jax
import jax.numpy as jnp
from jax import lax
from jax.experimental import pallas as pl
from jax.experimental.pallas import tpu as pltpu
from jax.sharding import PartitionSpec as P

NZ = 16
GROUP = 5

cheb_center = 1.125
cheb_radius = 0.875
SMALL = pl.CostEstimate(flops=1, bytes_accessed=1, transcendentals=0)
LARGE = pl.CostEstimate(flops=10**10, bytes_accessed=2**24, transcendentals=0)
VMEM_LIMIT = 16 * 1024 * 1024


def in_vmem(count):
    return [pl.BlockSpec(memory_space=pltpu.VMEM)] * count


def in_smem():
    return pl.BlockSpec(memory_space=pltpu.SMEM)


def row_of(place, rho, slab, count, rows):
    upward = slab * place + rho
    downward = slab * place + (slab - 1 - rho)
    row = jnp.where(place < count // 2, upward, downward)
    return jnp.clip(row, 0, rows - 1)


def turn_kernel(count, slab, rows, z_ref, x_ref, turned, *outs):
    z = z_ref[0]
    turned[...] = jnp.swapaxes(x_ref[...], 0, 1).astype(jnp.bfloat16)
    for p in range(count):
        place = jnp.bitwise_xor(z, p)
        for rho in range(outs[p].shape[0]):
            outs[p][rho] = turned[row_of(place, rho, slab, count, rows)]


def rim_kernel(turned, mean_ref, fields_ref, source_ref, after, last, first):
    rows, here, cells = turned.shape
    fields = fields_ref.shape[0]
    deep = last.shape[0] - 2 * here
    for out, row, inner in ((first, 0, 1), (last, rows - 1, rows - 2)):
        out[:here] = turned[row].astype(jnp.float32)
        out[here : here + 1, :] = mean_ref[row : row + 1, :]
        for field in range(fields):
            out[here + 1 + field : here + 2 + field, :] = fields_ref[field, row : row + 1, :]
        at = here + 1 + fields
        out[at : at + 1, :] = mean_ref[inner : inner + 1, :]
        rest = deep - fields - 2
        if rest:
            out[at + 1 : at + 1 + rest, :] = jnp.zeros((rest, cells), jnp.float32)
        out[here + deep :] = source_ref[0 if row == 0 else 1]


def late_kernel(count, slab, rows, z_ref, turned, low_ref, high_ref, *refs):
    outs = refs[2:]
    z = z_ref[0]
    here = turned.shape[1]
    for p in range(count):
        place = jnp.bitwise_xor(z, p)
        for k in range(1, outs[p].shape[0]):
            rho = slab - outs[p].shape[0] + 1 + k
            outs[p][k] = turned[row_of(place, rho, slab, count, rows)]
        outs[p][0] = turned[row_of(place, -1, slab, count, rows)]

        @pl.when(place == 0)
        def _():
            outs[p][0] = low_ref[:here].astype(jnp.bfloat16)

        @pl.when(place == count - 1)
        def _():
            outs[p][0] = high_ref[:here].astype(jnp.bfloat16)


def masks(cells):
    lane = lax.broadcasted_iota(jnp.int32, (1, cells), 1)
    in_z = lane % NZ
    one = jnp.float32(1.0)
    zero = jnp.float32(0.0)
    return (
        jnp.where(lane < cells - NZ, one, zero),
        jnp.where(lane >= NZ, one, zero),
        jnp.where(in_z < NZ - 1, one, zero),
        jnp.where(in_z > 0, one, zero),
    )


def beside(field, mask_set):
    cells = field.shape[-1]
    axis = field.ndim - 1
    return (
        pltpu.roll(field, cells - NZ, axis) * mask_set[0],
        pltpu.roll(field, NZ, axis) * mask_set[1],
        pltpu.roll(field, cells - 1, axis) * mask_set[2],
        pltpu.roll(field, 1, axis) * mask_set[3],
    )


def dense_kernel(groups, fields, modes_here, z_ref, entry_ref, value_ref, dense_ref, own_ref):
    size = dense_ref.shape[1]
    entries = entry_ref.shape[1]
    flip = z_ref[0] * modes_here
    mode_id = jnp.bitwise_xor(lax.broadcasted_iota(jnp.int32, (size, entries), 0), flip)
    pick = jnp.where(mode_id == entry_ref[0:1], 1.0, 0.0).astype(jnp.bfloat16)
    depth = -(-fields // 16) * 16
    here = lax.broadcasted_iota(jnp.int32, (depth, entries), 0) == entry_ref[2:3]
    partner = jnp.where(here, entry_ref[1:2].astype(jnp.float32), 0.0).astype(jnp.bfloat16)
    value = jnp.where(here, value_ref[...], 0.0).astype(jnp.bfloat16)
    dims = (((1,), (1,)), ((), ()))
    partner_of = lax.dot_general(pick, partner, dims, preferred_element_type=jnp.float32)
    value_of = lax.dot_general(pick, value, dims, preferred_element_type=jnp.float32)
    column = jnp.bitwise_xor(lax.broadcasted_iota(jnp.int32, (size, size), 1), flip)
    column = column.astype(jnp.float32)
    own_ref[...] = jnp.broadcast_to(value_of[:, 0:1], own_ref.shape)
    for g in range(groups):
        for k in range(GROUP):
            at = 1 + g * GROUP + k
            if at >= fields:
                tile = jnp.zeros((size, size), jnp.float32)
            else:
                tile = jnp.where(
                    column == partner_of[:, at : at + 1], value_of[:, at : at + 1], 0.0
                )
            dense_ref[g, :, k * size : (k + 1) * size] = tile.astype(jnp.bfloat16)


def weight_kernel(
    count,
    z_ref,
    mean_ref,
    fields_ref,
    low_ref,
    high_ref,
    weight_ref,
    faces_ref,
    inverse_ref,
    beyond_ref,
    stack_ref,
    turned,
):
    fields, rows, cells = fields_ref.shape
    deep = stack_ref.shape[0]
    mask_set = masks(cells)
    start = (low_ref.shape[0] - deep) // 2
    stack_ref[0] = mean_ref[...]
    stack_ref[1 : fields + 1] = fields_ref[...]
    stack_ref[fields + 1 :] = jnp.zeros((deep - fields - 1, rows, cells), jnp.float32)
    turned[1 : rows + 1] = jnp.swapaxes(stack_ref[...], 0, 1)
    turned[0] = low_ref[start : start + deep, :]
    turned[rows + 1] = high_ref[start : start + deep, :]
    z = z_ref[0]
    slab = weight_ref.shape[0]
    ahead = jnp.where(z < count // 2, 1, -1)
    for rho in range(slab):
        row = 1 + row_of(z, rho, slab, count, rows)
        centre = turned[row]
        others = (turned[row + ahead], turned[row - ahead]) + beside(centre, mask_set)
        for f, other in enumerate(others):
            weight_ref[rho, f] = 0.5 * (centre + other)
    place = lax.broadcasted_iota(jnp.int32, (rows, cells), 0)
    centre = mean_ref[...]
    high, low = high_ref[start : start + 1, :], low_ref[start : start + 1, :]
    up = jnp.where(place == rows - 1, high, pltpu.roll(centre, rows - 1, 0))
    down = jnp.where(place == 0, low, pltpu.roll(centre, 1, 0))
    diag = None
    for f, other in enumerate((up, down) + beside(centre, mask_set)):
        weight = 0.5 * (centre + other)
        diag = weight if diag is None else diag + weight
        faces_ref[f] = weight if f < 2 else weight * mask_set[f - 2]
    inverse_ref[...] = 1.0 / diag
    second = start + fields + 1
    edges = (
        (low, low_ref[second : second + 1, :], centre[0:1], z_ref[1] > 0),
        (high, high_ref[second : second + 1, :], centre[rows - 1 : rows], z_ref[1] < z_ref[2] - 1),
    )
    for k, (own, outer, inner, there) in enumerate(edges):
        diag = 0.5 * (own + outer) + 0.5 * (own + inner)
        for other in beside(own, mask_set):
            diag = diag + 0.5 * (own + other)
        beyond_ref[k : k + 1, :] = jnp.where(there, 1.0 / jnp.where(there, diag, 1.0), 0.0)


def mix_kernel(count, groups, fields, window, skip, begin, extra, *refs):
    arrays = max(a for a, _ in window) + 1
    sources = refs[: arrays * count]
    dense_ref, own_ref, weight_ref = refs[arrays * count : arrays * count + 3]
    outs = refs[arrays * count + 3 + extra : -4]
    rows_ref, diff_ref, term_ref, total_ref = refs[-4:]
    size, cells = total_ref.shape
    here = size // count
    bf16 = jnp.bfloat16
    for k, (array, row) in enumerate(window):
        for p in range(count):
            part = sources[array * count + (count - p) % count]
            rows_ref[k, p * here : (p + 1) * here, :] = part[row]
    mask_set = masks(cells)
    def each_row(r, carry):
        row = jnp.where(r == 0, begin[0], begin[1] + r)
        r_in = r + jnp.where(r == 0, 0, skip)
        mean_weights = [weight_ref[row, f, 0:1, :] for f in range(6)]
        for t in range(0, size, 16):
            at = slice(t, t + 16)
            centre = rows_ref[r_in + 1, at].astype(jnp.float32)
            others = (
                rows_ref[r_in + 2, at].astype(jnp.float32),
                rows_ref[r_in, at].astype(jnp.float32),
            )
            mean = None
            for f, other in enumerate(others + beside(centre, mask_set)):
                diff = centre - other
                diff_ref[f, at] = diff.astype(bf16)
                part = mean_weights[f] * diff
                mean = part if mean is None else mean + part
            total_ref[at, :] = jnp.concatenate([own_ref[at]] * (cells // 128), 1) * mean
        for g in range(groups):
            for k in range(GROUP):
                field = min(1 + g * GROUP + k, fields - 1)
                weights = [
                    jnp.broadcast_to(weight_ref[row, f, field : field + 1, :], (16, cells))
                    for f in range(6)
                ]
                weights = [w.astype(bf16) for w in weights]
                for t in range(0, size, 16):
                    part = [weights[f] * diff_ref[f, t : t + 16] for f in range(6)]
                    term = ((part[0] + part[1]) + (part[2] + part[3])) + (part[4] + part[5])
                    term_ref[k * size + t : k * size + t + 16, :] = term
            total_ref[...] += jnp.dot(
                dense_ref[g], term_ref[...], preferred_element_type=jnp.float32
            )
        for p in range(count):
            outs[p][r] = total_ref[p * here : (p + 1) * here, :].astype(bf16)
        return carry

    lax.fori_loop(0, outs[0].shape[0], each_row, 0)


def edge_kernel(count, z_ref, low_rim, high_rim, beyond, *refs):
    parts = refs[:count]
    low, high = refs[-2:]
    here = low.shape[0]
    z = z_ref[0]
    start = low_rim.shape[0] - here
    scale = beyond[...] * (1.0 / cheb_center)
    for k in range(count):
        image = parts[k][0].astype(jnp.float32)

        @pl.when(z == k)
        def _():
            high[...] = (high_rim[start:] - image) * scale[1:2]

        @pl.when(jnp.bitwise_xor(z, count - 1) == k)
        def _():
            low[...] = (low_rim[start:] - image) * scale[0:1]


def post_kernel(count, slab, half, rows, rho_zero, rho_one, z_ref, *refs):
    early = refs[:count]
    late = refs[count : 2 * count]
    source, iterate, low, high, faces, inverse = refs[2 * count : 2 * count + 6]
    updated, residual, image = refs[2 * count + 6 :]
    z = z_ref[0]
    modes, _, cells = source.shape
    for k in range(count):
        place = jnp.bitwise_xor(z, (count - k) % count)
        for rho in range(slab):
            if 1 <= rho <= half:
                part = early[k][rho - 1]
            else:
                part = late[k][max(rho - half, 0)]
            image[row_of(place, rho, slab, count, rows)] = part.astype(jnp.float32)
    residual[...] = source[...] - jnp.swapaxes(image[...], 0, 1)
    place = lax.broadcasted_iota(jnp.int32, (rows, cells), 0)
    inv = inverse[...]
    for m in range(modes):
        res = residual[m]
        first = res * (inv * (1.0 / cheb_center))
        up = jnp.where(place == rows - 1, high[m : m + 1, :], pltpu.roll(first, rows - 1, 0))
        down = jnp.where(place == 0, low[m : m + 1, :], pltpu.roll(first, 1, 0))
        near = faces[0] * up + faces[1] * down
        near = near + faces[2] * pltpu.roll(first, cells - NZ, 1)
        near = near + faces[3] * pltpu.roll(first, NZ, 1)
        near = near + faces[4] * pltpu.roll(first, cells - 1, 1)
        near = near + faces[5] * pltpu.roll(first, 1, 1)
        smoothed = (1.0 - 1.0 / cheb_center) * res + near
        step = (1.0 + rho_one * rho_zero) * first + (2.0 * rho_one / cheb_radius) * smoothed * inv
        updated[m] = iterate[m] + step


def body(iterate, source, mean_coef, kl_fields, tri_index, tri_value):
    count = lax.axis_size("mode")
    doms = lax.axis_size("dom")
    z = lax.axis_index("mode")
    places = [z, lax.axis_index("dom"), doms]
    z_arg = jnp.stack([jnp.asarray(a, jnp.int32) for a in places])
    here, rows, cells = iterate.shape
    size = here * count
    slab = rows // count
    half = slab // 2
    fields = kl_fields.shape[0] + 1
    groups = -(-(fields - 1) // GROUP)
    bf16 = jnp.bfloat16
    params = pltpu.CompilerParams(vmem_limit_bytes=VMEM_LIMIT)

    deep = -(-(fields + 1) // 8) * 8

    turned, *early = pl.pallas_call(
        functools.partial(turn_kernel, count, slab, rows),
        out_shape=[jax.ShapeDtypeStruct((rows, here, cells), bf16)]
        + [jax.ShapeDtypeStruct((half + 2, here, cells), bf16)] * count,
        in_specs=[in_smem()] + in_vmem(1),
        out_specs=in_vmem(count + 1),
        compiler_params=params,
        cost_estimate=SMALL,
        name="turn",
    )(z_arg, iterate)

    def swap(arrays):
        taken = [arrays[0]]
        for p in reversed(range(1, count)):
            taken.append(lax.ppermute(arrays[p], "mode", [(i, i ^ p) for i in range(count)]))
        return taken

    early = swap(early)
    entries, values, _ = lax.optimization_barrier((tri_index, tri_value, turned))
    dense, own = pl.pallas_call(
        functools.partial(dense_kernel, groups, fields, here),
        out_shape=[
            jax.ShapeDtypeStruct((groups, size, GROUP * size), bf16),
            jax.ShapeDtypeStruct((size, 128), jnp.float32),
        ],
        in_specs=[in_smem()] + in_vmem(2),
        out_specs=in_vmem(2),
        compiler_params=params,
        cost_estimate=SMALL,
        name="dense",
    )(z_arg, entries.T, values[None])
    upward = [(i, i + 1) for i in range(doms - 1)]
    downward = [(b, a) for a, b in upward]
    source_rows = jnp.stack([source[:, 0], source[:, rows - 1]])
    last_rim, first_rim = pl.pallas_call(
        rim_kernel,
        out_shape=[jax.ShapeDtypeStruct((2 * here + deep, cells), jnp.float32)] * 2,
        in_specs=in_vmem(4) + [pl.BlockSpec(memory_space=pl.ANY)],
        out_specs=in_vmem(2),
        compiler_params=params,
        cost_estimate=SMALL,
        name="rim",
    )(turned, mean_coef, kl_fields, source_rows, own)
    low_rim = lax.ppermute(last_rim, "dom", upward)
    high_rim = lax.ppermute(first_rim, "dom", downward)
    weights, faces, inverse, beyond = pl.pallas_call(
        functools.partial(weight_kernel, count),
        out_shape=[
            jax.ShapeDtypeStruct((slab, 6, deep, cells), jnp.float32),
            jax.ShapeDtypeStruct((6, rows, cells), jnp.float32),
            jax.ShapeDtypeStruct((rows, cells), jnp.float32),
            jax.ShapeDtypeStruct((2, cells), jnp.float32),
        ],
        in_specs=[in_smem()] + in_vmem(4),
        out_specs=in_vmem(4),
        scratch_shapes=[
            pltpu.VMEM((deep, rows, cells), jnp.float32),
            pltpu.VMEM((rows + 2, deep, cells), jnp.float32),
        ],
        compiler_params=params,
        cost_estimate=SMALL,
        name="weights",
    )(z_arg, mean_coef, kl_fields, low_rim, high_rim)
    late = pl.pallas_call(
        functools.partial(late_kernel, count, slab, rows),
        out_shape=[jax.ShapeDtypeStruct((slab - half, here, cells), bf16)] * count,
        in_specs=[in_smem()] + in_vmem(3) + [pl.BlockSpec(memory_space=pl.ANY)] * 2,
        out_specs=in_vmem(count),
        compiler_params=params,
        cost_estimate=SMALL,
        name="late",
    )(z_arg, turned, low_rim, high_rim, early[1], inverse)
    late = swap(late)

    def mix(arrays, window, skip, begin, rows_out, after=()):
        flat = [a for group in arrays for a in group]
        return pl.pallas_call(
            functools.partial(
                mix_kernel, count, groups, fields, window, skip, begin, len(after)
            ),
            out_shape=[jax.ShapeDtypeStruct((rows_out, here, cells), bf16)] * count,
            in_specs=in_vmem(len(flat) + 3)
            + [pl.BlockSpec(memory_space=pl.ANY)] * len(after),
            out_specs=in_vmem(count),
            scratch_shapes=[
                pltpu.VMEM((len(window), size, cells), bf16),
                pltpu.VMEM((6, size, cells), bf16),
                pltpu.VMEM((GROUP * size, cells), bf16),
                pltpu.VMEM((size, cells), jnp.float32),
            ],
            compiler_params=params,
            cost_estimate=LARGE,
            name="mix",
        )(*flat, dense, own, weights, *after)

    window = tuple((0, k) for k in range(half + 2))
    mixed = mix([early], window, 0, (1, 1), half)
    back_early = swap(mixed)
    window = ((1, 0), (0, 0), (0, 1), (0, half), (0, half + 1))
    window += tuple((1, k) for k in range(1, slab - half))
    mixed_late = mix([early, late], window, 2, (0, half), slab - half, mixed[-1:])
    back_late = swap(mixed_late)

    def swap_edge(array, p):
        pairs = []
        for d in range(doms):
            for place, target in ((0, d - 1), (count - 1, d + 1)):
                if 0 <= target < doms:
                    pairs.append((d * count + place, target * count + (place ^ p)))
        return lax.ppermute(array, ("dom", "mode"), pairs)

    near_edges, *_ = lax.optimization_barrier(
        (tuple(a[:1] for a in mixed_late), back_late[-1], *back_early[1:])
    )
    edges = [swap_edge(a, p) for p, a in enumerate(near_edges)]
    low, high = pl.pallas_call(
        functools.partial(edge_kernel, count),
        out_shape=[jax.ShapeDtypeStruct((here, cells), jnp.float32)] * 2,
        in_specs=[in_smem()]
        + in_vmem(count + 3)
        + [pl.BlockSpec(memory_space=pl.ANY)] * (count - 1),
        out_specs=in_vmem(2),
        compiler_params=params,
        cost_estimate=SMALL,
        name="edge",
    )(z_arg, low_rim, high_rim, beyond, *edges, *back_early[1:])

    sigma = cheb_center / cheb_radius
    rho_zero = 1.0 / sigma
    rho_one = 1.0 / (2.0 * sigma - rho_zero)
    block = min(16, here)
    row_spec = pl.BlockSpec((block, cells), lambda i: (i, 0))
    early_spec = pl.BlockSpec((half, block, cells), lambda i: (0, i, 0))
    late_spec = pl.BlockSpec((slab - half, block, cells), lambda i: (0, i, 0))
    flat_spec = pl.BlockSpec((block, rows, cells), lambda i: (i, 0, 0))
    updated, residual = pl.pallas_call(
        functools.partial(post_kernel, count, slab, half, rows, rho_zero, rho_one),
        grid=(here // block,),
        out_shape=[jax.ShapeDtypeStruct((here, rows, cells), jnp.float32)] * 2,
        in_specs=[in_smem()]
        + [early_spec] * count
        + [late_spec] * count
        + [flat_spec, flat_spec, row_spec, row_spec]
        + [
            pl.BlockSpec((6, rows, cells), lambda i: (0, 0, 0)),
            pl.BlockSpec((rows, cells), lambda i: (0, 0)),
        ],
        out_specs=[flat_spec, flat_spec],
        scratch_shapes=[pltpu.VMEM((rows, block, cells), jnp.float32)],
        compiler_params=params,
        name="post",
    )(
        z_arg,
        *back_early,
        *back_late,
        source,
        iterate,
        low,
        high,
        faces,
        inverse,
    )
    return updated, residual


def solution(mesh):
    return jax.shard_map(
        body,
        mesh=mesh,
        in_specs=(
            P("mode", "dom", None),
            P("mode", "dom", None),
            P("dom", None),
            P(None, "dom", None),
            P(),
            P(),
        ),
        out_specs=(P("mode", "dom", None), P("mode", "dom", None)),
        check_vma=False,
    )
```

```python
import functools
import jax
import jax.numpy as jnp
from jax import lax
from jax.experimental import pallas as pl
from jax.experimental.pallas import tpu as pltpu
from jax.sharding import PartitionSpec as P

NZ = 16
GROUP = 5

cheb_center = 1.125
cheb_radius = 0.875
SMALL = pl.CostEstimate(flops=1, bytes_accessed=1, transcendentals=0)
LARGE = pl.CostEstimate(flops=10**10, bytes_accessed=2**24, transcendentals=0)
VMEM_LIMIT = 16 * 1024 * 1024


def in_vmem(count):
    return [pl.BlockSpec(memory_space=pltpu.VMEM)] * count


def in_smem():
    return pl.BlockSpec(memory_space=pltpu.SMEM)


def row_of(place, rho, slab, count, rows):
    upward = slab * place + rho
    downward = slab * place + (slab - 1 - rho)
    row = jnp.where(place < count // 2, upward, downward)
    return jnp.clip(row, 0, rows - 1)


def turn_kernel(count, slab, rows, z_ref, x_ref, turned, *outs):
    z = z_ref[0]
    turned[...] = jnp.swapaxes(x_ref[...], 0, 1).astype(jnp.bfloat16)
    for p in range(count):
        place = jnp.bitwise_xor(z, p)
        for rho in range(outs[p].shape[0]):
            outs[p][rho] = turned[row_of(place, rho, slab, count, rows)]


def rim_kernel(turned, mean_ref, fields_ref, after, last, first):
    rows, here, cells = turned.shape
    fields = fields_ref.shape[0]
    for out, row in ((first, 0), (last, rows - 1)):
        out[:here] = turned[row].astype(jnp.float32)
        out[here : here + 1, :] = mean_ref[row : row + 1, :]
        for field in range(fields):
            out[here + 1 + field : here + 2 + field, :] = fields_ref[field, row : row + 1, :]
        rest = out.shape[0] - here - 1 - fields
        out[here + 1 + fields :, :] = jnp.zeros((rest, cells), jnp.float32)


def late_kernel(count, slab, rows, z_ref, turned, *refs):
    outs = refs[2:]
    z = z_ref[0]
    for p in range(count):
        place = jnp.bitwise_xor(z, p)
        for k in range(outs[p].shape[0]):
            rho = slab + 1 - outs[p].shape[0] + k
            outs[p][k] = turned[row_of(place, rho, slab, count, rows)]


def beyond_kernel(count, slab, rows, z_ref, turned, low_ref, high_ref, *outs):
    z = z_ref[0]
    here = turned.shape[1]
    for p in range(count):
        place = jnp.bitwise_xor(z, p)
        outs[p][0] = turned[row_of(place, -1, slab, count, rows)]

        @pl.when(place == 0)
        def _():
            outs[p][0] = low_ref[:here].astype(jnp.bfloat16)

        @pl.when(place == count - 1)
        def _():
            outs[p][0] = high_ref[:here].astype(jnp.bfloat16)


def masks(cells):
    lane = lax.broadcasted_iota(jnp.int32, (1, cells), 1)
    in_z = lane % NZ
    one = jnp.float32(1.0)
    zero = jnp.float32(0.0)
    return (
        jnp.where(lane < cells - NZ, one, zero),
        jnp.where(lane >= NZ, one, zero),
        jnp.where(in_z < NZ - 1, one, zero),
        jnp.where(in_z > 0, one, zero),
    )


def beside(field, mask_set):
    cells = field.shape[-1]
    axis = field.ndim - 1
    return (
        pltpu.roll(field, cells - NZ, axis) * mask_set[0],
        pltpu.roll(field, NZ, axis) * mask_set[1],
        pltpu.roll(field, cells - 1, axis) * mask_set[2],
        pltpu.roll(field, 1, axis) * mask_set[3],
    )


def dense_kernel(groups, fields, modes_here, z_ref, entry_ref, value_ref, dense_ref, own_ref):
    size = dense_ref.shape[1]
    entries = entry_ref.shape[1]
    flip = z_ref[0] * modes_here
    mode_id = jnp.bitwise_xor(lax.broadcasted_iota(jnp.int32, (size, entries), 0), flip)
    pick = jnp.where(mode_id == entry_ref[0:1], 1.0, 0.0).astype(jnp.bfloat16)
    depth = -(-fields // 16) * 16
    here = lax.broadcasted_iota(jnp.int32, (depth, entries), 0) == entry_ref[2:3]
    partner = jnp.where(here, entry_ref[1:2].astype(jnp.float32), 0.0).astype(jnp.bfloat16)
    value = jnp.where(here, value_ref[...], 0.0).astype(jnp.bfloat16)
    dims = (((1,), (1,)), ((), ()))
    partner_of = lax.dot_general(pick, partner, dims, preferred_element_type=jnp.float32)
    value_of = lax.dot_general(pick, value, dims, preferred_element_type=jnp.float32)
    column = jnp.bitwise_xor(lax.broadcasted_iota(jnp.int32, (size, size), 1), flip)
    column = column.astype(jnp.float32)
    own_ref[...] = jnp.broadcast_to(value_of[:, 0:1], own_ref.shape)
    for g in range(groups):
        for k in range(GROUP):
            at = 1 + g * GROUP + k
            if at >= fields:
                tile = jnp.zeros((size, size), jnp.float32)
            else:
                tile = jnp.where(
                    column == partner_of[:, at : at + 1], value_of[:, at : at + 1], 0.0
                )
            dense_ref[g, :, k * size : (k + 1) * size] = tile.astype(jnp.bfloat16)


def weight_kernel(
    count,
    z_ref,
    mean_ref,
    fields_ref,
    low_ref,
    high_ref,
    weight_ref,
    faces_ref,
    inverse_ref,
    stack_ref,
    turned,
):
    fields, rows, cells = fields_ref.shape
    deep = stack_ref.shape[0]
    mask_set = masks(cells)
    start = low_ref.shape[0] - deep
    stack_ref[0] = mean_ref[...]
    stack_ref[1 : fields + 1] = fields_ref[...]
    stack_ref[fields + 1 :] = jnp.zeros((deep - fields - 1, rows, cells), jnp.float32)
    turned[1 : rows + 1] = jnp.swapaxes(stack_ref[...], 0, 1)
    turned[0] = low_ref[start:, :]
    turned[rows + 1] = high_ref[start:, :]
    z = z_ref[0]
    slab = weight_ref.shape[0]
    ahead = jnp.where(z < count // 2, 1, -1)
    for rho in range(slab):
        row = 1 + row_of(z, rho, slab, count, rows)
        centre = turned[row]
        others = (turned[row + ahead], turned[row - ahead]) + beside(centre, mask_set)
        for f, other in enumerate(others):
            weight_ref[rho, f] = 0.5 * (centre + other)
    place = lax.broadcasted_iota(jnp.int32, (rows, cells), 0)
    centre = mean_ref[...]
    high, low = high_ref[start : start + 1, :], low_ref[start : start + 1, :]
    up = jnp.where(place == rows - 1, high, pltpu.roll(centre, rows - 1, 0))
    down = jnp.where(place == 0, low, pltpu.roll(centre, 1, 0))
    diag = None
    for f, other in enumerate((up, down) + beside(centre, mask_set)):
        weight = 0.5 * (centre + other)
        diag = weight if diag is None else diag + weight
        faces_ref[f] = weight if f < 2 else weight * mask_set[f - 2]
    inverse_ref[...] = 1.0 / diag


def mix_kernel(count, groups, fields, window, skip, begin, extra, *refs):
    arrays = max(a for a, _ in window) + 1
    sources = refs[: arrays * count]
    dense_ref, own_ref, weight_ref = refs[arrays * count : arrays * count + 3]
    outs = refs[arrays * count + 3 + extra : -4]
    rows_ref, diff_ref, term_ref, total_ref = refs[-4:]
    size, cells = total_ref.shape
    here = size // count
    bf16 = jnp.bfloat16
    for k, (array, row) in enumerate(window):
        for p in range(count):
            part = sources[array * count + (count - p) % count]
            rows_ref[k, p * here : (p + 1) * here, :] = part[row]
    mask_set = masks(cells)
    def each_row(r, carry):
        row = jnp.where(r == 0, begin[0], begin[1] + r)
        r_in = r + jnp.where(r == 0, 0, skip)
        mean_weights = [weight_ref[row, f, 0:1, :] for f in range(6)]
        for t in range(0, size, 16):
            at = slice(t, t + 16)
            centre = rows_ref[r_in + 1, at].astype(jnp.float32)
            others = (
                rows_ref[r_in + 2, at].astype(jnp.float32),
                rows_ref[r_in, at].astype(jnp.float32),
            )
            mean = None
            for f, other in enumerate(others + beside(centre, mask_set)):
                diff = centre - other
                diff_ref[f, at] = diff.astype(bf16)
                part = mean_weights[f] * diff
                mean = part if mean is None else mean + part
            total_ref[at, :] = jnp.concatenate([own_ref[at]] * (cells // 128), 1) * mean
        for g in range(groups):
            for k in range(GROUP):
                field = min(1 + g * GROUP + k, fields - 1)
                weights = [
                    jnp.broadcast_to(weight_ref[row, f, field : field + 1, :], (16, cells))
                    for f in range(6)
                ]
                weights = [w.astype(bf16) for w in weights]
                for t in range(0, size, 16):
                    part = [weights[f] * diff_ref[f, t : t + 16] for f in range(6)]
                    term = ((part[0] + part[1]) + (part[2] + part[3])) + (part[4] + part[5])
                    term_ref[k * size + t : k * size + t + 16, :] = term
            total_ref[...] += jnp.dot(
                dense_ref[g], term_ref[...], preferred_element_type=jnp.float32
            )
        for p in range(count):
            outs[p][r] = total_ref[p * here : (p + 1) * here, :].astype(bf16)
        return carry

    lax.fori_loop(0, outs[0].shape[0], each_row, 0)


def edge_kernel(count, z_ref, *refs):
    parts = refs[:count]
    bottom_source, top_source, inverse = refs[count : count + 3]
    bottom, top = refs[-2:]
    z = z_ref[0]
    rows = inverse.shape[0]
    for k in range(count):
        place = jnp.bitwise_xor(z, (count - k) % count)
        image = parts[k][0].astype(jnp.float32)

        @pl.when(place == 0)
        def _():
            scale = inverse[0:1] * (1.0 / cheb_center)
            bottom[...] = (bottom_source[...] - image) * scale

        @pl.when(place == count - 1)
        def _():
            scale = inverse[rows - 1 : rows] * (1.0 / cheb_center)
            top[...] = (top_source[...] - image) * scale


def post_kernel(count, slab, half, rows, rho_zero, rho_one, z_ref, *refs):
    early = refs[:count]
    late = refs[count : 2 * count]
    source, iterate, low, high, faces, inverse = refs[2 * count : 2 * count + 6]
    updated, residual, image = refs[2 * count + 6 :]
    z = z_ref[0]
    modes, _, cells = source.shape
    for k in range(count):
        place = jnp.bitwise_xor(z, (count - k) % count)
        for rho in range(slab):
            part = early[k][rho] if rho < half else late[k][rho - half]
            image[row_of(place, rho, slab, count, rows)] = part.astype(jnp.float32)
    residual[...] = source[...] - jnp.swapaxes(image[...], 0, 1)
    place = lax.broadcasted_iota(jnp.int32, (rows, cells), 0)
    inv = inverse[...]
    for m in range(modes):
        res = residual[m]
        first = res * (inv * (1.0 / cheb_center))
        up = jnp.where(place == rows - 1, high[m : m + 1, :], pltpu.roll(first, rows - 1, 0))
        down = jnp.where(place == 0, low[m : m + 1, :], pltpu.roll(first, 1, 0))
        near = faces[0] * up + faces[1] * down
        near = near + faces[2] * pltpu.roll(first, cells - NZ, 1)
        near = near + faces[3] * pltpu.roll(first, NZ, 1)
        near = near + faces[4] * pltpu.roll(first, cells - 1, 1)
        near = near + faces[5] * pltpu.roll(first, 1, 1)
        smoothed = (1.0 - 1.0 / cheb_center) * res + near
        step = (1.0 + rho_one * rho_zero) * first + (2.0 * rho_one / cheb_radius) * smoothed * inv
        updated[m] = iterate[m] + step


def body(iterate, source, mean_coef, kl_fields, tri_index, tri_value):
    count = lax.axis_size("mode")
    doms = lax.axis_size("dom")
    z = lax.axis_index("mode")
    z_arg = z.astype(jnp.int32).reshape(1)
    here, rows, cells = iterate.shape
    size = here * count
    slab = rows // count
    half = slab // 2
    fields = kl_fields.shape[0] + 1
    groups = -(-(fields - 1) // GROUP)
    bf16 = jnp.bfloat16
    params = pltpu.CompilerParams(vmem_limit_bytes=VMEM_LIMIT)

    deep = -(-fields // 8) * 8

    turned, *early = pl.pallas_call(
        functools.partial(turn_kernel, count, slab, rows),
        out_shape=[jax.ShapeDtypeStruct((rows, here, cells), bf16)]
        + [jax.ShapeDtypeStruct((half + 1, here, cells), bf16)] * count,
        in_specs=[in_smem()] + in_vmem(1),
        out_specs=in_vmem(count + 1),
        compiler_params=params,
        cost_estimate=SMALL,
        name="turn",
    )(z_arg, iterate)

    def swap(arrays):
        taken = [arrays[0]]
        for p in reversed(range(1, count)):
            taken.append(lax.ppermute(arrays[p], "mode", [(i, i ^ p) for i in range(count)]))
        return taken

    early = swap(early)
    entries, values, _ = lax.optimization_barrier((tri_index, tri_value, turned))
    dense, own = pl.pallas_call(
        functools.partial(dense_kernel, groups, fields, here),
        out_shape=[
            jax.ShapeDtypeStruct((groups, size, GROUP * size), bf16),
            jax.ShapeDtypeStruct((size, 128), jnp.float32),
        ],
        in_specs=[in_smem()] + in_vmem(2),
        out_specs=in_vmem(2),
        compiler_params=params,
        cost_estimate=SMALL,
        name="dense",
    )(z_arg, entries.T, values[None])
    upward = [(i, i + 1) for i in range(doms - 1)]
    downward = [(b, a) for a, b in upward]
    last_rim, first_rim = pl.pallas_call(
        rim_kernel,
        out_shape=[jax.ShapeDtypeStruct((here + deep, cells), jnp.float32)] * 2,
        in_specs=in_vmem(3) + [pl.BlockSpec(memory_space=pl.ANY)],
        out_specs=in_vmem(2),
        compiler_params=params,
        cost_estimate=SMALL,
        name="rim",
    )(turned, mean_coef, kl_fields, own)
    low_rim = lax.ppermute(last_rim, "dom", upward)
    high_rim = lax.ppermute(first_rim, "dom", downward)
    weights, faces, inverse = pl.pallas_call(
        functools.partial(weight_kernel, count),
        out_shape=[
            jax.ShapeDtypeStruct((slab, 6, deep, cells), jnp.float32),
            jax.ShapeDtypeStruct((6, rows, cells), jnp.float32),
            jax.ShapeDtypeStruct((rows, cells), jnp.float32),
        ],
        in_specs=[in_smem()] + in_vmem(4),
        out_specs=in_vmem(3),
        scratch_shapes=[
            pltpu.VMEM((deep, rows, cells), jnp.float32),
            pltpu.VMEM((rows + 2, deep, cells), jnp.float32),
        ],
        compiler_params=params,
        cost_estimate=SMALL,
        name="weights",
    )(z_arg, mean_coef, kl_fields, low_rim, high_rim)
    rims = pl.pallas_call(
        functools.partial(beyond_kernel, count, slab, rows),
        out_shape=[jax.ShapeDtypeStruct((1, here, cells), bf16)] * count,
        in_specs=[in_smem()] + in_vmem(3),
        out_specs=in_vmem(count),
        compiler_params=params,
        cost_estimate=SMALL,
        name="beyond",
    )(z_arg, turned, low_rim, high_rim)
    rims = swap(rims)
    late = pl.pallas_call(
        functools.partial(late_kernel, count, slab, rows),
        out_shape=[jax.ShapeDtypeStruct((slab - half, here, cells), bf16)] * count,
        in_specs=[in_smem()] + in_vmem(1) + [pl.BlockSpec(memory_space=pl.ANY)] * 2,
        out_specs=in_vmem(count),
        compiler_params=params,
        cost_estimate=SMALL,
        name="late",
    )(z_arg, turned, early[-2], inverse)
    late = swap(late)

    def mix(arrays, window, skip, begin, rows_out, after=()):
        flat = [a for group in arrays for a in group]
        return pl.pallas_call(
            functools.partial(
                mix_kernel, count, groups, fields, window, skip, begin, len(after)
            ),
            out_shape=[jax.ShapeDtypeStruct((rows_out, here, cells), bf16)] * count,
            in_specs=in_vmem(len(flat) + 3)
            + [pl.BlockSpec(memory_space=pl.ANY)] * len(after),
            out_specs=in_vmem(count),
            scratch_shapes=[
                pltpu.VMEM((len(window), size, cells), bf16),
                pltpu.VMEM((6, size, cells), bf16),
                pltpu.VMEM((GROUP * size, cells), bf16),
                pltpu.VMEM((size, cells), jnp.float32),
            ],
            compiler_params=params,
            cost_estimate=LARGE,
            name="mix",
        )(*flat, dense, own, weights, *after)

    window = ((0, 0),) + tuple((1, k) for k in range(half + 1))
    mixed = mix([rims, early], window, 0, (0, 0), half)
    back_early = swap(mixed)
    window = ((0, half - 1), (0, half)) + tuple((1, k) for k in range(slab - half))
    back_late = swap(mix([early, late], window, 0, (half, half), slab - half, mixed[-1:]))

    bottom, top = pl.pallas_call(
        functools.partial(edge_kernel, count),
        out_shape=[jax.ShapeDtypeStruct((here, cells), jnp.float32)] * 2,
        in_specs=[in_smem()] + in_vmem(count + 3),
        out_specs=in_vmem(2),
        compiler_params=params,
        cost_estimate=SMALL,
        name="edge",
    )(z_arg, *back_early, source[:, 0], source[:, rows - 1], inverse)
    low = lax.ppermute(top, "dom", upward)
    high = lax.ppermute(bottom, "dom", downward)

    sigma = cheb_center / cheb_radius
    rho_zero = 1.0 / sigma
    rho_one = 1.0 / (2.0 * sigma - rho_zero)
    block = min(16, here)
    row_spec = pl.BlockSpec((block, cells), lambda i: (i, 0))
    early_spec = pl.BlockSpec((half, block, cells), lambda i: (0, i, 0))
    late_spec = pl.BlockSpec((slab - half, block, cells), lambda i: (0, i, 0))
    flat_spec = pl.BlockSpec((block, rows, cells), lambda i: (i, 0, 0))
    updated, residual = pl.pallas_call(
        functools.partial(post_kernel, count, slab, half, rows, rho_zero, rho_one),
        grid=(here // block,),
        out_shape=[jax.ShapeDtypeStruct((here, rows, cells), jnp.float32)] * 2,
        in_specs=[in_smem()]
        + [early_spec] * count
        + [late_spec] * count
        + [flat_spec, flat_spec, row_spec, row_spec]
        + [
            pl.BlockSpec((6, rows, cells), lambda i: (0, 0, 0)),
            pl.BlockSpec((rows, cells), lambda i: (0, 0)),
        ],
        out_specs=[flat_spec, flat_spec],
        scratch_shapes=[pltpu.VMEM((rows, block, cells), jnp.float32)],
        compiler_params=params,
        name="post",
    )(
        z_arg,
        *back_early,
        *back_late,
        source,
        iterate,
        low,
        high,
        faces,
        inverse,
    )
    return updated, residual


def solution(mesh):
    return jax.shard_map(
        body,
        mesh=mesh,
        in_specs=(
            P("mode", "dom", None),
            P("mode", "dom", None),
            P("dom", None),
            P(None, "dom", None),
            P(),
            P(),
        ),
        out_specs=(P("mode", "dom", None), P("mode", "dom", None)),
        check_vma=False,
    )
```

```python
import functools
import jax
import jax.numpy as jnp
from jax import lax
from jax.experimental import pallas as pl
from jax.experimental.pallas import tpu as pltpu
from jax.sharding import PartitionSpec as P

NZ = 16
GROUP = 5

cheb_center = 1.125
cheb_radius = 0.875
SMALL = pl.CostEstimate(flops=1, bytes_accessed=1, transcendentals=0)
LARGE = pl.CostEstimate(flops=10**10, bytes_accessed=2**24, transcendentals=0)
VMEM_LIMIT = 16 * 1024 * 1024


def in_vmem(count):
    return [pl.BlockSpec(memory_space=pltpu.VMEM)] * count


def in_smem():
    return pl.BlockSpec(memory_space=pltpu.SMEM)


def row_of(place, rho, slab, count, rows):
    upward = slab * place + rho
    downward = slab * place + (slab - 1 - rho)
    row = jnp.where(place < count // 2, upward, downward)
    return jnp.clip(row, 0, rows - 1)


def turn_kernel(count, slab, rows, z_ref, x_ref, turned, *outs):
    z = z_ref[0]
    turned[...] = jnp.swapaxes(x_ref[...], 0, 1).astype(jnp.bfloat16)
    for p in range(count):
        place = jnp.bitwise_xor(z, p)
        for rho in range(outs[p].shape[0]):
            outs[p][rho] = turned[row_of(place, rho, slab, count, rows)]


def rim_kernel(turned, mean_ref, fields_ref, *refs):
    last, first = refs[-2:]
    rows, here, cells = turned.shape
    fields = fields_ref.shape[0]
    for out, row in ((first, 0), (last, rows - 1)):
        out[:here] = turned[row].astype(jnp.float32)
        out[here : here + 1, :] = mean_ref[row : row + 1, :]
        for field in range(fields):
            out[here + 1 + field : here + 2 + field, :] = fields_ref[field, row : row + 1, :]
        rest = out.shape[0] - here - 1 - fields
        out[here + 1 + fields :, :] = jnp.zeros((rest, cells), jnp.float32)


def late_kernel(count, slab, rows, z_ref, turned, *refs):
    outs = refs[2:]
    z = z_ref[0]
    for p in range(count):
        place = jnp.bitwise_xor(z, p)
        for k in range(outs[p].shape[0]):
            rho = slab + 1 - outs[p].shape[0] + k
            outs[p][k] = turned[row_of(place, rho, slab, count, rows)]


def beyond_kernel(count, slab, rows, z_ref, turned, low_ref, high_ref, *refs):
    outs = refs[-count:]
    z = z_ref[0]
    here = turned.shape[1]
    for p in range(count):
        place = jnp.bitwise_xor(z, p)
        outs[p][0] = turned[row_of(place, -1, slab, count, rows)]

        @pl.when(place == 0)
        def _():
            outs[p][0] = low_ref[:here].astype(jnp.bfloat16)

        @pl.when(place == count - 1)
        def _():
            outs[p][0] = high_ref[:here].astype(jnp.bfloat16)


def masks(cells):
    lane = lax.broadcasted_iota(jnp.int32, (1, cells), 1)
    in_z = lane % NZ
    one = jnp.float32(1.0)
    zero = jnp.float32(0.0)
    return (
        jnp.where(lane < cells - NZ, one, zero),
        jnp.where(lane >= NZ, one, zero),
        jnp.where(in_z < NZ - 1, one, zero),
        jnp.where(in_z > 0, one, zero),
    )


def beside(field, mask_set):
    cells = field.shape[-1]
    axis = field.ndim - 1
    return (
        pltpu.roll(field, cells - NZ, axis) * mask_set[0],
        pltpu.roll(field, NZ, axis) * mask_set[1],
        pltpu.roll(field, cells - 1, axis) * mask_set[2],
        pltpu.roll(field, 1, axis) * mask_set[3],
    )


def dense_kernel(groups, fields, modes_here, z_ref, entry_ref, value_ref, dense_ref, own_ref):
    size = dense_ref.shape[1]
    entries = entry_ref.shape[1]
    flip = z_ref[0] * modes_here
    mode_id = jnp.bitwise_xor(lax.broadcasted_iota(jnp.int32, (size, entries), 0), flip)
    pick = jnp.where(mode_id == entry_ref[0:1], 1.0, 0.0).astype(jnp.bfloat16)
    depth = -(-fields // 16) * 16
    here = lax.broadcasted_iota(jnp.int32, (depth, entries), 0) == entry_ref[2:3]
    partner = jnp.where(here, entry_ref[1:2].astype(jnp.float32), 0.0).astype(jnp.bfloat16)
    value = jnp.where(here, value_ref[...], 0.0).astype(jnp.bfloat16)
    dims = (((1,), (1,)), ((), ()))
    partner_of = lax.dot_general(pick, partner, dims, preferred_element_type=jnp.float32)
    value_of = lax.dot_general(pick, value, dims, preferred_element_type=jnp.float32)
    column = jnp.bitwise_xor(lax.broadcasted_iota(jnp.int32, (size, size), 1), flip)
    column = column.astype(jnp.float32)
    own_ref[...] = jnp.broadcast_to(value_of[:, 0:1], own_ref.shape)
    for g in range(groups):
        for k in range(GROUP):
            at = 1 + g * GROUP + k
            if at >= fields:
                tile = jnp.zeros((size, size), jnp.float32)
            else:
                tile = jnp.where(
                    column == partner_of[:, at : at + 1], value_of[:, at : at + 1], 0.0
                )
            dense_ref[g, :, k * size : (k + 1) * size] = tile.astype(jnp.bfloat16)


def weight_kernel(
    count,
    z_ref,
    mean_ref,
    fields_ref,
    low_ref,
    high_ref,
    weight_ref,
    faces_ref,
    inverse_ref,
    stack_ref,
    turned,
):
    fields, rows, cells = fields_ref.shape
    deep = stack_ref.shape[0]
    mask_set = masks(cells)
    start = low_ref.shape[0] - deep
    stack_ref[0] = mean_ref[...]
    stack_ref[1 : fields + 1] = fields_ref[...]
    stack_ref[fields + 1 :] = jnp.zeros((deep - fields - 1, rows, cells), jnp.float32)
    turned[1 : rows + 1] = jnp.swapaxes(stack_ref[...], 0, 1)
    turned[0] = low_ref[start:, :]
    turned[rows + 1] = high_ref[start:, :]
    z = z_ref[0]
    slab = weight_ref.shape[0]
    ahead = jnp.where(z < count // 2, 1, -1)
    for rho in range(slab):
        row = 1 + row_of(z, rho, slab, count, rows)
        centre = turned[row]
        others = (turned[row + ahead], turned[row - ahead]) + beside(centre, mask_set)
        for f, other in enumerate(others):
            weight_ref[rho, f] = 0.5 * (centre + other)
    place = lax.broadcasted_iota(jnp.int32, (rows, cells), 0)
    centre = mean_ref[...]
    high, low = high_ref[start : start + 1, :], low_ref[start : start + 1, :]
    up = jnp.where(place == rows - 1, high, pltpu.roll(centre, rows - 1, 0))
    down = jnp.where(place == 0, low, pltpu.roll(centre, 1, 0))
    diag = None
    for f, other in enumerate((up, down) + beside(centre, mask_set)):
        weight = 0.5 * (centre + other)
        diag = weight if diag is None else diag + weight
        faces_ref[f] = weight if f < 2 else weight * mask_set[f - 2]
    inverse_ref[...] = 1.0 / diag


def mix_kernel(count, groups, fields, window, skip, begin, extra, *refs):
    arrays = max(a for a, _ in window) + 1
    sources = refs[: arrays * count]
    dense_ref, own_ref, weight_ref = refs[arrays * count : arrays * count + 3]
    outs = refs[arrays * count + 3 + extra : -4]
    rows_ref, diff_ref, term_ref, total_ref = refs[-4:]
    size, cells = total_ref.shape
    here = size // count
    bf16 = jnp.bfloat16
    for k, (array, row) in enumerate(window):
        for p in range(count):
            part = sources[array * count + (count - p) % count]
            rows_ref[k, p * here : (p + 1) * here, :] = part[row]
    mask_set = masks(cells)
    def each_row(r, carry):
        row = jnp.where(r == 0, begin[0], begin[1] + r)
        r_in = r + jnp.where(r == 0, 0, skip)
        mean_weights = [weight_ref[row, f, 0:1, :] for f in range(6)]
        for t in range(0, size, 16):
            at = slice(t, t + 16)
            centre = rows_ref[r_in + 1, at].astype(jnp.float32)
            others = (
                rows_ref[r_in + 2, at].astype(jnp.float32),
                rows_ref[r_in, at].astype(jnp.float32),
            )
            mean = None
            for f, other in enumerate(others + beside(centre, mask_set)):
                diff = centre - other
                diff_ref[f, at] = diff.astype(bf16)
                part = mean_weights[f] * diff
                mean = part if mean is None else mean + part
            total_ref[at, :] = jnp.concatenate([own_ref[at]] * (cells // 128), 1) * mean
        for g in range(groups):
            for k in range(GROUP):
                field = min(1 + g * GROUP + k, fields - 1)
                weights = [
                    jnp.broadcast_to(weight_ref[row, f, field : field + 1, :], (16, cells))
                    for f in range(6)
                ]
                weights = [w.astype(bf16) for w in weights]
                for t in range(0, size, 16):
                    part = [weights[f] * diff_ref[f, t : t + 16] for f in range(6)]
                    term = ((part[0] + part[1]) + (part[2] + part[3])) + (part[4] + part[5])
                    term_ref[k * size + t : k * size + t + 16, :] = term
            total_ref[...] += jnp.dot(
                dense_ref[g], term_ref[...], preferred_element_type=jnp.float32
            )
        for p in range(count):
            outs[p][r] = total_ref[p * here : (p + 1) * here, :].astype(bf16)
        return carry

    lax.fori_loop(0, outs[0].shape[0], each_row, 0)


def edge_kernel(count, z_ref, *refs):
    parts = refs[:count]
    bottom_source, top_source, inverse = refs[count : count + 3]
    bottom, top = refs[-2:]
    z = z_ref[0]
    rows = inverse.shape[0]
    for k in range(count):
        place = jnp.bitwise_xor(z, (count - k) % count)
        image = parts[k][0].astype(jnp.float32)

        @pl.when(place == 0)
        def _():
            scale = inverse[0:1] * (1.0 / cheb_center)
            bottom[...] = (bottom_source[...] - image) * scale

        @pl.when(place == count - 1)
        def _():
            scale = inverse[rows - 1 : rows] * (1.0 / cheb_center)
            top[...] = (top_source[...] - image) * scale


def post_kernel(count, slab, half, rows, rho_zero, rho_one, z_ref, *refs):
    early = refs[:count]
    late = refs[count : 2 * count]
    source, iterate, low, high, faces, inverse = refs[2 * count : 2 * count + 6]
    updated, residual, image = refs[2 * count + 6 :]
    z = z_ref[0]
    modes, _, cells = source.shape
    for k in range(count):
        place = jnp.bitwise_xor(z, (count - k) % count)
        for rho in range(slab):
            part = early[k][rho] if rho < half else late[k][rho - half]
            image[row_of(place, rho, slab, count, rows)] = part.astype(jnp.float32)
    residual[...] = source[...] - jnp.swapaxes(image[...], 0, 1)
    place = lax.broadcasted_iota(jnp.int32, (rows, cells), 0)
    inv = inverse[...]
    for m in range(modes):
        res = residual[m]
        first = res * (inv * (1.0 / cheb_center))
        up = jnp.where(place == rows - 1, high[m : m + 1, :], pltpu.roll(first, rows - 1, 0))
        down = jnp.where(place == 0, low[m : m + 1, :], pltpu.roll(first, 1, 0))
        near = faces[0] * up + faces[1] * down
        near = near + faces[2] * pltpu.roll(first, cells - NZ, 1)
        near = near + faces[3] * pltpu.roll(first, NZ, 1)
        near = near + faces[4] * pltpu.roll(first, cells - 1, 1)
        near = near + faces[5] * pltpu.roll(first, 1, 1)
        smoothed = (1.0 - 1.0 / cheb_center) * res + near
        step = (1.0 + rho_one * rho_zero) * first + (2.0 * rho_one / cheb_radius) * smoothed * inv
        updated[m] = iterate[m] + step


def body(iterate, source, mean_coef, kl_fields, tri_index, tri_value):
    count = lax.axis_size("mode")
    doms = lax.axis_size("dom")
    z = lax.axis_index("mode")
    z_arg = z.astype(jnp.int32).reshape(1)
    here, rows, cells = iterate.shape
    size = here * count
    slab = rows // count
    half = slab // 2
    fields = kl_fields.shape[0] + 1
    groups = -(-(fields - 1) // GROUP)
    bf16 = jnp.bfloat16
    params = pltpu.CompilerParams(vmem_limit_bytes=VMEM_LIMIT)

    deep = -(-fields // 8) * 8

    turned, *early = pl.pallas_call(
        functools.partial(turn_kernel, count, slab, rows),
        out_shape=[jax.ShapeDtypeStruct((rows, here, cells), bf16)]
        + [jax.ShapeDtypeStruct((half + 1, here, cells), bf16)] * count,
        in_specs=[in_smem()] + in_vmem(1),
        out_specs=in_vmem(count + 1),
        compiler_params=params,
        cost_estimate=SMALL,
        name="turn",
    )(z_arg, iterate)

    def swap(arrays):
        taken = [arrays[0]]
        for p in reversed(range(1, count)):
            taken.append(lax.ppermute(arrays[p], "mode", [(i, i ^ p) for i in range(count)]))
        return taken

    early = swap(early)
    entries, values, _ = lax.optimization_barrier((tri_index, tri_value, turned))
    dense, own = pl.pallas_call(
        functools.partial(dense_kernel, groups, fields, here),
        out_shape=[
            jax.ShapeDtypeStruct((groups, size, GROUP * size), bf16),
            jax.ShapeDtypeStruct((size, 128), jnp.float32),
        ],
        in_specs=[in_smem()] + in_vmem(2),
        out_specs=in_vmem(2),
        compiler_params=params,
        cost_estimate=SMALL,
        name="dense",
    )(z_arg, entries.T, values[None])
    upward = [(i, i + 1) for i in range(doms - 1)]
    downward = [(b, a) for a, b in upward]
    before = []
    last_rim, first_rim = pl.pallas_call(
        rim_kernel,
        out_shape=[jax.ShapeDtypeStruct((here + deep, cells), jnp.float32)] * 2,
        in_specs=in_vmem(3) + [pl.BlockSpec(memory_space=pl.ANY)] * len(before),
        out_specs=in_vmem(2),
        compiler_params=params,
        cost_estimate=SMALL,
        name="rim",
    )(turned, mean_coef, kl_fields, *before)
    low_rim = lax.ppermute(last_rim, "dom", upward)
    high_rim = lax.ppermute(first_rim, "dom", downward)
    weights, faces, inverse = pl.pallas_call(
        functools.partial(weight_kernel, count),
        out_shape=[
            jax.ShapeDtypeStruct((slab, 6, deep, cells), jnp.float32),
            jax.ShapeDtypeStruct((6, rows, cells), jnp.float32),
            jax.ShapeDtypeStruct((rows, cells), jnp.float32),
        ],
        in_specs=[in_smem()] + in_vmem(4),
        out_specs=in_vmem(3),
        scratch_shapes=[
            pltpu.VMEM((deep, rows, cells), jnp.float32),
            pltpu.VMEM((rows + 2, deep, cells), jnp.float32),
        ],
        compiler_params=params,
        cost_estimate=SMALL,
        name="weights",
    )(z_arg, mean_coef, kl_fields, low_rim, high_rim)
    before = [own]
    rims = pl.pallas_call(
        functools.partial(beyond_kernel, count, slab, rows),
        out_shape=[jax.ShapeDtypeStruct((1, here, cells), bf16)] * count,
        in_specs=[in_smem()] + in_vmem(3) + [pl.BlockSpec(memory_space=pl.ANY)] * len(before),
        out_specs=in_vmem(count),
        compiler_params=params,
        cost_estimate=SMALL,
        name="beyond",
    )(z_arg, turned, low_rim, high_rim, *before)
    rims = swap(rims)
    late = pl.pallas_call(
        functools.partial(late_kernel, count, slab, rows),
        out_shape=[jax.ShapeDtypeStruct((slab - half, here, cells), bf16)] * count,
        in_specs=[in_smem()] + in_vmem(1) + [pl.BlockSpec(memory_space=pl.ANY)] * 2,
        out_specs=in_vmem(count),
        compiler_params=params,
        cost_estimate=SMALL,
        name="late",
    )(z_arg, turned, early[-2], inverse)
    late = swap(late)

    def mix(arrays, window, skip, begin, rows_out, after=()):
        flat = [a for group in arrays for a in group]
        return pl.pallas_call(
            functools.partial(
                mix_kernel, count, groups, fields, window, skip, begin, len(after)
            ),
            out_shape=[jax.ShapeDtypeStruct((rows_out, here, cells), bf16)] * count,
            in_specs=in_vmem(len(flat) + 3)
            + [pl.BlockSpec(memory_space=pl.ANY)] * len(after),
            out_specs=in_vmem(count),
            scratch_shapes=[
                pltpu.VMEM((len(window), size, cells), bf16),
                pltpu.VMEM((6, size, cells), bf16),
                pltpu.VMEM((GROUP * size, cells), bf16),
                pltpu.VMEM((size, cells), jnp.float32),
            ],
            compiler_params=params,
            cost_estimate=LARGE,
            name="mix",
        )(*flat, dense, own, weights, *after)

    window = ((0, 0),) + tuple((1, k) for k in range(half + 1))
    mixed = mix([rims, early], window, 0, (0, 0), half)
    back_early = swap(mixed)
    window = ((0, half - 1), (0, half)) + tuple((1, k) for k in range(slab - half))
    back_late = swap(mix([early, late], window, 0, (half, half), slab - half, mixed[-1:]))

    bottom, top = pl.pallas_call(
        functools.partial(edge_kernel, count),
        out_shape=[jax.ShapeDtypeStruct((here, cells), jnp.float32)] * 2,
        in_specs=[in_smem()] + in_vmem(count + 3),
        out_specs=in_vmem(2),
        compiler_params=params,
        cost_estimate=SMALL,
        name="edge",
    )(z_arg, *back_early, source[:, 0], source[:, rows - 1], inverse)
    low = lax.ppermute(top, "dom", upward)
    high = lax.ppermute(bottom, "dom", downward)

    sigma = cheb_center / cheb_radius
    rho_zero = 1.0 / sigma
    rho_one = 1.0 / (2.0 * sigma - rho_zero)
    block = min(16, here)
    row_spec = pl.BlockSpec((block, cells), lambda i: (i, 0))
    early_spec = pl.BlockSpec((half, block, cells), lambda i: (0, i, 0))
    late_spec = pl.BlockSpec((slab - half, block, cells), lambda i: (0, i, 0))
    flat_spec = pl.BlockSpec((block, rows, cells), lambda i: (i, 0, 0))
    updated, residual = pl.pallas_call(
        functools.partial(post_kernel, count, slab, half, rows, rho_zero, rho_one),
        grid=(here // block,),
        out_shape=[jax.ShapeDtypeStruct((here, rows, cells), jnp.float32)] * 2,
        in_specs=[in_smem()]
        + [early_spec] * count
        + [late_spec] * count
        + [flat_spec, flat_spec, row_spec, row_spec]
        + [
            pl.BlockSpec((6, rows, cells), lambda i: (0, 0, 0)),
            pl.BlockSpec((rows, cells), lambda i: (0, 0)),
        ],
        out_specs=[flat_spec, flat_spec],
        scratch_shapes=[pltpu.VMEM((rows, block, cells), jnp.float32)],
        compiler_params=params,
        name="post",
    )(
        z_arg,
        *back_early,
        *back_late,
        source,
        iterate,
        low,
        high,
        faces,
        inverse,
    )
    return updated, residual


def solution(mesh):
    return jax.shard_map(
        body,
        mesh=mesh,
        in_specs=(
            P("mode", "dom", None),
            P("mode", "dom", None),
            P("dom", None),
            P(None, "dom", None),
            P(),
            P(),
        ),
        out_specs=(P("mode", "dom", None), P("mode", "dom", None)),
        check_vma=False,
    )
```

```python
import functools
import jax
import jax.numpy as jnp
from jax import lax
from jax.experimental import pallas as pl
from jax.experimental.pallas import tpu as pltpu
from jax.sharding import PartitionSpec as P

NZ = 16
GROUP = 5

cheb_center = 1.125
cheb_radius = 0.875
SMALL = pl.CostEstimate(flops=1, bytes_accessed=1, transcendentals=0)
LARGE = pl.CostEstimate(flops=10**10, bytes_accessed=2**24, transcendentals=0)
VMEM_LIMIT = 16 * 1024 * 1024


def in_vmem(count):
    return [pl.BlockSpec(memory_space=pltpu.VMEM)] * count


def in_smem():
    return pl.BlockSpec(memory_space=pltpu.SMEM)


def row_of(place, rho, slab, count, rows):
    upward = slab * place + rho
    downward = slab * place + (slab - 1 - rho)
    row = jnp.where(place < count // 2, upward, downward)
    return jnp.clip(row, 0, rows - 1)


def turn_kernel(count, slab, rows, z_ref, x_ref, turned, *outs):
    z = z_ref[0]
    turned[...] = jnp.swapaxes(x_ref[...], 0, 1).astype(jnp.bfloat16)
    for p in range(count):
        place = jnp.bitwise_xor(z, p)
        for rho in range(outs[p].shape[0]):
            outs[p][rho] = turned[row_of(place, rho, slab, count, rows)]


def rim_kernel(turned, mean_ref, fields_ref, *refs):
    last, first = refs[-2:]
    rows, here, cells = turned.shape
    fields = fields_ref.shape[0]
    for out, row in ((first, 0), (last, rows - 1)):
        out[:here] = turned[row].astype(jnp.float32)
        out[here : here + 1, :] = mean_ref[row : row + 1, :]
        for field in range(fields):
            out[here + 1 + field : here + 2 + field, :] = fields_ref[field, row : row + 1, :]
        rest = out.shape[0] - here - 1 - fields
        out[here + 1 + fields :, :] = jnp.zeros((rest, cells), jnp.float32)


def late_kernel(count, slab, rows, z_ref, turned, *refs):
    outs = refs[2:]
    z = z_ref[0]
    for p in range(count):
        place = jnp.bitwise_xor(z, p)
        for k in range(outs[p].shape[0]):
            rho = slab + 1 - outs[p].shape[0] + k
            outs[p][k] = turned[row_of(place, rho, slab, count, rows)]


def beyond_kernel(count, slab, rows, z_ref, turned, low_ref, high_ref, *refs):
    outs = refs[-count:]
    z = z_ref[0]
    here = turned.shape[1]
    for p in range(count):
        place = jnp.bitwise_xor(z, p)
        outs[p][0] = turned[row_of(place, -1, slab, count, rows)]

        @pl.when(place == 0)
        def _():
            outs[p][0] = low_ref[:here].astype(jnp.bfloat16)

        @pl.when(place == count - 1)
        def _():
            outs[p][0] = high_ref[:here].astype(jnp.bfloat16)


def masks(cells):
    lane = lax.broadcasted_iota(jnp.int32, (1, cells), 1)
    in_z = lane % NZ
    one = jnp.float32(1.0)
    zero = jnp.float32(0.0)
    return (
        jnp.where(lane < cells - NZ, one, zero),
        jnp.where(lane >= NZ, one, zero),
        jnp.where(in_z < NZ - 1, one, zero),
        jnp.where(in_z > 0, one, zero),
    )


def beside(field, mask_set):
    cells = field.shape[-1]
    axis = field.ndim - 1
    return (
        pltpu.roll(field, cells - NZ, axis) * mask_set[0],
        pltpu.roll(field, NZ, axis) * mask_set[1],
        pltpu.roll(field, cells - 1, axis) * mask_set[2],
        pltpu.roll(field, 1, axis) * mask_set[3],
    )


def dense_kernel(groups, fields, modes_here, z_ref, entry_ref, value_ref, dense_ref, own_ref):
    size = dense_ref.shape[1]
    entries = entry_ref.shape[1]
    flip = z_ref[0] * modes_here
    mode_id = jnp.bitwise_xor(lax.broadcasted_iota(jnp.int32, (size, entries), 0), flip)
    pick = jnp.where(mode_id == entry_ref[0:1], 1.0, 0.0).astype(jnp.bfloat16)
    depth = -(-fields // 16) * 16
    here = lax.broadcasted_iota(jnp.int32, (depth, entries), 0) == entry_ref[2:3]
    partner = jnp.where(here, entry_ref[1:2].astype(jnp.float32), 0.0).astype(jnp.bfloat16)
    value = jnp.where(here, value_ref[...], 0.0).astype(jnp.bfloat16)
    dims = (((1,), (1,)), ((), ()))
    partner_of = lax.dot_general(pick, partner, dims, preferred_element_type=jnp.float32)
    value_of = lax.dot_general(pick, value, dims, preferred_element_type=jnp.float32)
    column = jnp.bitwise_xor(lax.broadcasted_iota(jnp.int32, (size, size), 1), flip)
    column = column.astype(jnp.float32)
    own_ref[...] = jnp.broadcast_to(value_of[:, 0:1], own_ref.shape)
    for g in range(groups):
        for k in range(GROUP):
            at = 1 + g * GROUP + k
            if at >= fields:
                tile = jnp.zeros((size, size), jnp.float32)
            else:
                tile = jnp.where(
                    column == partner_of[:, at : at + 1], value_of[:, at : at + 1], 0.0
                )
            dense_ref[g, :, k * size : (k + 1) * size] = tile.astype(jnp.bfloat16)


def weight_kernel(
    count,
    z_ref,
    mean_ref,
    fields_ref,
    low_ref,
    high_ref,
    weight_ref,
    faces_ref,
    inverse_ref,
    stack_ref,
    turned,
):
    fields, rows, cells = fields_ref.shape
    deep = stack_ref.shape[0]
    mask_set = masks(cells)
    start = low_ref.shape[0] - deep
    stack_ref[0] = mean_ref[...]
    stack_ref[1 : fields + 1] = fields_ref[...]
    stack_ref[fields + 1 :] = jnp.zeros((deep - fields - 1, rows, cells), jnp.float32)
    turned[1 : rows + 1] = jnp.swapaxes(stack_ref[...], 0, 1)
    turned[0] = low_ref[start:, :]
    turned[rows + 1] = high_ref[start:, :]
    z = z_ref[0]
    slab = weight_ref.shape[0]
    ahead = jnp.where(z < count // 2, 1, -1)
    for rho in range(slab):
        row = 1 + row_of(z, rho, slab, count, rows)
        centre = turned[row]
        others = (turned[row + ahead], turned[row - ahead]) + beside(centre, mask_set)
        for f, other in enumerate(others):
            weight_ref[rho, f] = 0.5 * (centre + other)
    place = lax.broadcasted_iota(jnp.int32, (rows, cells), 0)
    centre = mean_ref[...]
    high, low = high_ref[start : start + 1, :], low_ref[start : start + 1, :]
    up = jnp.where(place == rows - 1, high, pltpu.roll(centre, rows - 1, 0))
    down = jnp.where(place == 0, low, pltpu.roll(centre, 1, 0))
    diag = None
    for f, other in enumerate((up, down) + beside(centre, mask_set)):
        weight = 0.5 * (centre + other)
        diag = weight if diag is None else diag + weight
        faces_ref[f] = weight if f < 2 else weight * mask_set[f - 2]
    inverse_ref[...] = 1.0 / diag


def mix_kernel(count, groups, fields, window, skip, begin, extra, *refs):
    arrays = max(a for a, _ in window) + 1
    sources = refs[: arrays * count]
    dense_ref, own_ref, weight_ref = refs[arrays * count : arrays * count + 3]
    outs = refs[arrays * count + 3 + extra : -4]
    rows_ref, diff_ref, term_ref, total_ref = refs[-4:]
    size, cells = total_ref.shape
    here = size // count
    bf16 = jnp.bfloat16
    for k, (array, row) in enumerate(window):
        for p in range(count):
            part = sources[array * count + (count - p) % count]
            rows_ref[k, p * here : (p + 1) * here, :] = part[row]
    mask_set = masks(cells)
    def each_row(r, carry):
        row = jnp.where(r == 0, begin[0], begin[1] + r)
        r_in = r + jnp.where(r == 0, 0, skip)
        mean_weights = [weight_ref[row, f, 0:1, :] for f in range(6)]
        for t in range(0, size, 16):
            at = slice(t, t + 16)
            centre = rows_ref[r_in + 1, at].astype(jnp.float32)
            others = (
                rows_ref[r_in + 2, at].astype(jnp.float32),
                rows_ref[r_in, at].astype(jnp.float32),
            )
            mean = None
            for f, other in enumerate(others + beside(centre, mask_set)):
                diff = centre - other
                diff_ref[f, at] = diff.astype(bf16)
                part = mean_weights[f] * diff
                mean = part if mean is None else mean + part
            total_ref[at, :] = jnp.concatenate([own_ref[at]] * (cells // 128), 1) * mean
        for g in range(groups):
            for k in range(GROUP):
                field = min(1 + g * GROUP + k, fields - 1)
                weights = [
                    jnp.broadcast_to(weight_ref[row, f, field : field + 1, :], (16, cells))
                    for f in range(6)
                ]
                weights = [w.astype(bf16) for w in weights]
                for t in range(0, size, 16):
                    part = [weights[f] * diff_ref[f, t : t + 16] for f in range(6)]
                    term = ((part[0] + part[1]) + (part[2] + part[3])) + (part[4] + part[5])
                    term_ref[k * size + t : k * size + t + 16, :] = term
            total_ref[...] += jnp.dot(
                dense_ref[g], term_ref[...], preferred_element_type=jnp.float32
            )
        for p in range(count):
            outs[p][r] = total_ref[p * here : (p + 1) * here, :].astype(bf16)
        return carry

    lax.fori_loop(0, outs[0].shape[0], each_row, 0)


def edge_kernel(count, z_ref, *refs):
    parts = refs[:count]
    bottom_source, top_source, inverse = refs[count : count + 3]
    bottom, top = refs[-2:]
    z = z_ref[0]
    rows = inverse.shape[0]
    for k in range(count):
        place = jnp.bitwise_xor(z, (count - k) % count)
        image = parts[k][0].astype(jnp.float32)

        @pl.when(place == 0)
        def _():
            scale = inverse[0:1] * (1.0 / cheb_center)
            bottom[...] = (bottom_source[...] - image) * scale

        @pl.when(place == count - 1)
        def _():
            scale = inverse[rows - 1 : rows] * (1.0 / cheb_center)
            top[...] = (top_source[...] - image) * scale


def post_kernel(count, slab, half, rows, rho_zero, rho_one, z_ref, *refs):
    early = refs[:count]
    late = refs[count : 2 * count]
    source, iterate, low, high, faces, inverse = refs[2 * count : 2 * count + 6]
    updated, residual, image = refs[2 * count + 6 :]
    z = z_ref[0]
    modes, _, cells = source.shape
    for k in range(count):
        place = jnp.bitwise_xor(z, (count - k) % count)
        for rho in range(slab):
            part = early[k][rho] if rho < half else late[k][rho - half]
            image[row_of(place, rho, slab, count, rows)] = part.astype(jnp.float32)
    residual[...] = source[...] - jnp.swapaxes(image[...], 0, 1)
    place = lax.broadcasted_iota(jnp.int32, (rows, cells), 0)
    inv = inverse[...]
    for m in range(modes):
        res = residual[m]
        first = res * (inv * (1.0 / cheb_center))
        up = jnp.where(place == rows - 1, high[m : m + 1, :], pltpu.roll(first, rows - 1, 0))
        down = jnp.where(place == 0, low[m : m + 1, :], pltpu.roll(first, 1, 0))
        near = faces[0] * up + faces[1] * down
        near = near + faces[2] * pltpu.roll(first, cells - NZ, 1)
        near = near + faces[3] * pltpu.roll(first, NZ, 1)
        near = near + faces[4] * pltpu.roll(first, cells - 1, 1)
        near = near + faces[5] * pltpu.roll(first, 1, 1)
        smoothed = (1.0 - 1.0 / cheb_center) * res + near
        step = (1.0 + rho_one * rho_zero) * first + (2.0 * rho_one / cheb_radius) * smoothed * inv
        updated[m] = iterate[m] + step


def body(iterate, source, mean_coef, kl_fields, tri_index, tri_value):
    count = lax.axis_size("mode")
    doms = lax.axis_size("dom")
    z = lax.axis_index("mode")
    z_arg = z.astype(jnp.int32).reshape(1)
    here, rows, cells = iterate.shape
    size = here * count
    slab = rows // count
    half = slab // 2
    fields = kl_fields.shape[0] + 1
    groups = -(-(fields - 1) // GROUP)
    bf16 = jnp.bfloat16
    params = pltpu.CompilerParams(vmem_limit_bytes=VMEM_LIMIT)

    deep = -(-fields // 8) * 8

    turned, *early = pl.pallas_call(
        functools.partial(turn_kernel, count, slab, rows),
        out_shape=[jax.ShapeDtypeStruct((rows, here, cells), bf16)]
        + [jax.ShapeDtypeStruct((half + 1, here, cells), bf16)] * count,
        in_specs=[in_smem()] + in_vmem(1),
        out_specs=in_vmem(count + 1),
        compiler_params=params,
        cost_estimate=SMALL,
        name="turn",
    )(z_arg, iterate)

    def swap(arrays):
        taken = [arrays[0]]
        for p in reversed(range(1, count)):
            taken.append(lax.ppermute(arrays[p], "mode", [(i, i ^ p) for i in range(count)]))
        return taken

    early = swap(early)
    entries, values, _ = lax.optimization_barrier((tri_index, tri_value, turned))
    dense, own = pl.pallas_call(
        functools.partial(dense_kernel, groups, fields, here),
        out_shape=[
            jax.ShapeDtypeStruct((groups, size, GROUP * size), bf16),
            jax.ShapeDtypeStruct((size, 128), jnp.float32),
        ],
        in_specs=[in_smem()] + in_vmem(2),
        out_specs=in_vmem(2),
        compiler_params=params,
        cost_estimate=SMALL,
        name="dense",
    )(z_arg, entries.T, values[None])
    upward = [(i, i + 1) for i in range(doms - 1)]
    downward = [(b, a) for a, b in upward]
    before = []
    last_rim, first_rim = pl.pallas_call(
        rim_kernel,
        out_shape=[jax.ShapeDtypeStruct((here + deep, cells), jnp.float32)] * 2,
        in_specs=in_vmem(3) + [pl.BlockSpec(memory_space=pl.ANY)] * len(before),
        out_specs=in_vmem(2),
        compiler_params=params,
        cost_estimate=SMALL,
        name="rim",
    )(turned, mean_coef, kl_fields, *before)
    low_rim = lax.ppermute(last_rim, "dom", upward)
    high_rim = lax.ppermute(first_rim, "dom", downward)
    weights, faces, inverse = pl.pallas_call(
        functools.partial(weight_kernel, count),
        out_shape=[
            jax.ShapeDtypeStruct((slab, 6, deep, cells), jnp.float32),
            jax.ShapeDtypeStruct((6, rows, cells), jnp.float32),
            jax.ShapeDtypeStruct((rows, cells), jnp.float32),
        ],
        in_specs=[in_smem()] + in_vmem(4),
        out_specs=in_vmem(3),
        scratch_shapes=[
            pltpu.VMEM((deep, rows, cells), jnp.float32),
            pltpu.VMEM((rows + 2, deep, cells), jnp.float32),
        ],
        compiler_params=params,
        cost_estimate=SMALL,
        name="weights",
    )(z_arg, mean_coef, kl_fields, low_rim, high_rim)
    before = [own]
    rims = pl.pallas_call(
        functools.partial(beyond_kernel, count, slab, rows),
        out_shape=[jax.ShapeDtypeStruct((1, here, cells), bf16)] * count,
        in_specs=[in_smem()] + in_vmem(3) + [pl.BlockSpec(memory_space=pl.ANY)] * len(before),
        out_specs=in_vmem(count),
        compiler_params=params,
        cost_estimate=SMALL,
        name="beyond",
    )(z_arg, turned, low_rim, high_rim, *before)
    rims = swap(rims)
    late = pl.pallas_call(
        functools.partial(late_kernel, count, slab, rows),
        out_shape=[jax.ShapeDtypeStruct((slab - half, here, cells), bf16)] * count,
        in_specs=[in_smem()] + in_vmem(1) + [pl.BlockSpec(memory_space=pl.ANY)] * 2,
        out_specs=in_vmem(count),
        compiler_params=params,
        cost_estimate=SMALL,
        name="late",
    )(z_arg, turned, early[-2], inverse)
    def mix(arrays, window, skip, begin, rows_out, after=()):
        flat = [a for group in arrays for a in group]
        return pl.pallas_call(
            functools.partial(
                mix_kernel, count, groups, fields, window, skip, begin, len(after)
            ),
            out_shape=[jax.ShapeDtypeStruct((rows_out, here, cells), bf16)] * count,
            in_specs=in_vmem(len(flat) + 3)
            + [pl.BlockSpec(memory_space=pl.ANY)] * len(after),
            out_specs=in_vmem(count),
            scratch_shapes=[
                pltpu.VMEM((len(window), size, cells), bf16),
                pltpu.VMEM((6, size, cells), bf16),
                pltpu.VMEM((GROUP * size, cells), bf16),
                pltpu.VMEM((size, cells), jnp.float32),
            ],
            compiler_params=params,
            cost_estimate=LARGE,
            name="mix",
        )(*flat, dense, own, weights, *after)

    window = ((0, 0),) + tuple((1, k) for k in range(half + 1))
    mixed = mix([rims, early], window, 0, (0, 0), half)
    back_early = swap(mixed)
    late = list(late)
    late[1], _ = lax.optimization_barrier((late[1], mixed[0]))
    late = swap(late)
    window = ((0, half - 1), (0, half)) + tuple((1, k) for k in range(slab - half))
    back_late = swap(mix([early, late], window, 0, (half, half), slab - half, mixed[-1:]))

    bottom, top = pl.pallas_call(
        functools.partial(edge_kernel, count),
        out_shape=[jax.ShapeDtypeStruct((here, cells), jnp.float32)] * 2,
        in_specs=[in_smem()] + in_vmem(count + 3),
        out_specs=in_vmem(2),
        compiler_params=params,
        cost_estimate=SMALL,
        name="edge",
    )(z_arg, *back_early, source[:, 0], source[:, rows - 1], inverse)
    low = lax.ppermute(top, "dom", upward)
    high = lax.ppermute(bottom, "dom", downward)

    sigma = cheb_center / cheb_radius
    rho_zero = 1.0 / sigma
    rho_one = 1.0 / (2.0 * sigma - rho_zero)
    block = min(16, here)
    row_spec = pl.BlockSpec((block, cells), lambda i: (i, 0))
    early_spec = pl.BlockSpec((half, block, cells), lambda i: (0, i, 0))
    late_spec = pl.BlockSpec((slab - half, block, cells), lambda i: (0, i, 0))
    flat_spec = pl.BlockSpec((block, rows, cells), lambda i: (i, 0, 0))
    updated, residual = pl.pallas_call(
        functools.partial(post_kernel, count, slab, half, rows, rho_zero, rho_one),
        grid=(here // block,),
        out_shape=[jax.ShapeDtypeStruct((here, rows, cells), jnp.float32)] * 2,
        in_specs=[in_smem()]
        + [early_spec] * count
        + [late_spec] * count
        + [flat_spec, flat_spec, row_spec, row_spec]
        + [
            pl.BlockSpec((6, rows, cells), lambda i: (0, 0, 0)),
            pl.BlockSpec((rows, cells), lambda i: (0, 0)),
        ],
        out_specs=[flat_spec, flat_spec],
        scratch_shapes=[pltpu.VMEM((rows, block, cells), jnp.float32)],
        compiler_params=params,
        name="post",
    )(
        z_arg,
        *back_early,
        *back_late,
        source,
        iterate,
        low,
        high,
        faces,
        inverse,
    )
    return updated, residual


def solution(mesh):
    return jax.shard_map(
        body,
        mesh=mesh,
        in_specs=(
            P("mode", "dom", None),
            P("mode", "dom", None),
            P("dom", None),
            P(None, "dom", None),
            P(),
            P(),
        ),
        out_specs=(P("mode", "dom", None), P("mode", "dom", None)),
        check_vma=False,
    )
```

```python
import functools
import jax
import jax.numpy as jnp
from jax import lax
from jax.experimental import pallas as pl
from jax.experimental.pallas import tpu as pltpu
from jax.sharding import PartitionSpec as P

NZ = 16
GROUP = 5

cheb_center = 1.125
cheb_radius = 0.875
SMALL = pl.CostEstimate(flops=1, bytes_accessed=1, transcendentals=0)
LARGE = pl.CostEstimate(flops=10**10, bytes_accessed=2**24, transcendentals=0)
VMEM_LIMIT = 16 * 1024 * 1024


def in_vmem(count):
    return [pl.BlockSpec(memory_space=pltpu.VMEM)] * count


def in_smem():
    return pl.BlockSpec(memory_space=pltpu.SMEM)


def row_of(place, rho, slab, count, rows):
    upward = slab * place + rho
    downward = slab * place + (slab - 1 - rho)
    row = jnp.where(place < count // 2, upward, downward)
    return jnp.clip(row, 0, rows - 1)


def turn_kernel(count, slab, rows, z_ref, x_ref, turned, *outs):
    z = z_ref[0]
    turned[...] = jnp.swapaxes(x_ref[...], 0, 1).astype(jnp.bfloat16)
    for p in range(count):
        place = jnp.bitwise_xor(z, p)
        for rho in range(outs[p].shape[0]):
            outs[p][rho] = turned[row_of(place, rho, slab, count, rows)]


def rim_kernel(turned, mean_ref, fields_ref, *refs):
    last, first = refs[-2:]
    rows, here, cells = turned.shape
    fields = fields_ref.shape[0]
    for out, row in ((first, 0), (last, rows - 1)):
        out[:here] = turned[row].astype(jnp.float32)
        out[here : here + 1, :] = mean_ref[row : row + 1, :]
        for field in range(fields):
            out[here + 1 + field : here + 2 + field, :] = fields_ref[field, row : row + 1, :]
        rest = out.shape[0] - here - 1 - fields
        out[here + 1 + fields :, :] = jnp.zeros((rest, cells), jnp.float32)


def late_kernel(count, slab, rows, z_ref, turned, *refs):
    outs = refs[2:]
    z = z_ref[0]
    for p in range(count):
        place = jnp.bitwise_xor(z, p)
        for k in range(outs[p].shape[0]):
            rho = slab + 1 - outs[p].shape[0] + k
            outs[p][k] = turned[row_of(place, rho, slab, count, rows)]


def beyond_kernel(count, slab, rows, z_ref, turned, low_ref, high_ref, *refs):
    outs = refs[-count:]
    z = z_ref[0]
    here = turned.shape[1]
    for p in range(count):
        place = jnp.bitwise_xor(z, p)
        outs[p][0] = turned[row_of(place, -1, slab, count, rows)]

        @pl.when(place == 0)
        def _():
            outs[p][0] = low_ref[:here].astype(jnp.bfloat16)

        @pl.when(place == count - 1)
        def _():
            outs[p][0] = high_ref[:here].astype(jnp.bfloat16)


def masks(cells):
    lane = lax.broadcasted_iota(jnp.int32, (1, cells), 1)
    in_z = lane % NZ
    one = jnp.float32(1.0)
    zero = jnp.float32(0.0)
    return (
        jnp.where(lane < cells - NZ, one, zero),
        jnp.where(lane >= NZ, one, zero),
        jnp.where(in_z < NZ - 1, one, zero),
        jnp.where(in_z > 0, one, zero),
    )


def beside(field, mask_set):
    cells = field.shape[-1]
    axis = field.ndim - 1
    return (
        pltpu.roll(field, cells - NZ, axis) * mask_set[0],
        pltpu.roll(field, NZ, axis) * mask_set[1],
        pltpu.roll(field, cells - 1, axis) * mask_set[2],
        pltpu.roll(field, 1, axis) * mask_set[3],
    )


def dense_kernel(groups, fields, modes_here, z_ref, entry_ref, value_ref, dense_ref, own_ref):
    size = dense_ref.shape[1]
    entries = entry_ref.shape[1]
    flip = z_ref[0] * modes_here
    mode_id = jnp.bitwise_xor(lax.broadcasted_iota(jnp.int32, (size, entries), 0), flip)
    pick = jnp.where(mode_id == entry_ref[0:1], 1.0, 0.0).astype(jnp.bfloat16)
    depth = -(-fields // 16) * 16
    here = lax.broadcasted_iota(jnp.int32, (depth, entries), 0) == entry_ref[2:3]
    partner = jnp.where(here, entry_ref[1:2].astype(jnp.float32), 0.0).astype(jnp.bfloat16)
    value = jnp.where(here, value_ref[...], 0.0).astype(jnp.bfloat16)
    dims = (((1,), (1,)), ((), ()))
    partner_of = lax.dot_general(pick, partner, dims, preferred_element_type=jnp.float32)
    value_of = lax.dot_general(pick, value, dims, preferred_element_type=jnp.float32)
    column = jnp.bitwise_xor(lax.broadcasted_iota(jnp.int32, (size, size), 1), flip)
    column = column.astype(jnp.float32)
    own_ref[...] = jnp.broadcast_to(value_of[:, 0:1], own_ref.shape)
    for g in range(groups):
        for k in range(GROUP):
            at = 1 + g * GROUP + k
            if at >= fields:
                tile = jnp.zeros((size, size), jnp.float32)
            else:
                tile = jnp.where(
                    column == partner_of[:, at : at + 1], value_of[:, at : at + 1], 0.0
                )
            dense_ref[g, :, k * size : (k + 1) * size] = tile.astype(jnp.bfloat16)


def weight_kernel(
    count,
    z_ref,
    mean_ref,
    fields_ref,
    low_ref,
    high_ref,
    weight_ref,
    faces_ref,
    inverse_ref,
    stack_ref,
    turned,
):
    fields, rows, cells = fields_ref.shape
    deep = stack_ref.shape[0]
    mask_set = masks(cells)
    start = low_ref.shape[0] - deep
    stack_ref[0] = mean_ref[...]
    stack_ref[1 : fields + 1] = fields_ref[...]
    stack_ref[fields + 1 :] = jnp.zeros((deep - fields - 1, rows, cells), jnp.float32)
    turned[1 : rows + 1] = jnp.swapaxes(stack_ref[...], 0, 1)
    turned[0] = low_ref[start:, :]
    turned[rows + 1] = high_ref[start:, :]
    z = z_ref[0]
    slab = weight_ref.shape[0]
    ahead = jnp.where(z < count // 2, 1, -1)
    for rho in range(slab):
        row = 1 + row_of(z, rho, slab, count, rows)
        centre = turned[row]
        others = (turned[row + ahead], turned[row - ahead]) + beside(centre, mask_set)
        for f, other in enumerate(others):
            weight_ref[rho, f] = 0.5 * (centre + other)
    place = lax.broadcasted_iota(jnp.int32, (rows, cells), 0)
    centre = mean_ref[...]
    high, low = high_ref[start : start + 1, :], low_ref[start : start + 1, :]
    up = jnp.where(place == rows - 1, high, pltpu.roll(centre, rows - 1, 0))
    down = jnp.where(place == 0, low, pltpu.roll(centre, 1, 0))
    diag = None
    for f, other in enumerate((up, down) + beside(centre, mask_set)):
        weight = 0.5 * (centre + other)
        diag = weight if diag is None else diag + weight
        faces_ref[f] = weight if f < 2 else weight * mask_set[f - 2]
    inverse_ref[...] = 1.0 / diag


def mix_kernel(count, groups, fields, window, skip, begin, extra, *refs):
    arrays = max(a for a, _ in window) + 1
    sources = refs[: arrays * count]
    dense_ref, own_ref, weight_ref = refs[arrays * count : arrays * count + 3]
    outs = refs[arrays * count + 3 + extra : -4]
    rows_ref, diff_ref, term_ref, total_ref = refs[-4:]
    size, cells = total_ref.shape
    here = size // count
    bf16 = jnp.bfloat16
    for k, (array, row) in enumerate(window):
        for p in range(count):
            part = sources[array * count + (count - p) % count]
            rows_ref[k, p * here : (p + 1) * here, :] = part[row]
    mask_set = masks(cells)
    def each_row(r, carry):
        row = jnp.where(r == 0, begin[0], begin[1] + r)
        r_in = r + jnp.where(r == 0, 0, skip)
        mean_weights = [weight_ref[row, f, 0:1, :] for f in range(6)]
        for t in range(0, size, 16):
            at = slice(t, t + 16)
            centre = rows_ref[r_in + 1, at].astype(jnp.float32)
            others = (
                rows_ref[r_in + 2, at].astype(jnp.float32),
                rows_ref[r_in, at].astype(jnp.float32),
            )
            mean = None
            for f, other in enumerate(others + beside(centre, mask_set)):
                diff = centre - other
                diff_ref[f, at] = diff.astype(bf16)
                part = mean_weights[f] * diff
                mean = part if mean is None else mean + part
            total_ref[at, :] = jnp.concatenate([own_ref[at]] * (cells // 128), 1) * mean
        for g in range(groups):
            for k in range(GROUP):
                field = min(1 + g * GROUP + k, fields - 1)
                weights = [
                    jnp.broadcast_to(weight_ref[row, f, field : field + 1, :], (16, cells))
                    for f in range(6)
                ]
                weights = [w.astype(bf16) for w in weights]
                for t in range(0, size, 16):
                    part = [weights[f] * diff_ref[f, t : t + 16] for f in range(6)]
                    term = ((part[0] + part[1]) + (part[2] + part[3])) + (part[4] + part[5])
                    term_ref[k * size + t : k * size + t + 16, :] = term
            total_ref[...] += jnp.dot(
                dense_ref[g], term_ref[...], preferred_element_type=jnp.float32
            )
        for p in range(count):
            outs[p][r] = total_ref[p * here : (p + 1) * here, :].astype(bf16)
        return carry

    lax.fori_loop(0, outs[0].shape[0], each_row, 0)


def edge_kernel(count, z_ref, *refs):
    parts = refs[:count]
    bottom_source, top_source, inverse = refs[count : count + 3]
    bottom, top = refs[-2:]
    z = z_ref[0]
    rows = inverse.shape[0]
    for k in range(count):
        place = jnp.bitwise_xor(z, (count - k) % count)
        image = parts[k][0].astype(jnp.float32)

        @pl.when(place == 0)
        def _():
            scale = inverse[0:1] * (1.0 / cheb_center)
            bottom[...] = (bottom_source[...] - image) * scale

        @pl.when(place == count - 1)
        def _():
            scale = inverse[rows - 1 : rows] * (1.0 / cheb_center)
            top[...] = (top_source[...] - image) * scale


def post_kernel(count, slab, half, rows, rho_zero, rho_one, z_ref, *refs):
    early = refs[:count]
    late = refs[count : 2 * count]
    source, iterate, low, high, faces, inverse = refs[2 * count : 2 * count + 6]
    updated, residual, image = refs[2 * count + 6 :]
    z = z_ref[0]
    modes, _, cells = source.shape
    for k in range(count):
        place = jnp.bitwise_xor(z, (count - k) % count)
        for rho in range(slab):
            part = early[k][rho] if rho < half else late[k][rho - half]
            image[row_of(place, rho, slab, count, rows)] = part
    residual[...] = source[...] - jnp.swapaxes(image[...], 0, 1).astype(jnp.float32)
    place = lax.broadcasted_iota(jnp.int32, (rows, cells), 0)
    inv = inverse[...]
    for m in range(modes):
        res = residual[m]
        first = res * (inv * (1.0 / cheb_center))
        up = jnp.where(place == rows - 1, high[m : m + 1, :], pltpu.roll(first, rows - 1, 0))
        down = jnp.where(place == 0, low[m : m + 1, :], pltpu.roll(first, 1, 0))
        near = faces[0] * up + faces[1] * down
        near = near + faces[2] * pltpu.roll(first, cells - NZ, 1)
        near = near + faces[3] * pltpu.roll(first, NZ, 1)
        near = near + faces[4] * pltpu.roll(first, cells - 1, 1)
        near = near + faces[5] * pltpu.roll(first, 1, 1)
        smoothed = (1.0 - 1.0 / cheb_center) * res + near
        step = (1.0 + rho_one * rho_zero) * first + (2.0 * rho_one / cheb_radius) * smoothed * inv
        updated[m] = iterate[m] + step


def body(iterate, source, mean_coef, kl_fields, tri_index, tri_value):
    count = lax.axis_size("mode")
    doms = lax.axis_size("dom")
    z = lax.axis_index("mode")
    z_arg = z.astype(jnp.int32).reshape(1)
    here, rows, cells = iterate.shape
    size = here * count
    slab = rows // count
    half = slab // 2
    fields = kl_fields.shape[0] + 1
    groups = -(-(fields - 1) // GROUP)
    bf16 = jnp.bfloat16
    params = pltpu.CompilerParams(vmem_limit_bytes=VMEM_LIMIT)

    deep = -(-fields // 8) * 8

    turned, *early = pl.pallas_call(
        functools.partial(turn_kernel, count, slab, rows),
        out_shape=[jax.ShapeDtypeStruct((rows, here, cells), bf16)]
        + [jax.ShapeDtypeStruct((half + 1, here, cells), bf16)] * count,
        in_specs=[in_smem()] + in_vmem(1),
        out_specs=in_vmem(count + 1),
        compiler_params=params,
        cost_estimate=SMALL,
        name="turn",
    )(z_arg, iterate)

    def swap(arrays):
        taken = [arrays[0]]
        for p in reversed(range(1, count)):
            taken.append(lax.ppermute(arrays[p], "mode", [(i, i ^ p) for i in range(count)]))
        return taken

    early = swap(early)
    entries, values, _ = lax.optimization_barrier((tri_index, tri_value, turned))
    dense, own = pl.pallas_call(
        functools.partial(dense_kernel, groups, fields, here),
        out_shape=[
            jax.ShapeDtypeStruct((groups, size, GROUP * size), bf16),
            jax.ShapeDtypeStruct((size, 128), jnp.float32),
        ],
        in_specs=[in_smem()] + in_vmem(2),
        out_specs=in_vmem(2),
        compiler_params=params,
        cost_estimate=SMALL,
        name="dense",
    )(z_arg, entries.T, values[None])
    upward = [(i, i + 1) for i in range(doms - 1)]
    downward = [(b, a) for a, b in upward]
    before = []
    last_rim, first_rim = pl.pallas_call(
        rim_kernel,
        out_shape=[jax.ShapeDtypeStruct((here + deep, cells), jnp.float32)] * 2,
        in_specs=in_vmem(3) + [pl.BlockSpec(memory_space=pl.ANY)] * len(before),
        out_specs=in_vmem(2),
        compiler_params=params,
        cost_estimate=SMALL,
        name="rim",
    )(turned, mean_coef, kl_fields, *before)
    low_rim = lax.ppermute(last_rim, "dom", upward)
    high_rim = lax.ppermute(first_rim, "dom", downward)
    weights, faces, inverse = pl.pallas_call(
        functools.partial(weight_kernel, count),
        out_shape=[
            jax.ShapeDtypeStruct((slab, 6, deep, cells), jnp.float32),
            jax.ShapeDtypeStruct((6, rows, cells), jnp.float32),
            jax.ShapeDtypeStruct((rows, cells), jnp.float32),
        ],
        in_specs=[in_smem()] + in_vmem(4),
        out_specs=in_vmem(3),
        scratch_shapes=[
            pltpu.VMEM((deep, rows, cells), jnp.float32),
            pltpu.VMEM((rows + 2, deep, cells), jnp.float32),
        ],
        compiler_params=params,
        cost_estimate=SMALL,
        name="weights",
    )(z_arg, mean_coef, kl_fields, low_rim, high_rim)
    before = [own]
    rims = pl.pallas_call(
        functools.partial(beyond_kernel, count, slab, rows),
        out_shape=[jax.ShapeDtypeStruct((1, here, cells), bf16)] * count,
        in_specs=[in_smem()] + in_vmem(3) + [pl.BlockSpec(memory_space=pl.ANY)] * len(before),
        out_specs=in_vmem(count),
        compiler_params=params,
        cost_estimate=SMALL,
        name="beyond",
    )(z_arg, turned, low_rim, high_rim, *before)
    rims = swap(rims)
    late = pl.pallas_call(
        functools.partial(late_kernel, count, slab, rows),
        out_shape=[jax.ShapeDtypeStruct((slab - half, here, cells), bf16)] * count,
        in_specs=[in_smem()] + in_vmem(1) + [pl.BlockSpec(memory_space=pl.ANY)] * 2,
        out_specs=in_vmem(count),
        compiler_params=params,
        cost_estimate=SMALL,
        name="late",
    )(z_arg, turned, early[-2], inverse)
    late = swap(late)

    def mix(arrays, window, skip, begin, rows_out, after=()):
        flat = [a for group in arrays for a in group]
        return pl.pallas_call(
            functools.partial(
                mix_kernel, count, groups, fields, window, skip, begin, len(after)
            ),
            out_shape=[jax.ShapeDtypeStruct((rows_out, here, cells), bf16)] * count,
            in_specs=in_vmem(len(flat) + 3)
            + [pl.BlockSpec(memory_space=pl.ANY)] * len(after),
            out_specs=in_vmem(count),
            scratch_shapes=[
                pltpu.VMEM((len(window), size, cells), bf16),
                pltpu.VMEM((6, size, cells), bf16),
                pltpu.VMEM((GROUP * size, cells), bf16),
                pltpu.VMEM((size, cells), jnp.float32),
            ],
            compiler_params=params,
            cost_estimate=LARGE,
            name="mix",
        )(*flat, dense, own, weights, *after)

    window = ((0, 0),) + tuple((1, k) for k in range(half + 1))
    mixed = mix([rims, early], window, 0, (0, 0), half)
    back_early = swap(mixed)
    window = ((0, half - 1), (0, half)) + tuple((1, k) for k in range(slab - half))
    back_late = swap(mix([early, late], window, 0, (half, half), slab - half, mixed[-1:]))

    bottom, top = pl.pallas_call(
        functools.partial(edge_kernel, count),
        out_shape=[jax.ShapeDtypeStruct((here, cells), jnp.float32)] * 2,
        in_specs=[in_smem()] + in_vmem(count + 3),
        out_specs=in_vmem(2),
        compiler_params=params,
        cost_estimate=SMALL,
        name="edge",
    )(z_arg, *back_early, source[:, 0], source[:, rows - 1], inverse)
    low = lax.ppermute(top, "dom", upward)
    high = lax.ppermute(bottom, "dom", downward)

    sigma = cheb_center / cheb_radius
    rho_zero = 1.0 / sigma
    rho_one = 1.0 / (2.0 * sigma - rho_zero)
    block = min(32, here)
    row_spec = pl.BlockSpec((block, cells), lambda i: (i, 0))
    early_spec = pl.BlockSpec((half, block, cells), lambda i: (0, i, 0))
    late_spec = pl.BlockSpec((slab - half, block, cells), lambda i: (0, i, 0))
    flat_spec = pl.BlockSpec((block, rows, cells), lambda i: (i, 0, 0))
    updated, residual = pl.pallas_call(
        functools.partial(post_kernel, count, slab, half, rows, rho_zero, rho_one),
        grid=(here // block,),
        out_shape=[jax.ShapeDtypeStruct((here, rows, cells), jnp.float32)] * 2,
        in_specs=[in_smem()]
        + [early_spec] * count
        + [late_spec] * count
        + [flat_spec, flat_spec, row_spec, row_spec]
        + [
            pl.BlockSpec((6, rows, cells), lambda i: (0, 0, 0)),
            pl.BlockSpec((rows, cells), lambda i: (0, 0)),
        ],
        out_specs=[flat_spec, flat_spec],
        scratch_shapes=[pltpu.VMEM((rows, block, cells), bf16)],
        compiler_params=params,
        name="post",
    )(
        z_arg,
        *back_early,
        *back_late,
        source,
        iterate,
        low,
        high,
        faces,
        inverse,
    )
    return updated, residual


def solution(mesh):
    return jax.shard_map(
        body,
        mesh=mesh,
        in_specs=(
            P("mode", "dom", None),
            P("mode", "dom", None),
            P("dom", None),
            P(None, "dom", None),
            P(),
            P(),
        ),
        out_specs=(P("mode", "dom", None), P("mode", "dom", None)),
        check_vma=False,
    )
```

```python
import functools
import jax
import jax.numpy as jnp
from jax import lax
from jax.experimental import pallas as pl
from jax.experimental.pallas import tpu as pltpu
from jax.sharding import PartitionSpec as P

NZ = 16
GROUP = 5

cheb_center = 1.125
cheb_radius = 0.875
SMALL = pl.CostEstimate(flops=1, bytes_accessed=1, transcendentals=0)
LARGE = pl.CostEstimate(flops=10**10, bytes_accessed=2**24, transcendentals=0)
VMEM_LIMIT = 16 * 1024 * 1024


def in_vmem(count):
    return [pl.BlockSpec(memory_space=pltpu.VMEM)] * count


def in_smem():
    return pl.BlockSpec(memory_space=pltpu.SMEM)


def row_of(place, rho, slab, count, rows):
    upward = slab * place + rho
    downward = slab * place + (slab - 1 - rho)
    row = jnp.where(place < count // 2, upward, downward)
    return jnp.clip(row, 0, rows - 1)


def turn_kernel(count, slab, rows, z_ref, x_ref, turned, *outs):
    z = z_ref[0]
    turned[...] = jnp.swapaxes(x_ref[...], 0, 1).astype(jnp.bfloat16)
    for p in range(count):
        place = jnp.bitwise_xor(z, p)
        for rho in range(outs[p].shape[0]):
            outs[p][rho] = turned[row_of(place, rho, slab, count, rows)]


def rim_kernel(turned, mean_ref, fields_ref, *refs):
    last, first = refs[-2:]
    rows, here, cells = turned.shape
    fields = fields_ref.shape[0]
    for out, row in ((first, 0), (last, rows - 1)):
        out[:here] = turned[row].astype(jnp.float32)
        out[here : here + 1, :] = mean_ref[row : row + 1, :]
        for field in range(fields):
            out[here + 1 + field : here + 2 + field, :] = fields_ref[field, row : row + 1, :]
        rest = out.shape[0] - here - 1 - fields
        out[here + 1 + fields :, :] = jnp.zeros((rest, cells), jnp.float32)


def late_kernel(count, slab, rows, z_ref, turned, *refs):
    outs = refs[2:]
    z = z_ref[0]
    for p in range(count):
        place = jnp.bitwise_xor(z, p)
        for k in range(outs[p].shape[0]):
            rho = slab + 1 - outs[p].shape[0] + k
            outs[p][k] = turned[row_of(place, rho, slab, count, rows)]


def beyond_kernel(count, slab, rows, z_ref, turned, low_ref, high_ref, *refs):
    outs = refs[-count:]
    z = z_ref[0]
    here = turned.shape[1]
    for p in range(count):
        place = jnp.bitwise_xor(z, p)
        outs[p][0] = turned[row_of(place, -1, slab, count, rows)]

        @pl.when(place == 0)
        def _():
            outs[p][0] = low_ref[:here].astype(jnp.bfloat16)

        @pl.when(place == count - 1)
        def _():
            outs[p][0] = high_ref[:here].astype(jnp.bfloat16)


def masks(cells):
    lane = lax.broadcasted_iota(jnp.int32, (1, cells), 1)
    in_z = lane % NZ
    one = jnp.float32(1.0)
    zero = jnp.float32(0.0)
    return (
        jnp.where(lane < cells - NZ, one, zero),
        jnp.where(lane >= NZ, one, zero),
        jnp.where(in_z < NZ - 1, one, zero),
        jnp.where(in_z > 0, one, zero),
    )


def beside(field, mask_set):
    cells = field.shape[-1]
    axis = field.ndim - 1
    return (
        pltpu.roll(field, cells - NZ, axis) * mask_set[0],
        pltpu.roll(field, NZ, axis) * mask_set[1],
        pltpu.roll(field, cells - 1, axis) * mask_set[2],
        pltpu.roll(field, 1, axis) * mask_set[3],
    )


def dense_kernel(groups, fields, modes_here, z_ref, entry_ref, value_ref, dense_ref, own_ref):
    size = dense_ref.shape[1]
    entries = entry_ref.shape[1]
    flip = z_ref[0] * modes_here
    mode_id = jnp.bitwise_xor(lax.broadcasted_iota(jnp.int32, (size, entries), 0), flip)
    pick = jnp.where(mode_id == entry_ref[0:1], 1.0, 0.0).astype(jnp.bfloat16)
    depth = -(-fields // 16) * 16
    here = lax.broadcasted_iota(jnp.int32, (depth, entries), 0) == entry_ref[2:3]
    partner = jnp.where(here, entry_ref[1:2].astype(jnp.float32), 0.0).astype(jnp.bfloat16)
    value = jnp.where(here, value_ref[...], 0.0).astype(jnp.bfloat16)
    dims = (((1,), (1,)), ((), ()))
    partner_of = lax.dot_general(pick, partner, dims, preferred_element_type=jnp.float32)
    value_of = lax.dot_general(pick, value, dims, preferred_element_type=jnp.float32)
    column = jnp.bitwise_xor(lax.broadcasted_iota(jnp.int32, (size, size), 1), flip)
    column = column.astype(jnp.float32)
    own_ref[...] = jnp.broadcast_to(value_of[:, 0:1], own_ref.shape)
    for g in range(groups):
        for k in range(GROUP):
            at = 1 + g * GROUP + k
            if at >= fields:
                tile = jnp.zeros((size, size), jnp.float32)
            else:
                tile = jnp.where(
                    column == partner_of[:, at : at + 1], value_of[:, at : at + 1], 0.0
                )
            dense_ref[g, :, k * size : (k + 1) * size] = tile.astype(jnp.bfloat16)


def weight_kernel(
    count,
    z_ref,
    mean_ref,
    fields_ref,
    low_ref,
    high_ref,
    weight_ref,
    faces_ref,
    inverse_ref,
    stack_ref,
    turned,
):
    fields, rows, cells = fields_ref.shape
    deep = stack_ref.shape[0]
    mask_set = masks(cells)
    start = low_ref.shape[0] - deep
    stack_ref[0] = mean_ref[...]
    stack_ref[1 : fields + 1] = fields_ref[...]
    stack_ref[fields + 1 :] = jnp.zeros((deep - fields - 1, rows, cells), jnp.float32)
    turned[1 : rows + 1] = jnp.swapaxes(stack_ref[...], 0, 1)
    turned[0] = low_ref[start:, :]
    turned[rows + 1] = high_ref[start:, :]
    z = z_ref[0]
    slab = weight_ref.shape[0]
    ahead = jnp.where(z < count // 2, 1, -1)
    for rho in range(slab):
        row = 1 + row_of(z, rho, slab, count, rows)
        centre = turned[row]
        others = (turned[row + ahead], turned[row - ahead]) + beside(centre, mask_set)
        for f, other in enumerate(others):
            weight_ref[rho, f] = 0.5 * (centre + other)
    place = lax.broadcasted_iota(jnp.int32, (rows, cells), 0)
    centre = mean_ref[...]
    high, low = high_ref[start : start + 1, :], low_ref[start : start + 1, :]
    up = jnp.where(place == rows - 1, high, pltpu.roll(centre, rows - 1, 0))
    down = jnp.where(place == 0, low, pltpu.roll(centre, 1, 0))
    diag = None
    for f, other in enumerate((up, down) + beside(centre, mask_set)):
        weight = 0.5 * (centre + other)
        diag = weight if diag is None else diag + weight
        faces_ref[f] = weight if f < 2 else weight * mask_set[f - 2]
    inverse_ref[...] = 1.0 / diag


def mix_kernel(count, groups, fields, window, skip, begin, extra, *refs):
    arrays = max(a for a, _ in window) + 1
    sources = refs[: arrays * count]
    dense_ref, own_ref, weight_ref = refs[arrays * count : arrays * count + 3]
    outs = refs[arrays * count + 3 + extra : -4]
    rows_ref, diff_ref, term_ref, total_ref = refs[-4:]
    size, cells = total_ref.shape
    here = size // count
    bf16 = jnp.bfloat16
    for k, (array, row) in enumerate(window):
        for p in range(count):
            part = sources[array * count + (count - p) % count]
            rows_ref[k, p * here : (p + 1) * here, :] = part[row]
    mask_set = masks(cells)
    def each_row(r, carry):
        row = jnp.where(r == 0, begin[0], begin[1] + r)
        r_in = r + jnp.where(r == 0, 0, skip)
        mean_weights = [weight_ref[row, f, 0:1, :] for f in range(6)]
        for t in range(0, size, 16):
            at = slice(t, t + 16)
            centre = rows_ref[r_in + 1, at].astype(jnp.float32)
            others = (
                rows_ref[r_in + 2, at].astype(jnp.float32),
                rows_ref[r_in, at].astype(jnp.float32),
            )
            mean = None
            for f, other in enumerate(others + beside(centre, mask_set)):
                diff = centre - other
                diff_ref[f, at] = diff.astype(bf16)
                part = mean_weights[f] * diff
                mean = part if mean is None else mean + part
            total_ref[at, :] = jnp.concatenate([own_ref[at]] * (cells // 128), 1) * mean
        for g in range(groups):
            for k in range(GROUP):
                field = min(1 + g * GROUP + k, fields - 1)
                weights = [
                    jnp.broadcast_to(weight_ref[row, f, field : field + 1, :], (16, cells))
                    for f in range(6)
                ]
                weights = [w.astype(bf16) for w in weights]
                for t in range(0, size, 16):
                    part = [weights[f] * diff_ref[f, t : t + 16] for f in range(6)]
                    term = ((part[0] + part[1]) + (part[2] + part[3])) + (part[4] + part[5])
                    term_ref[k * size + t : k * size + t + 16, :] = term
            total_ref[...] += jnp.dot(
                dense_ref[g], term_ref[...], preferred_element_type=jnp.float32
            )
        for p in range(count):
            outs[p][r] = total_ref[p * here : (p + 1) * here, :].astype(bf16)
        return carry

    lax.fori_loop(0, outs[0].shape[0], each_row, 0)


def edge_kernel(count, z_ref, *refs):
    parts = refs[:count]
    bottom_source, top_source, inverse = refs[count : count + 3]
    bottom, top = refs[-2:]
    z = z_ref[0]
    rows = inverse.shape[0]
    for k in range(count):
        place = jnp.bitwise_xor(z, (count - k) % count)
        image = parts[k][0].astype(jnp.float32)

        @pl.when(place == 0)
        def _():
            scale = inverse[0:1] * (1.0 / cheb_center)
            bottom[...] = (bottom_source[...] - image) * scale

        @pl.when(place == count - 1)
        def _():
            scale = inverse[rows - 1 : rows] * (1.0 / cheb_center)
            top[...] = (top_source[...] - image) * scale


def post_kernel(count, slab, half, rows, rho_zero, rho_one, z_ref, *refs):
    early = refs[:count]
    late = refs[count : 2 * count]
    source, iterate, low, high, faces, inverse = refs[2 * count : 2 * count + 6]
    updated, residual, image = refs[2 * count + 6 :]
    z = z_ref[0]
    modes, _, cells = source.shape
    for k in range(count):
        place = jnp.bitwise_xor(z, (count - k) % count)
        for rho in range(slab):
            part = early[k][rho] if rho < half else late[k][rho - half]
            image[row_of(place, rho, slab, count, rows)] = part
    residual[...] = source[...] - jnp.swapaxes(image[...], 0, 1).astype(jnp.float32)
    place = lax.broadcasted_iota(jnp.int32, (rows, cells), 0)
    inv = inverse[...]
    for m in range(modes):
        res = residual[m]
        first = res * (inv * (1.0 / cheb_center))
        up = jnp.where(place == rows - 1, high[m : m + 1, :], pltpu.roll(first, rows - 1, 0))
        down = jnp.where(place == 0, low[m : m + 1, :], pltpu.roll(first, 1, 0))
        near = faces[0] * up + faces[1] * down
        near = near + faces[2] * pltpu.roll(first, cells - NZ, 1)
        near = near + faces[3] * pltpu.roll(first, NZ, 1)
        near = near + faces[4] * pltpu.roll(first, cells - 1, 1)
        near = near + faces[5] * pltpu.roll(first, 1, 1)
        smoothed = (1.0 - 1.0 / cheb_center) * res + near
        step = (1.0 + rho_one * rho_zero) * first + (2.0 * rho_one / cheb_radius) * smoothed * inv
        updated[m] = iterate[m] + step


def body(iterate, source, mean_coef, kl_fields, tri_index, tri_value):
    count = lax.axis_size("mode")
    doms = lax.axis_size("dom")
    z = lax.axis_index("mode")
    z_arg = z.astype(jnp.int32).reshape(1)
    here, rows, cells = iterate.shape
    size = here * count
    slab = rows // count
    half = slab // 2
    fields = kl_fields.shape[0] + 1
    groups = -(-(fields - 1) // GROUP)
    bf16 = jnp.bfloat16
    params = pltpu.CompilerParams(vmem_limit_bytes=VMEM_LIMIT)

    deep = -(-fields // 8) * 8

    turned, *early = pl.pallas_call(
        functools.partial(turn_kernel, count, slab, rows),
        out_shape=[jax.ShapeDtypeStruct((rows, here, cells), bf16)]
        + [jax.ShapeDtypeStruct((half + 1, here, cells), bf16)] * count,
        in_specs=[in_smem()] + in_vmem(1),
        out_specs=in_vmem(count + 1),
        compiler_params=params,
        cost_estimate=SMALL,
        name="turn",
    )(z_arg, iterate)

    def swap(arrays):
        taken = [arrays[0]]
        for p in reversed(range(1, count)):
            taken.append(lax.ppermute(arrays[p], "mode", [(i, i ^ p) for i in range(count)]))
        return taken

    early = swap(early)
    entries, values, _ = lax.optimization_barrier((tri_index, tri_value, turned))
    dense, own = pl.pallas_call(
        functools.partial(dense_kernel, groups, fields, here),
        out_shape=[
            jax.ShapeDtypeStruct((groups, size, GROUP * size), bf16),
            jax.ShapeDtypeStruct((size, 128), jnp.float32),
        ],
        in_specs=[in_smem()] + in_vmem(2),
        out_specs=in_vmem(2),
        compiler_params=params,
        cost_estimate=SMALL,
        name="dense",
    )(z_arg, entries.T, values[None])
    upward = [(i, i + 1) for i in range(doms - 1)]
    downward = [(b, a) for a, b in upward]
    before = []
    last_rim, first_rim = pl.pallas_call(
        rim_kernel,
        out_shape=[jax.ShapeDtypeStruct((here + deep, cells), jnp.float32)] * 2,
        in_specs=in_vmem(3) + [pl.BlockSpec(memory_space=pl.ANY)] * len(before),
        out_specs=in_vmem(2),
        compiler_params=params,
        cost_estimate=SMALL,
        name="rim",
    )(turned, mean_coef, kl_fields, *before)
    low_rim = lax.ppermute(last_rim, "dom", upward)
    high_rim = lax.ppermute(first_rim, "dom", downward)
    weights, faces, inverse = pl.pallas_call(
        functools.partial(weight_kernel, count),
        out_shape=[
            jax.ShapeDtypeStruct((slab, 6, deep, cells), jnp.float32),
            jax.ShapeDtypeStruct((6, rows, cells), jnp.float32),
            jax.ShapeDtypeStruct((rows, cells), jnp.float32),
        ],
        in_specs=[in_smem()] + in_vmem(4),
        out_specs=in_vmem(3),
        scratch_shapes=[
            pltpu.VMEM((deep, rows, cells), jnp.float32),
            pltpu.VMEM((rows + 2, deep, cells), jnp.float32),
        ],
        compiler_params=params,
        cost_estimate=SMALL,
        name="weights",
    )(z_arg, mean_coef, kl_fields, low_rim, high_rim)
    before = [own]
    rims = pl.pallas_call(
        functools.partial(beyond_kernel, count, slab, rows),
        out_shape=[jax.ShapeDtypeStruct((1, here, cells), bf16)] * count,
        in_specs=[in_smem()] + in_vmem(3) + [pl.BlockSpec(memory_space=pl.ANY)] * len(before),
        out_specs=in_vmem(count),
        compiler_params=params,
        cost_estimate=SMALL,
        name="beyond",
    )(z_arg, turned, low_rim, high_rim, *before)
    rims = swap(rims)
    late = pl.pallas_call(
        functools.partial(late_kernel, count, slab, rows),
        out_shape=[jax.ShapeDtypeStruct((slab - half, here, cells), bf16)] * count,
        in_specs=[in_smem()] + in_vmem(1) + [pl.BlockSpec(memory_space=pl.ANY)] * 2,
        out_specs=in_vmem(count),
        compiler_params=params,
        cost_estimate=SMALL,
        name="late",
    )(z_arg, turned, own, inverse)
    late = swap(late)

    def mix(arrays, window, skip, begin, rows_out, after=()):
        flat = [a for group in arrays for a in group]
        return pl.pallas_call(
            functools.partial(
                mix_kernel, count, groups, fields, window, skip, begin, len(after)
            ),
            out_shape=[jax.ShapeDtypeStruct((rows_out, here, cells), bf16)] * count,
            in_specs=in_vmem(len(flat) + 3)
            + [pl.BlockSpec(memory_space=pl.ANY)] * len(after),
            out_specs=in_vmem(count),
            scratch_shapes=[
                pltpu.VMEM((len(window), size, cells), bf16),
                pltpu.VMEM((6, size, cells), bf16),
                pltpu.VMEM((GROUP * size, cells), bf16),
                pltpu.VMEM((size, cells), jnp.float32),
            ],
            compiler_params=params,
            cost_estimate=LARGE,
            name="mix",
        )(*flat, dense, own, weights, *after)

    window = ((0, 0),) + tuple((1, k) for k in range(half + 1))
    mixed = mix([rims, early], window, 0, (0, 0), half)
    back_early = swap(mixed)
    window = ((0, half - 1), (0, half)) + tuple((1, k) for k in range(slab - half))
    back_late = swap(mix([early, late], window, 0, (half, half), slab - half, mixed[-1:]))

    bottom, top = pl.pallas_call(
        functools.partial(edge_kernel, count),
        out_shape=[jax.ShapeDtypeStruct((here, cells), jnp.float32)] * 2,
        in_specs=[in_smem()] + in_vmem(count + 3),
        out_specs=in_vmem(2),
        compiler_params=params,
        cost_estimate=SMALL,
        name="edge",
    )(z_arg, *back_early, source[:, 0], source[:, rows - 1], inverse)
    low = lax.ppermute(top, "dom", upward)
    high = lax.ppermute(bottom, "dom", downward)

    sigma = cheb_center / cheb_radius
    rho_zero = 1.0 / sigma
    rho_one = 1.0 / (2.0 * sigma - rho_zero)
    block = min(32, here)
    row_spec = pl.BlockSpec((block, cells), lambda i: (i, 0))
    early_spec = pl.BlockSpec((half, block, cells), lambda i: (0, i, 0))
    late_spec = pl.BlockSpec((slab - half, block, cells), lambda i: (0, i, 0))
    flat_spec = pl.BlockSpec((block, rows, cells), lambda i: (i, 0, 0))
    updated, residual = pl.pallas_call(
        functools.partial(post_kernel, count, slab, half, rows, rho_zero, rho_one),
        grid=(here // block,),
        out_shape=[jax.ShapeDtypeStruct((here, rows, cells), jnp.float32)] * 2,
        in_specs=[in_smem()]
        + [early_spec] * count
        + [late_spec] * count
        + [flat_spec, flat_spec, row_spec, row_spec]
        + [
            pl.BlockSpec((6, rows, cells), lambda i: (0, 0, 0)),
            pl.BlockSpec((rows, cells), lambda i: (0, 0)),
        ],
        out_specs=[flat_spec, flat_spec],
        scratch_shapes=[pltpu.VMEM((rows, block, cells), bf16)],
        compiler_params=params,
        name="post",
    )(
        z_arg,
        *back_early,
        *back_late,
        source,
        iterate,
        low,
        high,
        faces,
        inverse,
    )
    return updated, residual


def solution(mesh):
    return jax.shard_map(
        body,
        mesh=mesh,
        in_specs=(
            P("mode", "dom", None),
            P("mode", "dom", None),
            P("dom", None),
            P(None, "dom", None),
            P(),
            P(),
        ),
        out_specs=(P("mode", "dom", None), P("mode", "dom", None)),
        check_vma=False,
    )
```
